32 devices in a mesh: seq: 4 (over y, core), fsdp: 8 (over z, x).
Axes of the slice: x: 2, y: 2, z: 4, core: 2. Of those that a mesh axis runs over, the one named last changes fastest.
Arguments:
- tokens: bfloat16 [8, 2, 1024, 2048], P('fsdp', None, 'seq'), may hold values from -6 to 6
- cotangent: bfloat16 [8, 2, 1024, 2048], P('fsdp', None, 'seq'), may hold values from -6 to 6
- w_qkv: bfloat16 [2048, 6144], P('fsdp'), may hold values from -0.125 to 0.125
- w_out: bfloat16 [2048, 2048], P('fsdp'), may hold values from -0.5 to 0.5
- w_gate_up: bfloat16 [2048, 16384], P('fsdp'), may hold values from -0.125 to 0.125
- w_down: bfloat16 [8192, 2048], P('fsdp'), may hold values from -0.0625 to 0.0625
- gain_attn: float32 [2048], replicated, may hold values from 0.5 to 1.5
- gain_ffn: float32 [2048], replicated, may hold values from 0.5 to 1.5
- gate_bias: float32 [16], replicated, may hold values from -1 to 3
- memory_in: float32 [8, 16, 128, 128], P('fsdp'), may hold values from -12300 to 12300
- norms_in: float32 [8, 16, 128], P('fsdp'), may hold values from 1 to 1025
- resets: int32 [8, 1], P('fsdp'), may hold values 0 or 1
- depth: int32 [8], P('fsdp'), may hold values from 1 to 2
Outputs:
- output: bfloat16 [8, 2, 1024, 2048], P('fsdp', None, 'seq')
- input_grad: bfloat16 [8, 2, 1024, 2048], P('fsdp', None, 'seq')
- grad_qkv: float32 [2048, 6144], P('fsdp')
- grad_out: float32 [2048, 2048], P('fsdp')
- grad_gate_up: float32 [2048, 16384], P('fsdp')
- grad_down: float32 [8192, 2048], P('fsdp')
- grad_gain_attn: float32 [2048], replicated
- grad_gain_ffn: float32 [2048], replicated
- grad_gate_bias: float32 [16], replicated
The draws below stay inside these ranges and needn't reach their ends.
All inputs are finite; a program needn't handle non-finite values. No bound on the sum of `resets` on one device may be relied on, other than what follows from the above.
Results may differ from the reference program's by a relative error of at most 0.022.
Values may be sent and summed in bfloat16 or wider, within the bound.
A program may use at most 576 MiB of HBM per device.

```python
import jax
import jax.numpy as jnp
from jax import lax

D = 2048
HEADS = 16
HEAD_DIM = 128
FF = 8192
SEG = 1024
SEGS = 2
SEQS = 8


def memory_parts(key):
    base = jax.random.fold_in(key, 7001)
    key_scale, key_spread, key_common, key_rough = jax.random.split(base, 4)
    log_scale = jax.random.uniform(key_scale, (SEQS, HEADS, 1), jnp.float32, jnp.log(0.05), jnp.log(0.5))
    spread = jax.random.uniform(key_spread, (SEQS, HEADS, HEAD_DIM), jnp.float32, 0.5, 1.5)
    norms = 1.0 + SEG * jnp.exp(log_scale) * spread
    common = jnp.clip(3.0 * jax.random.normal(key_common, (SEQS, HEADS, 1, HEAD_DIM), jnp.float32), -8.0, 8.0)
    rough = jnp.clip(jax.random.normal(key_rough, (SEQS, HEADS, HEAD_DIM, HEAD_DIM), jnp.float32), -4.0, 4.0)
    memory = norms[..., :, None] * (common + rough)
    return (memory, norms)


def draw_memory_in(key, part):
    return memory_parts(key)[0]


def draw_norms_in(key, part):
    return memory_parts(key)[1]


def place_ends(array, rng, low, high):
    index_at = [jax.random.randint(jax.random.fold_in(rng, axis), (), 0, length) for axis, length in enumerate(array.shape)]
    main_axis = array.shape.index(max(array.shape))
    beside = index_at[:main_axis] + [(index_at[main_axis] + 1) % array.shape[main_axis]] + index_at[main_axis + 1:]
    return array.at[tuple(index_at)].set(low).at[tuple(beside)].set(high)


def block_scale(key, dims, cuts, low, high):
    def one(axis_at, shards_of):
        heights = jax.random.uniform(jax.random.fold_in(jax.random.fold_in(key, 6), axis_at), (shards_of,), jnp.float32, low / len(cuts), high / len(cuts))
        return jnp.repeat(jnp.exp(heights), dims[axis_at] // shards_of).reshape((-1,) + (1,) * (len(dims) - axis_at - 1))

    gain = one(*cuts[0])
    for cut in cuts[1:]:
        gain = gain * one(*cut)
    return gain


def bell_draw(stream_key, dims, scale, most, cuts=(), kind=jnp.bfloat16):
    values = scale * jax.random.normal(stream_key, dims, jnp.float32)
    if cuts:
        values = values * block_scale(stream_key, dims, cuts, -0.22, 0.18)
    return jnp.clip(values, -most, most).astype(kind)


def setup_inputs(seed: int = 0) -> dict:
    seeds = jax.random.split(jax.random.key(seed), 14)
    return {
        "tokens": bell_draw(seeds[0], (SEQS, SEGS, SEG, D), 1.0, 6.0, ((0, 8), (2, 4))),
        "cotangent": bell_draw(seeds[1], (SEQS, SEGS, SEG, D), 1.0, 6.0, ((0, 8), (2, 4))),
        "w_qkv": bell_draw(seeds[2], (D, 3 * D), D ** -0.5, 0.125, ((0, 8),)),
        "w_out": bell_draw(seeds[3], (D, D), (D // 16) ** -0.5, 0.5, ((0, 8),)),
        "w_gate_up": bell_draw(seeds[4], (D, 2 * FF), D ** -0.5, 0.125, ((0, 8),)),
        "w_down": bell_draw(seeds[5], (FF, D), FF ** -0.5, 0.0625, ((0, 8),)),
        "gain_attn": jnp.clip(1.0 + 0.1 * jax.random.normal(seeds[6], (D,), jnp.float32), 0.5, 1.5),
        "gain_ffn": jnp.clip(1.0 + 0.1 * jax.random.normal(seeds[7], (D,), jnp.float32), 0.5, 1.5),
        "gate_bias": jnp.clip(jax.random.uniform(seeds[8], (HEADS,), jnp.float32, -1.0, 3.0), -1.0, 3.0),
        "memory_in": draw_memory_in(jax.random.fold_in(seeds[13], 71), 0),
        "norms_in": draw_norms_in(jax.random.fold_in(seeds[13], 71), 0),
        "resets": place_ends((jax.random.randint(seeds[11], (SEQS, SEGS - 1), 0, 2) < 1).astype(jnp.int32), jax.random.fold_in(seeds[11], 1), 0, 1),
        "depth": place_ends(jax.random.randint(seeds[12], (SEQS,), 1, SEGS + 1), jax.random.fold_in(seeds[12], 1), 1, SEGS).astype(jnp.int32),
    }


@jax.custom_vjp
def low(v):
    return lax.optimization_barrier(v.astype(jnp.bfloat16)).astype(jnp.float32)

@jax.custom_vjp
def low_back(v):
    return v

def low_keep(v):
    return (low(v), None)

def low_pass(kept, grad):
    return (grad,)

def back_keep(v):
    return (v, None)

def back_low(kept, grad):
    return (low(grad),)
low.defvjp(low_keep, low_pass)
low_back.defvjp(back_keep, back_low)
norm_eps = 1e-05

def hdot(left, right):
    return jnp.dot(left, right, precision=lax.Precision.HIGHEST, preferred_element_type=jnp.float32)

def rms(value_rows_segment):
    return value_rows_segment * lax.rsqrt(lax.optimization_barrier(jnp.mean(value_rows_segment * value_rows_segment, axis=-1, keepdims=True)) + norm_eps)

def feature(value_rows_segment):
    return jnp.where(value_rows_segment > 0, value_rows_segment + 1.0, jnp.exp(jnp.minimum(value_rows_segment, 0.0)))

def attend(block):
    query, key, value_rows_segment = block
    scores = jnp.einsum('qhd,khd->hqk', query, key, precision=lax.Precision.HIGHEST) * (1.0 / HEAD_DIM ** 0.5)
    scores = low_back(scores)
    places = jnp.arange(SEG, dtype=jnp.int32)
    allowed = places[None, :] <= places[:, None]
    scores = jnp.where(allowed[None], scores, -1e+30)
    top = lax.optimization_barrier(jnp.max(scores, axis=-1, keepdims=True))
    weights = jnp.exp(scores - top)
    probs = weights / lax.optimization_barrier(jnp.sum(weights, axis=-1, keepdims=True))
    return low_back(jnp.einsum('hqk,khd->qhd', low(probs), value_rows_segment, precision=lax.Precision.HIGHEST))

def memory_step(carry, items):
    memory, norms = carry
    feature_queries, feature_keys, value_rows_segment, start, cut, held_m, held_z = items
    memory_matrix_entry = jnp.where(start > 0, jnp.zeros_like(memory), jnp.where(cut > 0, held_m, memory))
    normalizer_entry = jnp.where(start > 0, jnp.ones_like(norms), jnp.where(cut > 0, held_z, norms))
    hidden_previous = lax.Precision.HIGHEST
    attention_memory_mix = jnp.einsum('zqi,qis->zqs', feature_queries, memory_matrix_entry, precision=hidden_previous) / jnp.einsum('rzo,zo->rz', feature_queries, normalizer_entry, precision=hidden_previous)[..., None]
    memory_recall_read = jnp.einsum('zqi,qis->zqs', feature_keys, memory_matrix_entry, precision=hidden_previous) / jnp.einsum('rzo,zo->rz', feature_keys, normalizer_entry, precision=hidden_previous)[..., None]
    memory_matrix_exit = memory_matrix_entry + jnp.einsum('ubf,ubc->bfc', feature_keys, value_rows_segment - memory_recall_read, precision=hidden_previous)
    z_out = normalizer_entry + lax.optimization_barrier(jnp.sum(feature_keys, axis=0))
    return ((memory_matrix_exit, z_out), (attention_memory_mix, memory_matrix_entry, normalizer_entry))

def layer(params, xs, starts, cuts, held_m, held_z, first_m, first_z):
    w_qkv, w_out, w_gate_up, w_down, gain_attn, gain_ffn, gate_bias = params
    flat = xs.reshape(SEGS * SEG, D)
    h_one = low(rms(flat) * gain_attn)
    qkv = low(low_back(hdot(h_one, w_qkv)))
    shaped = qkv.reshape(SEGS, SEG, 3, HEADS, HEAD_DIM)
    query, key, value_rows_segment = (shaped[:, :, 0], shaped[:, :, 1], shaped[:, :, 2])
    adot = lax.map(jax.checkpoint(attend), (query, key, value_rows_segment))
    init = (first_m, first_z)
    _, (attention_memory_mix, m_ins, z_ins) = lax.scan(memory_step, init, (feature(query), feature(key), value_rows_segment, starts, cuts, held_m, held_z))
    gate = jax.nn.sigmoid(gate_bias)[:, None]
    mixed = gate * attention_memory_mix + (1.0 - gate) * adot
    attn = low(low_back(mixed.reshape(SEGS * SEG, D)))
    x_one = flat + low_back(hdot(attn, w_out))
    h_two = low(rms(x_one) * gain_ffn)
    gate_up = low(low_back(hdot(h_two, w_gate_up)))
    hidden = low(jax.nn.silu(gate_up[:, :FF]) * gate_up[:, FF:])
    result = x_one + hdot(hidden, w_down)
    return (result.reshape(SEGS, SEG, D), (m_ins, z_ins))

def reference(tokens, cotangent, w_qkv, w_out, w_gate_up, w_down, gain_attn, gain_ffn, gate_bias, memory_in, norms_in, resets, depth):
    params = (w_qkv.astype(jnp.float32), w_out.astype(jnp.float32), w_gate_up.astype(jnp.float32), w_down.astype(jnp.float32), gain_attn.astype(jnp.float32), gain_ffn.astype(jnp.float32), gate_bias.astype(jnp.float32))

    def one(carry, items):
        xs, cs, first_m, first_z, flags, steps = items
        first_m = first_m.astype(jnp.float32)
        first_z = first_z.astype(jnp.float32)
        starts = jnp.concatenate([jnp.zeros((1,), jnp.int32), flags.astype(jnp.int32)])
        places = jnp.arange(SEGS, dtype=jnp.int32)
        cuts = ((places % steps == 0) & (places > 0)).astype(jnp.int32)
        xf = xs.astype(jnp.float32)
        _, (held_m, held_z) = layer(params, xf, starts, jnp.zeros((SEGS,), jnp.int32), jnp.zeros((SEGS, HEADS, HEAD_DIM, HEAD_DIM), jnp.float32), jnp.ones((SEGS, HEADS, HEAD_DIM), jnp.float32), first_m, first_z)
        result, back = jax.vjp(lambda p, v: layer(p, v, starts, cuts, held_m, held_z, first_m, first_z)[0], params, xf)
        grad_p, grad_x = back(cs.astype(jnp.float32))
        carry = jax.tree.map(lambda a, b: a + b, carry, grad_p)
        return (carry, (result.astype(jnp.bfloat16), grad_x.astype(jnp.bfloat16)))
    zeros = jax.tree.map(jnp.zeros_like, params)
    sums, (output, input_grad) = lax.scan(one, zeros, (tokens, cotangent, memory_in, norms_in, resets, depth))
    return (output, input_grad, sums[0], sums[1], sums[2], sums[3], sums[4], sums[5], sums[6])
```

```python
import jax
import jax.numpy as jnp
from jax import lax
from jax.sharding import PartitionSpec as P

norm_eps = 1e-05
bf16 = jnp.bfloat16
f32 = jnp.float32


def rms(value_rows_segment):
    return value_rows_segment * lax.rsqrt(
        jnp.mean(value_rows_segment * value_rows_segment, axis=-1, keepdims=True) + norm_eps
    )


def feature(value_rows_segment):
    return jnp.where(
        value_rows_segment > 0,
        value_rows_segment + 1.0,
        jnp.exp(jnp.minimum(value_rows_segment, 0.0)),
    )


def swiglu(gate_part, up_part):
    return jax.nn.silu(gate_part) * up_part


def local_memory(query, key, value_rows_segment, memory_matrix_entry, normalizer_entry):
    high = lax.Precision.HIGHEST
    feature_queries = feature(query)
    feature_keys = feature(key)
    attention_memory_mix = (
        jnp.einsum("zqi,qis->zqs", feature_queries, memory_matrix_entry, precision=high)
        / jnp.einsum("rzo,zo->rz", feature_queries, normalizer_entry, precision=high)[..., None]
    )
    memory_recall_read = (
        jnp.einsum("zqi,qis->zqs", feature_keys, memory_matrix_entry, precision=high)
        / jnp.einsum("rzo,zo->rz", feature_keys, normalizer_entry, precision=high)[..., None]
    )
    memory_delta_write = jnp.einsum(
        "ubf,ubc->bfc", feature_keys, value_rows_segment - memory_recall_read, precision=high
    )
    return (attention_memory_mix, memory_delta_write, jnp.sum(feature_keys, axis=0))


def ring_order(n):
    if n % 4 or n < 8:
        return list(range(n))
    wide = n // 4
    walk = []
    for r in range(4):
        cols = range(1, wide) if r % 2 == 0 else range(wide - 1, 0, -1)
        walk += [r * wide + c for c in cols]
    return walk + [r * wide for r in reversed(range(4))]


def tie(value, other):
    return lax.optimization_barrier((value, other))[0]


class Ring:
    def __init__(self, n):
        self.n = n
        self.order = ring_order(n)
        self.where = [self.order.index(i) for i in range(n)]
        self.me = lax.axis_index("fsdp")
        self.order_array = jnp.array(self.order, dtype=jnp.int32)
        self.at = jnp.array(self.where, dtype=jnp.int32)[self.me]

    def owner(self, step, way):
        return self.order_array[(self.at - way * step) % self.n]

    def send(self, value, way):
        n, order = self.n, self.order
        return lax.ppermute(
            value, "fsdp", [(order[p], order[(p + way) % n]) for p in range(n)]
        )

    def gather(self, block, way):
        out = jnp.zeros((self.n,) + block.shape, block.dtype)
        out = lax.dynamic_update_slice(out, block[None], (self.me,) + (0,) * block.ndim)
        travelling = block
        marks = []
        for step in range(1, self.n):
            travelling = self.send(travelling, way)
            marks.append(travelling)
            out = lax.dynamic_update_slice(
                out, travelling[None], (self.owner(step, way),) + (0,) * block.ndim
            )
        return out, marks

    def scatter(self, parts, way):
        def part(step):
            return lax.dynamic_index_in_dim(parts, self.owner(step, way), 0, keepdims=False)

        travelling = part(1 - self.n)
        for step in range(2 - self.n, 1):
            arrived = self.send(travelling, way)
            travelling = (arrived.astype(f32) + part(step).astype(f32)).astype(bf16)
        return travelling


class Team:
    def __init__(self, n):
        self.n = n
        self.me = lax.axis_index("seq")

    def send(self, value, other):
        return lax.ppermute(value, "seq", [(i, other(i)) for i in range(self.n)])

    def gather(self, block):
        n = self.n
        held = [(self.me, block)]
        travelling = block
        for step in range(1, n // 2):
            travelling = self.send(travelling, lambda i: (i + 2) % n)
            held.append(((self.me - 2 * step) % n, travelling))
        held += [(i ^ 1, self.send(value, lambda i: i ^ 1)) for i, value in list(held)]
        return held

    def scatter(self, part):
        n, pairs = self.n, self.n // 2
        other = self.me ^ 1

        def at(base, k):
            return (base + 2 * k) % n

        sums = [None] * pairs
        for k in reversed(range(pairs)):
            arrived = self.send(part(at(other, k)), lambda i: i ^ 1)
            sums[k] = arrived.astype(f32) + part(at(self.me, k)).astype(f32)
        total = sums[pairs - 1]
        for step in range(pairs - 1):
            arrived = self.send(total.astype(bf16), lambda i: (i + 2) % n)
            total = arrived.astype(f32) + sums[(-2 - step) % pairs]
        return total

    def exchange(self, part):
        held = [(self.me, part(self.me))]
        for k in range(1, self.n):
            held.append((self.me ^ k, self.send(part(self.me ^ k), lambda i: i ^ k)))
        return held


def place(held, axis, count):
    out = jnp.zeros((count,) + held[0][1].shape, held[0][1].dtype)
    for i, value in held:
        out = lax.dynamic_update_slice(out, value[None], (i,) + (0,) * value.ndim)
    return jnp.squeeze(jnp.moveaxis(out, 0, axis), axis + 1)


def mm(left, right):
    return jnp.dot(left, right, preferred_element_type=f32)


def mm_nt(left, right):
    return lax.dot_general(left, right, (((1,), (1,)), ((), ())), preferred_element_type=f32)


def mm_tn(left, right):
    return lax.dot_general(left, right, (((0,), (0,)), ((), ())), preferred_element_type=f32)


def make_body(n_seq, n_fsdp):
    def body(
        tokens,
        cotangent,
        w_qkv,
        w_out,
        w_gate_up,
        w_down,
        gain_attn,
        gain_ffn,
        gate_bias,
        memory_in,
        norms_in,
        resets,
        depth,
    ):
        _, segs, local, width = tokens.shape
        heads = gate_bias.shape[0]
        hdim = width // heads
        my_heads = heads // n_seq
        my_width = width // n_seq
        seg = local * n_seq
        rows = segs * local
        total_rows = segs * seg
        shard = w_qkv.shape[0]
        hidden_shard = w_down.shape[0]
        my_hidden = hidden_shard // n_seq
        scale = 1.0 / hdim**0.5
        ring = Ring(n_fsdp)
        team = Team(n_seq)
        me = team.me

        def mine(array, axis):
            return lax.dynamic_index_in_dim(array, me, axis, keepdims=False)

        qkv_own = mine(w_qkv.reshape(shard, 3, n_seq, my_width), 2)
        gate_up_own = mine(w_gate_up.reshape(shard, 2, n_fsdp, n_seq, my_hidden), 3)
        down_own = mine(w_down.reshape(n_seq, my_hidden, width), 0)
        out_rows = shard // n_seq
        out_own = mine(w_out.reshape(n_seq, out_rows, width), 0)

        def gather_rows(block, after):
            half = block.shape[0] // 2
            top, bottom = block[:half], block[half:]
            if after is not None:
                top, bottom = tie(top, after[0]), tie(bottom, after[1])
            a, marks_a = ring.gather(top, 1)
            b, marks_b = ring.gather(bottom, -1)
            return jnp.stack([a, b], axis=1), (marks_a[-2], marks_b[-2])

        def gather_pair(one, two, after):
            a, marks_a = ring.gather(tie(one, after[0]), 1)
            b, marks_b = ring.gather(tie(two, after[1]), -1)
            return a, b, (marks_a[-2], marks_b[-2])

        w_q, after = gather_rows(qkv_own.reshape(shard, 3 * my_width), None)
        w_q = w_q.reshape(width, 3 * my_width)
        w_o, after = gather_rows(out_own, after)
        w_o = w_o.reshape(n_fsdp, 1, out_rows, width)
        w_o = place(team.gather(w_o), 1, n_seq).reshape(width, width)
        w_g, w_u, after = gather_pair(
            gate_up_own[:, 0].reshape(shard, -1), gate_up_own[:, 1].reshape(shard, -1), after
        )
        w_g = w_g.reshape(width, -1)
        w_u = w_u.reshape(width, -1)
        w_d, after = gather_rows(down_own, after)
        w_d = w_d.reshape(n_fsdp * my_hidden, width)

        def gather_tokens(value):
            held = team.gather(value.reshape(segs, 1, local, width))
            return place(held, 1, n_seq).reshape(total_rows, width)

        def scatter_tokens(value):
            parts = value.reshape(segs, n_seq, local, width)
            return team.scatter(
                lambda i: lax.dynamic_index_in_dim(parts, i, 1, keepdims=False)
            ).reshape(rows, width)

        x_flat = tokens.reshape(rows, width).astype(f32)
        r_one = rms(x_flat)
        h_one = gather_tokens((r_one * gain_attn).astype(bf16))
        grad_y = cotangent.reshape(rows, width)
        grad_y_all = gather_tokens(grad_y)

        qkv = mm(h_one, w_q).astype(bf16).reshape(segs, seg, 3, my_heads, hdim)
        places = jnp.arange(seg, dtype=jnp.int32)
        allowed = (places[None, :] <= places[:, None])[None]
        bias = lax.dynamic_slice(gate_bias, (me * my_heads,), (my_heads,))
        gate = jax.nn.sigmoid(bias)[None, :, None]
        memory = lax.dynamic_slice(
            memory_in[0], (me * my_heads, 0, 0), (my_heads, hdim, hdim)
        )
        norms = lax.dynamic_slice(norms_in[0], (me * my_heads, 0), (my_heads, hdim))
        saved = []
        mixes = []
        for s in range(segs):
            query, key, value = qkv[s, :, 0], qkv[s, :, 1], qkv[s, :, 2]
            scores = jnp.einsum("qhd,khd->hqk", query, key, preferred_element_type=f32) * scale
            scores = jnp.where(allowed, scores, -1e30)
            top = jnp.max(scores, axis=-1, keepdims=True)
            weights = jnp.exp(scores - top)
            total = jnp.sum(weights, axis=-1, keepdims=True)
            probs = (weights / total).astype(bf16)
            lse = top + jnp.log(total)
            adot = jnp.einsum("hqk,khd->qhd", probs, value, preferred_element_type=f32)
            if s > 0:
                fresh = resets[0, s - 1] > 0
                memory = jnp.where(fresh, jnp.zeros_like(memory), memory)
                norms = jnp.where(fresh, jnp.ones_like(norms), norms)
            qf, kf, vf = query.astype(f32), key.astype(f32), value.astype(f32)
            amem, delta, key_sum = local_memory(qf, kf, vf, memory, norms)
            mixes.append((gate * amem + (1.0 - gate) * adot).reshape(seg, my_width))
            saved.append((query, key, value, lse, adot, amem, qf, kf, vf, memory, norms))
            memory = memory + delta
            norms = norms + key_sum
        attn_heads = jnp.stack(mixes).astype(bf16).reshape(segs, n_seq, local, my_width)
        attn = place(
            team.exchange(
                lambda i: lax.dynamic_index_in_dim(attn_heads, i, 1, keepdims=False).reshape(
                    rows, 1, my_width
                )
            ),
            1,
            n_seq,
        ).reshape(rows, width)
        x_one = x_flat + mm(attn, w_o)
        r_two = rms(x_one)
        h_two = gather_tokens((r_two * gain_ffn).astype(bf16))
        gate_part = mm(h_two, w_g).astype(bf16)
        up_part = mm(h_two, w_u).astype(bf16)
        hidden = swiglu(gate_part.astype(f32), up_part.astype(f32)).astype(bf16)
        output = x_one + scatter_tokens(mm(hidden, w_d).astype(bf16))
        output = output.astype(bf16).reshape(tokens.shape)

        def scatter_ring(left, grad, shape, way):
            parts = mm_tn(left, grad).astype(bf16)
            return ring.scatter(parts.reshape((n_fsdp, -1) + parts.shape[1:]), way)

        half = width // 2
        down_terms = (
            scatter_ring(hidden, grad_y_all[:, :half], None, 1),
            scatter_ring(hidden, grad_y_all[:, half:], None, -1),
        )
        grad_hidden = mm_nt(grad_y_all, w_d)
        _, swiglu_back = jax.vjp(swiglu, gate_part.astype(f32), up_part.astype(f32))
        grad_gate, grad_up = swiglu_back(grad_hidden)
        grad_gate, grad_up = grad_gate.astype(bf16), grad_up.astype(bf16)
        gate_up_terms = (
            scatter_ring(h_two, grad_gate, None, 1),
            scatter_ring(h_two, grad_up, None, -1),
        )
        grad_h_two = scatter_tokens((mm_nt(grad_gate, w_g) + mm_nt(grad_up, w_u)).astype(bf16))
        gain_ffn_term = jnp.sum(grad_h_two * r_two, axis=0)
        _, norm_two_back = jax.vjp(rms, x_one)
        grad_x_one = grad_y.astype(f32) + norm_two_back(grad_h_two * gain_ffn)[0]
        grad_o = grad_x_one.astype(bf16)

        out_parts = mm_tn(attn, grad_o).astype(bf16).reshape(n_fsdp, n_seq, out_rows, width)
        out_sum = team.scatter(
            lambda i: lax.dynamic_index_in_dim(out_parts, i, 1, keepdims=False)
        ).astype(bf16)
        out_terms = (
            ring.scatter(out_sum[:, : out_rows // 2], 1),
            ring.scatter(out_sum[:, out_rows // 2 :], -1),
        )

        grad_attn = mm_nt(grad_o, w_o).astype(bf16).reshape(rows, n_seq, my_width)
        grad_attn = place(
            team.exchange(
                lambda i: lax.dynamic_index_in_dim(grad_attn, i, 1, keepdims=False).reshape(
                    segs, 1, local, my_width
                )
            ),
            1,
            n_seq,
        )
        grad_attn = grad_attn.astype(f32).reshape(segs, seg, my_heads, hdim)
        bias_term = jnp.zeros((my_heads,), f32)
        grads = [None] * segs
        grad_m = jnp.zeros((my_heads, hdim, hdim), f32)
        grad_z = jnp.zeros((my_heads, hdim), f32)
        for s in reversed(range(segs)):
            query, key, value, lse, adot, amem, qf, kf, vf, memory, norms = saved[s]
            grad_mix = grad_attn[s]
            bias_term = (
                bias_term
                + jnp.sum(grad_mix * (amem - adot), axis=(0, 2)) * (gate * (1.0 - gate))[0, :, 0]
            )
            grad_amem = gate * grad_mix
            grad_adot = ((1.0 - gate) * grad_mix).astype(bf16)
            scores = jnp.einsum("qhd,khd->hqk", query, key, preferred_element_type=f32) * scale
            scores = jnp.where(allowed, scores, -1e30)
            probs = jnp.exp(scores - lse)
            grad_p = jnp.einsum("qhd,khd->hqk", grad_adot, value, preferred_element_type=f32)
            grad_s = (
                probs * (grad_p - jnp.sum(probs * grad_p, axis=-1, keepdims=True))
            ).astype(bf16)
            q_att = jnp.einsum("hqk,khd->qhd", grad_s, key, preferred_element_type=f32) * scale
            k_att = jnp.einsum("hqk,qhd->khd", grad_s, query, preferred_element_type=f32) * scale
            v_att = jnp.einsum(
                "hqk,qhd->khd", probs.astype(bf16), grad_adot, preferred_element_type=f32
            )
            _, memory_back = jax.vjp(local_memory, qf, kf, vf, memory, norms)
            q_mem, k_mem, v_mem, m_back, z_back = memory_back((grad_amem, grad_m, grad_z))
            if s > 0:
                cut = (resets[0, s - 1] > 0) | (s % depth[0] == 0)
                grad_m = jnp.where(cut, jnp.zeros_like(grad_m), m_back + grad_m)
                grad_z = jnp.where(cut, jnp.zeros_like(grad_z), z_back + grad_z)
            grads[s] = jnp.stack(
                [q_att + q_mem, k_att + k_mem, v_att + v_mem], axis=1
            ).astype(bf16)
        grad_qkv_rows = jnp.stack(grads).reshape(total_rows, 3 * my_width)
        half = 3 * my_width // 2
        qkv_terms = (
            scatter_ring(h_one, grad_qkv_rows[:, :half], None, 1),
            scatter_ring(h_one, grad_qkv_rows[:, half:], None, -1),
        )
        grad_h_one = scatter_tokens(mm_nt(grad_qkv_rows, w_q).astype(bf16))
        gain_attn_term = jnp.sum(grad_h_one * r_one, axis=0)
        _, norm_one_back = jax.vjp(rms, x_flat)
        grad_x = grad_x_one + norm_one_back(grad_h_one * gain_attn)[0]
        input_grad = grad_x.astype(bf16).reshape(tokens.shape)

        down_all = place(
            team.gather(jnp.concatenate(down_terms, axis=-1)[None]), 0, n_seq
        ).reshape(hidden_shard, width)
        gate_up_all = place(
            team.gather(jnp.stack(gate_up_terms, axis=1).reshape(shard, 2, n_fsdp, 1, my_hidden)),
            3,
            n_seq,
        ).reshape(shard, -1)
        out_all = place(team.gather(jnp.concatenate(out_terms, axis=0)[None]), 0, n_seq).reshape(
            shard, width
        )
        qkv_all = place(
            team.gather(jnp.concatenate(qkv_terms, axis=-1).reshape(shard, 3, 1, my_width)),
            2,
            n_seq,
        ).reshape(shard, -1)
        bias_all = lax.dynamic_update_slice(
            jnp.zeros((heads,), f32), bias_term, (me * my_heads,)
        )
        grad_gain_attn, grad_gain_ffn, grad_gate_bias = lax.psum(
            (gain_attn_term, gain_ffn_term, bias_all), ("seq", "fsdp")
        )
        return (
            output,
            input_grad,
            qkv_all.astype(f32),
            out_all.astype(f32),
            gate_up_all.astype(f32),
            down_all.astype(f32),
            grad_gain_attn,
            grad_gain_ffn,
            grad_gate_bias,
        )

    return body


def solution(mesh):
    in_specs = (
        P("fsdp", None, "seq", None),
        P("fsdp", None, "seq", None),
        P("fsdp", None),
        P("fsdp", None),
        P("fsdp", None),
        P("fsdp", None),
        P(),
        P(),
        P(),
        P("fsdp", None, None, None),
        P("fsdp", None, None),
        P("fsdp", None),
        P("fsdp"),
    )
    out_specs = (
        P("fsdp", None, "seq", None),
        P("fsdp", None, "seq", None),
        P("fsdp", None),
        P("fsdp", None),
        P("fsdp", None),
        P("fsdp", None),
        P(),
        P(),
        P(),
    )
    body = make_body(mesh.shape["seq"], mesh.shape["fsdp"])
    return jax.shard_map(body, mesh=mesh, in_specs=in_specs, out_specs=out_specs, check_vma=False)
```

```python
import functools

import jax
import jax.numpy as jnp
from jax import lax
from jax.experimental import pallas as pl
from jax.experimental.pallas import tpu as pltpu
from jax.sharding import PartitionSpec as P

norm_eps = 1e-05
bf16 = jnp.bfloat16
f32 = jnp.float32


def rms(value_rows_segment):
    return value_rows_segment * lax.rsqrt(
        jnp.mean(value_rows_segment * value_rows_segment, axis=-1, keepdims=True) + norm_eps
    )


def swiglu(gate_part, up_part):
    return jax.nn.silu(gate_part) * up_part


def feature(value_rows_segment):
    return jnp.where(
        value_rows_segment > 0,
        value_rows_segment + 1.0,
        jnp.exp(jnp.minimum(value_rows_segment, 0.0)),
    )


def contract(left, right, left_dim, right_dim):
    return lax.dot_general(
        left, right, (((left_dim,), (right_dim,)), ((), ())), preferred_element_type=f32
    )


def split(value):
    high = value.astype(bf16)
    return high, (value - high.astype(f32)).astype(bf16)


def fine(left, right, left_dim, right_dim):
    lh, ll = left
    rh, rl = right
    return (
        contract(lh, rl, left_dim, right_dim)
        + contract(ll, rh, left_dim, right_dim)
        + contract(lh, rh, left_dim, right_dim)
    )


LOG2E = 1.4426950408889634


def scores_of(key, query, block, i):
    n = (i + 1) * block
    sc = contract(key[:n], query, 1, 1)
    rows = lax.broadcasted_iota(jnp.int32, (block, block), 0)
    cols = lax.broadcasted_iota(jnp.int32, (block, block), 1)
    last = jnp.where(rows <= cols, sc[n - block :], -1e30)
    if i == 0:
        return last
    return jnp.concatenate([sc[: n - block], last], axis=0)


def forward_kernel(
    block, segs, gate, resets, q_ref, k_ref, v_ref, m_ref, z_ref, a_ref, lse_ref, mem_ref, nrm_ref, mem, nrm
):
    h, s = pl.program_id(0), pl.program_id(1)
    seg, hdim = q_ref.shape
    scale = LOG2E / hdim**0.5

    @pl.when(s == 0)
    def _():
        mem[...] = m_ref[0]
        nrm[...] = z_ref[0]

    @pl.when(s > 0)
    def _():
        @pl.when(resets[jnp.maximum(s - 1, 0)] > 0)
        def _():
            mem[...] = jnp.zeros_like(mem)
            nrm[...] = jnp.ones_like(nrm)

    mem_ref[0, 0] = mem[...]
    nrm_ref[0, 0] = nrm[...]
    g = gate[h]
    mem_parts = split(mem[...])
    key, value = k_ref[...], v_ref[...]
    value_t = value.T
    for i in range(seg // block):
        rows = slice(i * block, (i + 1) * block)
        query = q_ref[rows, :]
        sc = scores_of(key, query, block, i)
        top = jnp.max(sc, axis=0, keepdims=True)
        weights = jnp.exp2((sc - top) * scale)
        total = jnp.sum(weights, axis=0, keepdims=True)
        lse_ref[0, 0, :, rows] = top * scale + jnp.log2(total)
        adot_t = contract(value_t[:, : (i + 1) * block], weights.astype(bf16), 1, 0)
        adot_t = adot_t * ((1.0 - g) / total)
        sq = feature(query.astype(f32))
        amem = fine(split(sq), mem_parts, 1, 0) * (
            g / jnp.sum(sq * nrm[...], axis=1, keepdims=True)
        )
        a_ref[rows, :] = (amem + adot_t.T).astype(bf16)

    @pl.when(s + 1 < segs)
    def _():
        sk = feature(key.astype(f32))
        sk_parts = split(sk)
        recall = fine(sk_parts, mem_parts, 1, 0) / jnp.sum(sk * nrm[...], axis=1, keepdims=True)
        delta = split(value.astype(f32) - recall)
        mem[...] = mem[...] + fine(sk_parts, delta, 0, 0)
        nrm[...] = nrm[...] + jnp.sum(sk, axis=0, keepdims=True)


def specs(seg, hdim, heads, back, segs):
    def at(part):
        return pl.BlockSpec(
            (seg, hdim), lambda h, t: ((segs - 1 - t) if back else t, part * heads + h)
        )

    return at


def attention_forward(qkv, gate, resets, memory, norms, segs):
    total_rows, cols = qkv.shape
    heads, hdim, _ = memory.shape
    seg = total_rows // segs
    at = specs(seg, hdim, heads, False, segs)
    return pl.pallas_call(
        functools.partial(forward_kernel, min(256, seg), segs),
        grid=(heads, segs),
        in_specs=[
            pl.BlockSpec(memory_space=pltpu.SMEM),
            pl.BlockSpec(memory_space=pltpu.SMEM),
            at(0),
            at(1),
            at(2),
            pl.BlockSpec((1, hdim, hdim), lambda h, t: (h, 0, 0)),
            pl.BlockSpec((1, 1, hdim), lambda h, t: (h, 0, 0)),
        ],
        out_specs=[
            at(0),
            pl.BlockSpec((1, 1, 1, seg), lambda h, t: (h, t, 0, 0)),
            pl.BlockSpec((1, 1, hdim, hdim), lambda h, t: (h, t, 0, 0)),
            pl.BlockSpec((1, 1, 1, hdim), lambda h, t: (h, t, 0, 0)),
        ],
        out_shape=[
            jax.ShapeDtypeStruct((total_rows, heads * hdim), bf16),
            jax.ShapeDtypeStruct((heads, segs, 1, seg), f32),
            jax.ShapeDtypeStruct((heads, segs, hdim, hdim), f32),
            jax.ShapeDtypeStruct((heads, segs, 1, hdim), f32),
        ],
        scratch_shapes=[pltpu.VMEM((hdim, hdim), f32), pltpu.VMEM((1, hdim), f32)],
        compiler_params=pltpu.CompilerParams(vmem_limit_bytes=48 << 20),
        cost_estimate=pl.CostEstimate(
            flops=30 * total_rows * seg * heads * hdim // 8,
            bytes_accessed=4 * total_rows * cols,
            transcendentals=total_rows * seg * heads // 2,
        ),
        name="attention_forward",
    )(gate, resets, qkv, qkv, qkv, memory, norms.reshape(heads, 1, hdim))


def backward_kernel(
    block, segs, gate, resets, depth, q_ref, k_ref, v_ref, da_ref, lse_ref, mem_ref, nrm_ref,
    dq_ref, dk_ref, dv_ref, bias_ref, dm, dz, dk_att, dv_att,
):
    h, t = pl.program_id(0), pl.program_id(1)
    s = segs - 1 - t
    seg, hdim = q_ref.shape
    scale = 1.0 / hdim**0.5
    g = gate[h]

    @pl.when(t == 0)
    def _():
        dm[...] = jnp.zeros_like(dm)
        dz[...] = jnp.zeros_like(dz)
        bias_ref[...] = jnp.zeros_like(bias_ref)

    dk_att[...] = jnp.zeros_like(dk_att)
    dv_att[...] = jnp.zeros_like(dv_att)
    mem, nrm = mem_ref[0, 0], nrm_ref[0, 0]
    mem_parts = split(mem)
    key, value = k_ref[...], v_ref[...]
    key_t = key.T
    term = jnp.zeros((1, 1), f32)
    m_next = jnp.zeros((hdim, hdim), f32)
    z_next = jnp.zeros((1, hdim), f32)
    for i in range(seg // block):
        n = (i + 1) * block
        rows = slice(i * block, n)
        query = q_ref[rows, :]
        sc = scores_of(key, query, block, i)
        probs = jnp.exp2(sc * (scale * LOG2E) - lse_ref[0, 0, :, rows])
        grad_mix = da_ref[rows, :].astype(f32)
        grad_adot = ((1.0 - g) * grad_mix).astype(bf16)
        grad_p = contract(value[:n], grad_adot, 1, 1)
        row = jnp.sum(probs * grad_p, axis=0, keepdims=True)
        grad_s = (probs * (grad_p - row)).astype(bf16)
        dk_att[:n, :] += contract(grad_s, query, 1, 0)
        dv_att[:n, :] += contract(probs.astype(bf16), grad_adot, 1, 0)
        dq = contract(key_t[:, :n], grad_s, 1, 0).T * scale

        qf = query.astype(f32)
        sq = feature(qf)
        slope = jnp.where(qf > 0, 1.0, sq)
        sq_parts = split(sq)
        inverse = 1.0 / jnp.sum(sq * nrm, axis=1, keepdims=True)
        amem = fine(sq_parts, mem_parts, 1, 0) * inverse
        mixed = jnp.sum(grad_mix * amem, axis=1, keepdims=True)
        term = term + (g * (1.0 - g)) * jnp.sum(mixed, axis=0, keepdims=True)
        term = term - g * jnp.sum(row, axis=1, keepdims=True)
        d_top = split(grad_mix * (g * inverse))
        d_low = -(g * mixed) * inverse
        d_sq = fine(d_top, mem_parts, 1, 1) + d_low * nrm
        dq_ref[rows, :] = (dq + d_sq * slope).astype(bf16)
        m_next = m_next + fine(sq_parts, d_top, 0, 0)
        z_next = z_next + jnp.sum(sq * d_low, axis=0, keepdims=True)
    bias_ref[...] += jnp.broadcast_to(term[None], bias_ref.shape)
    dk_ref[...] = (dk_att[...] * scale).astype(bf16)
    dv_ref[...] = dv_att[...].astype(bf16)

    @pl.when(s + 1 < segs)
    def _():
        dm_now, dz_now = dm[...], dz[...]
        dm_parts = split(dm_now)
        kf = key.astype(f32)
        sk = feature(kf)
        slope = jnp.where(kf > 0, 1.0, sk)
        sk_parts = split(sk)
        inverse = 1.0 / jnp.sum(sk * nrm, axis=1, keepdims=True)
        recall = fine(sk_parts, mem_parts, 1, 0) * inverse
        delta = value.astype(f32) - recall
        d_delta = fine(sk_parts, dm_parts, 1, 0)
        d_top = split(-d_delta * inverse)
        d_low = jnp.sum(d_delta * recall, axis=1, keepdims=True) * inverse
        d_sk = (
            fine(split(delta), dm_parts, 1, 1)
            + dz_now
            + fine(d_top, mem_parts, 1, 1)
            + d_low * nrm
        )
        dk_ref[...] = (dk_att[...] * scale + d_sk * slope).astype(bf16)
        dv_ref[...] = (dv_att[...] + d_delta).astype(bf16)
        dm[...] = dm_now + fine(sk_parts, d_top, 0, 0)
        dz[...] = dz_now + jnp.sum(sk * d_low, axis=0, keepdims=True)

    @pl.when(s > 0)
    def _():
        cut = (resets[jnp.maximum(s - 1, 0)] > 0) | (lax.rem(s, depth[0]) == 0)
        dm[...] = jnp.where(cut, 0.0, dm[...] + m_next)
        dz[...] = jnp.where(cut, 0.0, dz[...] + z_next)


def attention_backward(qkv, grad_attn, gate, resets, depth, lse, mems, nrms, segs):
    total_rows, cols = qkv.shape
    heads, _, hdim, _ = mems.shape
    seg = total_rows // segs
    at = specs(seg, hdim, heads, True, segs)
    smem = pl.BlockSpec(memory_space=pltpu.SMEM)
    grad = jax.ShapeDtypeStruct((total_rows, heads * hdim), bf16)
    return pl.pallas_call(
        functools.partial(backward_kernel, min(256, seg), segs),
        grid=(heads, segs),
        in_specs=[
            smem,
            smem,
            smem,
            at(0),
            at(1),
            at(2),
            at(0),
            pl.BlockSpec((1, 1, 1, seg), lambda h, t: (h, segs - 1 - t, 0, 0)),
            pl.BlockSpec((1, 1, hdim, hdim), lambda h, t: (h, segs - 1 - t, 0, 0)),
            pl.BlockSpec((1, 1, 1, hdim), lambda h, t: (h, segs - 1 - t, 0, 0)),
        ],
        out_specs=[at(0), at(0), at(0), pl.BlockSpec((1, 8, hdim), lambda h, t: (h, 0, 0))],
        out_shape=[grad, grad, grad, jax.ShapeDtypeStruct((heads, 8, hdim), f32)],
        scratch_shapes=[
            pltpu.VMEM((hdim, hdim), f32),
            pltpu.VMEM((1, hdim), f32),
            pltpu.VMEM((seg, hdim), f32),
            pltpu.VMEM((seg, hdim), f32),
        ],
        compiler_params=pltpu.CompilerParams(vmem_limit_bytes=48 << 20),
        cost_estimate=pl.CostEstimate(
            flops=60 * total_rows * seg * heads * hdim // 8,
            bytes_accessed=4 * total_rows * cols,
            transcendentals=total_rows * seg * heads // 2,
        ),
        name="attention_backward",
    )(gate, resets, depth, qkv, qkv, qkv, grad_attn, lse, mems, nrms)


def tie(value, *others):
    return lax.optimization_barrier((value,) + others)[0]


MESH = pl.DeviceIdType.MESH


class Team:
    def __init__(self, n):
        self.n = n
        self.pairs = n // 2
        self.me = lax.axis_index("seq")
        self.calls = 0

    def call(self, kernel, inputs, out_shapes, scratch, name, cost):
        self.calls += 1
        anywhere = pl.BlockSpec(memory_space=pl.ANY)
        return pl.pallas_call(
            kernel,
            in_specs=[anywhere] * len(inputs),
            out_specs=[anywhere] * len(out_shapes),
            out_shape=out_shapes,
            scratch_shapes=scratch,
            compiler_params=pltpu.CompilerParams(
                collective_id=self.calls, has_side_effects=True, vmem_limit_bytes=48 << 20
            ),
            cost_estimate=pl.CostEstimate(flops=0, bytes_accessed=cost, transcendentals=0),
            name=name,
        )(*inputs)

    @staticmethod
    def greet(peers):
        barrier = pltpu.get_barrier_semaphore()
        for peer in peers:
            pl.semaphore_signal(barrier, inc=1, device_id={"seq": peer}, device_id_type=MESH)
        pl.semaphore_wait(barrier, len(peers))

    def gather(self, blocks, outer):
        n, pairs, count = self.n, self.pairs, len(blocks)
        shapes = [
            jax.ShapeDtypeStruct(
                ((n, b.shape[0]) if outer else (b.shape[0], n)) + b.shape[1:], b.dtype
            )
            for b in blocks
        ]
        steps = [(a, c) for a, b in enumerate(blocks) for c in range(b.shape[0])]
        total = len(steps)

        def kernel(*refs):
            ins, outs = refs[:count], refs[count : 2 * count]
            keep, y_out, y_in, c_out, c_in = refs[2 * count :]
            me = lax.axis_index("seq")
            core = lax.rem(me, 2)
            partner = me + 1 - 2 * core
            ahead = [lax.rem(me + 2 * k, n) for k in range(pairs)]
            behind = [lax.rem(me + n - 2 * k, n) for k in range(pairs)]
            self.greet([partner] + ahead[1:])

            def at(a, dev, c):
                return outs[a].at[dev, c] if outer else outs[a].at[c, dev]

            def remote(src, a, dev, c, out_sem, in_sem, to):
                return pltpu.make_async_remote_copy(
                    src_ref=src,
                    dst_ref=at(a, dev, c),
                    send_sem=out_sem,
                    recv_sem=in_sem,
                    device_id={"seq": to},
                    device_id_type=MESH,
                )

            started = []
            for i, (a, c) in enumerate(steps):
                for k in range(1, pairs):
                    copy = remote(
                        ins[a].at[c], a, me, c, y_out.at[k - 1, i], y_in.at[k - 1, i], ahead[k]
                    )
                    copy.start()
                    started.append(copy)
            crossed = []
            for i, (a, c) in enumerate(steps):
                copy = remote(ins[a].at[c], a, me, c, c_out.at[0, i], c_in.at[0, i], partner)
                copy.start()
                crossed.append(copy)
                copy = pltpu.make_async_copy(ins[a].at[c], at(a, me, c), keep.at[i])
                copy.start()
            for i, (a, c) in enumerate(steps):
                for k in range(1, pairs):
                    remote(
                        ins[a].at[c], a, behind[k], c, y_out.at[k - 1, i], y_in.at[k - 1, i], ahead[k]
                    ).wait_recv()
                    copy = remote(
                        at(a, behind[k], c),
                        a,
                        behind[k],
                        c,
                        c_out.at[k, i],
                        c_in.at[k, i],
                        partner,
                    )
                    copy.start()
                    crossed.append(copy)
            for copy in started:
                copy.wait_send()
            for copy in crossed:
                copy.wait()
            for i, (a, c) in enumerate(steps):
                pltpu.make_async_copy(ins[a].at[c], at(a, me, c), keep.at[i]).wait()

        dma = pltpu.SemaphoreType.DMA
        held = max(pairs - 1, 1)
        return self.call(
            kernel,
            blocks,
            shapes,
            [
                dma((total,)),
                dma((held, total)),
                dma((held, total)),
                dma((pairs, total)),
                dma((pairs, total)),
            ],
            "gather_team",
            sum(60 * b.size * 2 for b in blocks),
        )

    def exchange(self, array, out_shape, source, target):
        n = self.n

        def kernel(in_ref, out_ref, keep, out_sem, in_sem):
            me = lax.axis_index("seq")
            core = lax.rem(me, 2)
            peers = [
                lax.rem(me - core + 2 * k, n) + (1 - core if flip else core)
                for k in range(self.pairs)
                for flip in (False, True)
            ]
            self.greet(peers[1:])
            own = pltpu.make_async_copy(source(in_ref, me), target(out_ref, me), keep)
            own.start()
            copies = []
            for k in reversed(range(1, n)):
                copy = pltpu.make_async_remote_copy(
                    src_ref=source(in_ref, peers[k]),
                    dst_ref=target(out_ref, me),
                    send_sem=out_sem.at[k - 1],
                    recv_sem=in_sem.at[k - 1],
                    device_id={"seq": peers[k]},
                    device_id_type=MESH,
                )
                copy.start()
                copies.append(copy)
            for copy in copies:
                copy.wait()
            own.wait()

        dma = pltpu.SemaphoreType.DMA
        return self.call(
            kernel,
            [array],
            [jax.ShapeDtypeStruct(out_shape, array.dtype)],
            [dma, dma((n - 1,)), dma((n - 1,))],
            "exchange_team",
            40 * array.size * 2,
        )[0]

    def scatter(self, parts, dtype):
        chunks, n, rows, columns = parts.shape
        pairs = self.pairs
        held = max(pairs - 1, 1)

        def kernel(in_ref, out_ref, mine, met, sent, come, result, load, c_out, c_in, y_out, y_in, store):
            me = lax.axis_index("seq")
            core = lax.rem(me, 2)
            partner = me + 1 - 2 * core
            ahead = [lax.rem(me + 2 * k, n) for k in range(pairs)]
            self.greet([partner] + ahead[1:])
            order = [(k, c) for k in list(range(1, pairs)) + [0] for c in range(chunks)]

            def read(k, c):
                return pltpu.make_async_copy(in_ref.at[c, ahead[k]], mine.at[k, c], load.at[k, c])

            def cross(k, c):
                return pltpu.make_async_remote_copy(
                    src_ref=in_ref.at[c, lax.rem(partner + 2 * k, n)],
                    dst_ref=met.at[k, c],
                    send_sem=c_out.at[k, c],
                    recv_sem=c_in.at[k, c],
                    device_id={"seq": partner},
                    device_id_type=MESH,
                )

            def pass_on(k, c):
                return pltpu.make_async_remote_copy(
                    src_ref=sent.at[k - 1, c],
                    dst_ref=come.at[k - 1, c],
                    send_sem=y_out.at[k - 1, c],
                    recv_sem=y_in.at[k - 1, c],
                    device_id={"seq": ahead[k]},
                    device_id_type=MESH,
                )

            for k, c in order:
                cross(k, c).start()
                read(k, c).start()
            for k, c in order:
                cross(k, c).wait_recv()
                read(k, c).wait()
                if k:
                    sent[k - 1, c] = (mine[k, c].astype(f32) + met[k, c].astype(f32)).astype(bf16)
                    pass_on(k, c).start()
            for c in range(chunks):
                total = mine[0, c].astype(f32) + met[0, c].astype(f32)
                for k in range(1, pairs):
                    pass_on(k, c).wait_recv()
                    total = total + come[k - 1, c].astype(f32)
                result[c] = total.astype(dtype)
                pltpu.make_async_copy(result.at[c], out_ref.at[c], store.at[c]).start()
            for k, c in order:
                cross(k, c).wait_send()
                if k:
                    pass_on(k, c).wait_send()
            for c in range(chunks):
                pltpu.make_async_copy(result.at[c], out_ref.at[c], store.at[c]).wait()

        dma = pltpu.SemaphoreType.DMA
        block = (chunks, rows, columns)
        return self.call(
            kernel,
            [parts],
            [jax.ShapeDtypeStruct(block, dtype)],
            [
                pltpu.VMEM((pairs,) + block, bf16),
                pltpu.VMEM((pairs,) + block, bf16),
                pltpu.VMEM((held,) + block, bf16),
                pltpu.VMEM((held,) + block, bf16),
                pltpu.VMEM(block, dtype),
                dma((pairs, chunks)),
                dma((pairs, chunks)),
                dma((pairs, chunks)),
                dma((held, chunks)),
                dma((held, chunks)),
                dma((chunks,)),
            ],
            "scatter_team",
            60 * parts.size // n * 2,
        )[0]


def own_columns(weight, me, groups, count, each):
    shard = weight.shape[0]
    per = weight.shape[1] // (groups * count * each)
    if each % 128:
        cut = weight.reshape(shard, groups, count, per, each)
        cut = lax.dynamic_index_in_dim(cut, me, 3, keepdims=False)
        return [cut[:, g].reshape(shard, count * each) for g in range(groups)]

    def kernel(me_ref, *refs):
        for g in range(groups):
            refs[groups + g][...] = refs[g][...]

    def source(g):
        return pl.BlockSpec((shard, each), lambda i, me_ref: (0, (g * count + i) * per + me_ref[0]))

    return pl.pallas_call(
        kernel,
        grid_spec=pltpu.PrefetchScalarGridSpec(
            num_scalar_prefetch=1,
            grid=(count,),
            in_specs=[source(g) for g in range(groups)],
            out_specs=[pl.BlockSpec((shard, each), lambda i, me_ref: (0, i))] * groups,
        ),
        out_shape=[jax.ShapeDtypeStruct((shard, count * each), weight.dtype)] * groups,
        name="own_columns",
    )(me.reshape(1), *([weight] * groups))


def spread_columns(pieces, count, each, block_rows):
    devices, rows, _ = pieces[0].shape
    groups = len(pieces)
    if each % 128:
        cut = jnp.stack(pieces).reshape(groups, devices, rows, count, each)
        return jnp.transpose(cut, (2, 0, 3, 1, 4)).reshape(rows, -1).astype(f32)
    wide = devices * each

    def kernel(in_ref, *refs):
        for j in range(devices):
            refs[-1][:, j * each : (j + 1) * each] = in_ref[j].astype(f32)

    out = None
    for g, piece in enumerate(pieces):
        out = pl.pallas_call(
            kernel,
            grid=(count, rows // block_rows),
            in_specs=[pl.BlockSpec((devices, block_rows, each), lambda i, r: (0, r, i))]
            + ([] if out is None else [pl.BlockSpec(memory_space=pl.ANY)]),
            out_specs=pl.BlockSpec((block_rows, wide), lambda i, r, g=g: (r, g * count + i)),
            out_shape=jax.ShapeDtypeStruct((rows, groups * count * wide), f32),
            input_output_aliases={} if out is None else {1: 0},
            name="spread_columns",
        )(*([piece] if out is None else [piece, out]))
    return out


def mm(left, right):
    return jnp.dot(left, right, preferred_element_type=f32)


def mm_nt(left, right):
    return lax.dot_general(left, right, (((1,), (1,)), ((), ())), preferred_element_type=f32)


def mm_tn(left, right):
    return lax.dot_general(left, right, (((0,), (0,)), ((), ())), preferred_element_type=f32)


def make_body(n_seq, n_fsdp):
    def body(
        tokens,
        cotangent,
        w_qkv,
        w_out,
        w_gate_up,
        w_down,
        gain_attn,
        gain_ffn,
        gate_bias,
        memory_in,
        norms_in,
        resets,
        depth,
    ):
        _, segs, local, width = tokens.shape
        heads = gate_bias.shape[0]
        hdim = width // heads
        my_heads = heads // n_seq
        my_width = width // n_seq
        seg = local * n_seq
        rows = segs * local
        total_rows = segs * seg
        shard = w_qkv.shape[0]
        hidden_shard = w_down.shape[0]
        my_hidden = hidden_shard // n_seq
        out_rows = shard // n_seq
        team = Team(n_seq)
        me = team.me

        (qkv_own,) = own_columns(w_qkv, me, 1, 3, my_width)
        gate_own, up_own = own_columns(w_gate_up, me, 2, n_fsdp, my_hidden)
        down_own = lax.dynamic_slice(w_down, (me * my_hidden, 0), (my_hidden, width))
        out_own = lax.dynamic_slice(w_out, (me * out_rows, 0), (out_rows, width))

        x_flat = tokens.reshape(rows, width).astype(f32)
        r_one = rms(x_flat)
        h_one_own = (r_one * gain_attn).astype(bf16)
        grad_y = cotangent.reshape(rows, width)

        def gather_rows(block):
            return lax.all_gather(block, "fsdp", axis=0, tiled=True)

        def gather_tokens(value):
            (out,) = team.gather([value.reshape(segs, local, width)], False)
            return out.reshape(total_rows, width)

        def scatter_tokens(value):
            return team.scatter(value.reshape(segs, n_seq, local, width), f32).reshape(rows, width)

        w_o = gather_rows(tie(out_own, h_one_own))
        w_q = gather_rows(tie(qkv_own, h_one_own))
        h_one = gather_tokens(h_one_own)
        w_g = gather_rows(tie(gate_own, h_one))
        (whole_o,) = team.gather([tie(w_o, h_one).reshape(n_fsdp, out_rows, width)], False)
        whole_o = whole_o.reshape(width, width)
        w_u = gather_rows(tie(up_own, whole_o))

        qkv = mm(h_one, w_q).astype(bf16)
        gate = jax.nn.sigmoid(lax.dynamic_slice(gate_bias, (me * my_heads,), (my_heads,)))
        memory = lax.dynamic_slice(memory_in[0], (me * my_heads, 0, 0), (my_heads, hdim, hdim))
        norms = lax.dynamic_slice(norms_in[0], (me * my_heads, 0), (my_heads, hdim))
        attn_heads, lse, mems, nrms = attention_forward(qkv, gate, resets[0], memory, norms, segs)

        w_d = gather_rows(tie(down_own, attn_heads))

        def columns_of(ref, i):
            return ref.at[:, :, pl.ds(pl.multiple_of(i * my_width, my_width), my_width)]

        def tokens_of(ref, i):
            return ref.at[:, i]

        attn = team.exchange(
            attn_heads.reshape(segs, n_seq, local, my_width),
            (segs, local, width),
            tokens_of,
            columns_of,
        ).reshape(rows, width)
        x_one = x_flat + mm(attn, whole_o)
        r_two = rms(x_one)
        h_two = gather_tokens((r_two * gain_ffn).astype(bf16))
        grad_y_all = gather_tokens(tie(grad_y, h_two))
        gate_part = mm(h_two, w_g).astype(bf16)
        up_part = mm(h_two, w_u).astype(bf16)
        hidden = swiglu(gate_part.astype(f32), up_part.astype(f32)).astype(bf16)

        def scatter_rows(parts):
            return lax.psum_scatter(parts, "fsdp", scatter_dimension=0, tiled=True)

        down_parts = mm_tn(hidden, grad_y_all).astype(bf16)
        down_term = scatter_rows(down_parts)
        grad_hidden = mm_nt(tie(grad_y_all, down_parts), w_d)
        _, swiglu_back = jax.vjp(swiglu, gate_part.astype(f32), up_part.astype(f32))
        grad_gate, grad_up = swiglu_back(grad_hidden)
        grad_gate, grad_up = grad_gate.astype(bf16), grad_up.astype(bf16)
        gate_parts = mm_tn(h_two, grad_gate).astype(bf16)
        gate_term = scatter_rows(gate_parts)
        up_parts = mm_tn(h_two, tie(grad_up, gate_parts)).astype(bf16)
        up_term = scatter_rows(up_parts)
        grad_gate, grad_up, _ = lax.optimization_barrier((grad_gate, grad_up, up_parts))
        grad_h_two = scatter_tokens((mm_nt(grad_gate, w_g) + mm_nt(grad_up, w_u)).astype(bf16))

        gain_ffn_term = jnp.sum(grad_h_two * r_two, axis=0)
        _, norm_two_back = jax.vjp(rms, x_one)
        grad_x_one = grad_y.astype(f32) + norm_two_back(grad_h_two * gain_ffn)[0]
        grad_o = grad_x_one.astype(bf16)

        grad_attn_parts = mm_nt(grad_o, whole_o).astype(bf16)
        grad_attn = team.exchange(
            grad_attn_parts.reshape(segs, local, width),
            (segs, n_seq, local, my_width),
            columns_of,
            tokens_of,
        ).reshape(total_rows, my_width)
        grads_q, grads_k, grads_v, bias_terms = attention_backward(
            qkv, grad_attn, gate, resets[0], depth, lse, mems, nrms, segs
        )
        grad_qkv_rows = jnp.concatenate([grads_q, grads_k, grads_v], axis=1)
        qkv_parts = mm_tn(h_one, grad_qkv_rows).astype(bf16)
        qkv_term = scatter_rows(tie(qkv_parts, gate_term))

        out_parts = mm_tn(attn, tie(grad_o, qkv_parts)).astype(bf16)
        out_sum = team.scatter(out_parts.reshape(n_fsdp, n_seq, out_rows, width), bf16)
        out_term = scatter_rows(tie(out_sum, up_term).reshape(-1, width))
        grad_qkv_rows = tie(grad_qkv_rows, qkv_parts)
        grad_h_one = scatter_tokens(mm_nt(grad_qkv_rows, w_q).astype(bf16))
        output = x_one + scatter_tokens(mm(tie(hidden, grad_h_one), w_d).astype(bf16))
        output = output.astype(bf16).reshape(tokens.shape)
        gain_attn_term = jnp.sum(grad_h_one * r_one, axis=0)
        _, norm_one_back = jax.vjp(rms, x_flat)
        grad_x = grad_x_one + norm_one_back(grad_h_one * gain_attn)[0]
        input_grad = grad_x.astype(bf16).reshape(tokens.shape)

        (down_all,) = team.gather([down_term[None]], True)
        (gate_all,) = team.gather([gate_term[None]], True)
        (up_all,) = team.gather([up_term[None]], True)
        qkv_all, out_all = team.gather([qkv_term[None], out_term[None]], True)
        down_all = down_all.reshape(hidden_shard, width).astype(f32)
        out_all = out_all.reshape(shard, width).astype(f32)
        gate_up_all = spread_columns([gate_all[:, 0], up_all[:, 0]], n_fsdp, my_hidden, shard)
        qkv_all = spread_columns([qkv_all[:, 0]], 3, my_width, shard // 2)

        bias_all = lax.dynamic_update_slice(
            jnp.zeros((heads,), f32), bias_terms[:, 0, 0], (me * my_heads,)
        )
        small = jnp.concatenate([gain_attn_term, gain_ffn_term, bias_all])
        for axis, n in (("seq", n_seq), ("fsdp", n_fsdp)):
            k = 1
            while k < n:
                small = small + lax.ppermute(small, axis, [(i, i ^ k) for i in range(n)])
                k *= 2
        return (
            output,
            input_grad,
            qkv_all,
            out_all,
            gate_up_all,
            down_all,
            small[:width],
            small[width : 2 * width],
            small[2 * width :],
        )

    return body


def solution(mesh):
    rows = P("fsdp", None)
    tokens = P("fsdp", None, "seq", None)
    body = make_body(mesh.shape["seq"], mesh.shape["fsdp"])
    return jax.shard_map(
        body,
        mesh=mesh,
        in_specs=(
            tokens,
            tokens,
            rows,
            rows,
            rows,
            rows,
            P(),
            P(),
            P(),
            P("fsdp", None, None, None),
            P("fsdp", None, None),
            rows,
            P("fsdp"),
        ),
        out_specs=(tokens, tokens, rows, rows, rows, rows, P(), P(), P()),
        check_vma=False,
    )
```

```python
import functools

import jax
import jax.numpy as jnp
from jax import lax
from jax.experimental import pallas as pl
from jax.experimental.pallas import tpu as pltpu
from jax.sharding import PartitionSpec as P

norm_eps = 1e-05
bf16 = jnp.bfloat16
f32 = jnp.float32


def rms(value_rows_segment):
    return value_rows_segment * lax.rsqrt(
        jnp.mean(value_rows_segment * value_rows_segment, axis=-1, keepdims=True) + norm_eps
    )


def swiglu(gate_part, up_part):
    return jax.nn.silu(gate_part) * up_part


def feature(value_rows_segment):
    return jnp.where(
        value_rows_segment > 0,
        value_rows_segment + 1.0,
        jnp.exp(jnp.minimum(value_rows_segment, 0.0)),
    )


def contract(left, right, left_dim, right_dim):
    return lax.dot_general(
        left, right, (((left_dim,), (right_dim,)), ((), ())), preferred_element_type=f32
    )


def split(value):
    high = value.astype(bf16)
    return high, (value - high.astype(f32)).astype(bf16)


def fine(left, right, left_dim, right_dim):
    lh, ll = left
    rh, rl = right
    return (
        contract(lh, rl, left_dim, right_dim)
        + contract(ll, rh, left_dim, right_dim)
        + contract(lh, rh, left_dim, right_dim)
    )


LOG2E = 1.4426950408889634


def scores_of(key, query, block, i):
    n = (i + 1) * block
    sc = contract(key[:n], query, 1, 1)
    rows = lax.broadcasted_iota(jnp.int32, (block, block), 0)
    cols = lax.broadcasted_iota(jnp.int32, (block, block), 1)
    last = jnp.where(rows <= cols, sc[n - block :], -1e30)
    if i == 0:
        return last
    return jnp.concatenate([sc[: n - block], last], axis=0)


def forward_kernel(
    block, segs, gate, resets, q_ref, k_ref, v_ref, m_ref, z_ref, a_ref, lse_ref, mem_ref, nrm_ref, mem, nrm
):
    h, s = pl.program_id(0), pl.program_id(1)
    seg, hdim = q_ref.shape
    scale = LOG2E / hdim**0.5

    @pl.when(s == 0)
    def _():
        mem[...] = m_ref[0]
        nrm[...] = z_ref[0]

    @pl.when(s > 0)
    def _():
        @pl.when(resets[jnp.maximum(s - 1, 0)] > 0)
        def _():
            mem[...] = jnp.zeros_like(mem)
            nrm[...] = jnp.ones_like(nrm)

    mem_ref[0, 0] = mem[...]
    nrm_ref[0, 0] = nrm[...]
    g = gate[h]
    mem_parts = split(mem[...])
    key, value = k_ref[...], v_ref[...]
    value_t = value.T
    for i in range(seg // block):
        rows = slice(i * block, (i + 1) * block)
        query = q_ref[rows, :]
        sc = scores_of(key, query, block, i)
        top = jnp.max(sc, axis=0, keepdims=True)
        weights = jnp.exp2((sc - top) * scale)
        total = jnp.sum(weights, axis=0, keepdims=True)
        lse_ref[0, 0, :, rows] = top * scale + jnp.log2(total)
        adot_t = contract(value_t[:, : (i + 1) * block], weights.astype(bf16), 1, 0)
        adot_t = adot_t * ((1.0 - g) / total)
        sq = feature(query.astype(f32))
        amem = fine(split(sq), mem_parts, 1, 0) * (
            g / jnp.sum(sq * nrm[...], axis=1, keepdims=True)
        )
        a_ref[rows, :] = (amem + adot_t.T).astype(bf16)

    @pl.when(s + 1 < segs)
    def _():
        sk = feature(key.astype(f32))
        sk_parts = split(sk)
        recall = fine(sk_parts, mem_parts, 1, 0) / jnp.sum(sk * nrm[...], axis=1, keepdims=True)
        delta = split(value.astype(f32) - recall)
        mem[...] = mem[...] + fine(sk_parts, delta, 0, 0)
        nrm[...] = nrm[...] + jnp.sum(sk, axis=0, keepdims=True)


def specs(seg, hdim, heads, back, segs):
    def at(part):
        return pl.BlockSpec(
            (seg, hdim), lambda h, t: ((segs - 1 - t) if back else t, part * heads + h)
        )

    return at


def attention_forward(qkv, gate, resets, memory, norms, segs):
    total_rows, cols = qkv.shape
    heads, hdim, _ = memory.shape
    seg = total_rows // segs
    at = specs(seg, hdim, heads, False, segs)
    return pl.pallas_call(
        functools.partial(forward_kernel, min(256, seg), segs),
        grid=(heads, segs),
        in_specs=[
            pl.BlockSpec(memory_space=pltpu.SMEM),
            pl.BlockSpec(memory_space=pltpu.SMEM),
            at(0),
            at(1),
            at(2),
            pl.BlockSpec((1, hdim, hdim), lambda h, t: (h, 0, 0)),
            pl.BlockSpec((1, 1, hdim), lambda h, t: (h, 0, 0)),
        ],
        out_specs=[
            at(0),
            pl.BlockSpec((1, 1, 1, seg), lambda h, t: (h, t, 0, 0)),
            pl.BlockSpec((1, 1, hdim, hdim), lambda h, t: (h, t, 0, 0)),
            pl.BlockSpec((1, 1, 1, hdim), lambda h, t: (h, t, 0, 0)),
        ],
        out_shape=[
            jax.ShapeDtypeStruct((total_rows, heads * hdim), bf16),
            jax.ShapeDtypeStruct((heads, segs, 1, seg), f32),
            jax.ShapeDtypeStruct((heads, segs, hdim, hdim), f32),
            jax.ShapeDtypeStruct((heads, segs, 1, hdim), f32),
        ],
        scratch_shapes=[pltpu.VMEM((hdim, hdim), f32), pltpu.VMEM((1, hdim), f32)],
        compiler_params=pltpu.CompilerParams(vmem_limit_bytes=48 << 20),
        cost_estimate=pl.CostEstimate(
            flops=30 * total_rows * seg * heads * hdim // 8,
            bytes_accessed=4 * total_rows * cols,
            transcendentals=total_rows * seg * heads // 2,
        ),
        name="attention_forward",
    )(gate, resets, qkv, qkv, qkv, memory, norms.reshape(heads, 1, hdim))


def backward_kernel(
    block, segs, gate, resets, depth, q_ref, k_ref, v_ref, da_ref, lse_ref, mem_ref, nrm_ref,
    dq_ref, dk_ref, dv_ref, bias_ref, dm, dz, dk_att, dv_att,
):
    h, t = pl.program_id(0), pl.program_id(1)
    s = segs - 1 - t
    seg, hdim = q_ref.shape
    scale = 1.0 / hdim**0.5
    g = gate[h]

    @pl.when(t == 0)
    def _():
        dm[...] = jnp.zeros_like(dm)
        dz[...] = jnp.zeros_like(dz)
        bias_ref[...] = jnp.zeros_like(bias_ref)

    dk_att[...] = jnp.zeros_like(dk_att)
    dv_att[...] = jnp.zeros_like(dv_att)
    mem, nrm = mem_ref[0, 0], nrm_ref[0, 0]
    mem_parts = split(mem)
    key, value = k_ref[...], v_ref[...]
    key_t = key.T
    term = jnp.zeros((1, 1), f32)
    m_next = jnp.zeros((hdim, hdim), f32)
    z_next = jnp.zeros((1, hdim), f32)
    for i in range(seg // block):
        n = (i + 1) * block
        rows = slice(i * block, n)
        query = q_ref[rows, :]
        sc = scores_of(key, query, block, i)
        probs = jnp.exp2(sc * (scale * LOG2E) - lse_ref[0, 0, :, rows])
        grad_mix = da_ref[rows, :].astype(f32)
        grad_adot = ((1.0 - g) * grad_mix).astype(bf16)
        grad_p = contract(value[:n], grad_adot, 1, 1)
        row = jnp.sum(probs * grad_p, axis=0, keepdims=True)
        grad_s = (probs * (grad_p - row)).astype(bf16)
        dk_att[:n, :] += contract(grad_s, query, 1, 0)
        dv_att[:n, :] += contract(probs.astype(bf16), grad_adot, 1, 0)
        dq = contract(key_t[:, :n], grad_s, 1, 0).T * scale

        qf = query.astype(f32)
        sq = feature(qf)
        slope = jnp.where(qf > 0, 1.0, sq)
        sq_parts = split(sq)
        inverse = 1.0 / jnp.sum(sq * nrm, axis=1, keepdims=True)
        amem = fine(sq_parts, mem_parts, 1, 0) * inverse
        mixed = jnp.sum(grad_mix * amem, axis=1, keepdims=True)
        term = term + (g * (1.0 - g)) * jnp.sum(mixed, axis=0, keepdims=True)
        term = term - g * jnp.sum(row, axis=1, keepdims=True)
        d_top = split(grad_mix * (g * inverse))
        d_low = -(g * mixed) * inverse
        d_sq = fine(d_top, mem_parts, 1, 1) + d_low * nrm
        dq_ref[rows, :] = (dq + d_sq * slope).astype(bf16)
        m_next = m_next + fine(sq_parts, d_top, 0, 0)
        z_next = z_next + jnp.sum(sq * d_low, axis=0, keepdims=True)
    bias_ref[...] += jnp.broadcast_to(term[None], bias_ref.shape)
    dk_ref[...] = (dk_att[...] * scale).astype(bf16)
    dv_ref[...] = dv_att[...].astype(bf16)

    @pl.when(s + 1 < segs)
    def _():
        dm_now, dz_now = dm[...], dz[...]
        dm_parts = split(dm_now)
        kf = key.astype(f32)
        sk = feature(kf)
        slope = jnp.where(kf > 0, 1.0, sk)
        sk_parts = split(sk)
        inverse = 1.0 / jnp.sum(sk * nrm, axis=1, keepdims=True)
        recall = fine(sk_parts, mem_parts, 1, 0) * inverse
        delta = value.astype(f32) - recall
        d_delta = fine(sk_parts, dm_parts, 1, 0)
        d_top = split(-d_delta * inverse)
        d_low = jnp.sum(d_delta * recall, axis=1, keepdims=True) * inverse
        d_sk = (
            fine(split(delta), dm_parts, 1, 1)
            + dz_now
            + fine(d_top, mem_parts, 1, 1)
            + d_low * nrm
        )
        dk_ref[...] = (dk_att[...] * scale + d_sk * slope).astype(bf16)
        dv_ref[...] = (dv_att[...] + d_delta).astype(bf16)
        dm[...] = dm_now + fine(sk_parts, d_top, 0, 0)
        dz[...] = dz_now + jnp.sum(sk * d_low, axis=0, keepdims=True)

    @pl.when(s > 0)
    def _():
        cut = (resets[jnp.maximum(s - 1, 0)] > 0) | (lax.rem(s, depth[0]) == 0)
        dm[...] = jnp.where(cut, 0.0, dm[...] + m_next)
        dz[...] = jnp.where(cut, 0.0, dz[...] + z_next)


def attention_backward(qkv, grad_attn, gate, resets, depth, lse, mems, nrms, segs):
    total_rows, cols = qkv.shape
    heads, _, hdim, _ = mems.shape
    seg = total_rows // segs
    at = specs(seg, hdim, heads, True, segs)
    smem = pl.BlockSpec(memory_space=pltpu.SMEM)
    grad = jax.ShapeDtypeStruct((total_rows, heads * hdim), bf16)
    return pl.pallas_call(
        functools.partial(backward_kernel, min(256, seg), segs),
        grid=(heads, segs),
        in_specs=[
            smem,
            smem,
            smem,
            at(0),
            at(1),
            at(2),
            at(0),
            pl.BlockSpec((1, 1, 1, seg), lambda h, t: (h, segs - 1 - t, 0, 0)),
            pl.BlockSpec((1, 1, hdim, hdim), lambda h, t: (h, segs - 1 - t, 0, 0)),
            pl.BlockSpec((1, 1, 1, hdim), lambda h, t: (h, segs - 1 - t, 0, 0)),
        ],
        out_specs=[at(0), at(0), at(0), pl.BlockSpec((1, 8, hdim), lambda h, t: (h, 0, 0))],
        out_shape=[grad, grad, grad, jax.ShapeDtypeStruct((heads, 8, hdim), f32)],
        scratch_shapes=[
            pltpu.VMEM((hdim, hdim), f32),
            pltpu.VMEM((1, hdim), f32),
            pltpu.VMEM((seg, hdim), f32),
            pltpu.VMEM((seg, hdim), f32),
        ],
        compiler_params=pltpu.CompilerParams(vmem_limit_bytes=48 << 20),
        cost_estimate=pl.CostEstimate(
            flops=60 * total_rows * seg * heads * hdim // 8,
            bytes_accessed=4 * total_rows * cols,
            transcendentals=total_rows * seg * heads // 2,
        ),
        name="attention_backward",
    )(gate, resets, depth, qkv, qkv, qkv, grad_attn, lse, mems, nrms)


def tie(value, *others):
    return lax.optimization_barrier((value,) + others)[0]


MESH = pl.DeviceIdType.MESH
dma = pltpu.SemaphoreType.DMA


class Axis:
    def __init__(self, name, rows, cols):
        self.name, self.rows, self.cols = name, rows, cols
        self.size = rows * cols

    def at(self, down, right):
        me = lax.axis_index(self.name)
        row, col = me // self.cols, lax.rem(me, self.cols)
        return lax.rem(row + down, self.rows) * self.cols + lax.rem(col + right, self.cols)

    def to(self, down, right):
        return {"device_id": {self.name: self.at(down, right)}, "device_id_type": MESH}


class Gather:
    def __init__(self, axis, block, outer):
        self.axis, self.outer, self.inputs = axis, outer, [block]
        n, self.chunks = axis.size, block.shape[0]
        lead = (n, self.chunks) if outer else (self.chunks, n)
        self.outputs = [jax.ShapeDtypeStruct(lead + block.shape[1:], block.dtype)]
        held, others = max(axis.rows - 1, 1), axis.cols - 1
        row, col = (held, self.chunks), (others, axis.rows, self.chunks)
        self.scratch = [dma((self.chunks,)), dma(row), dma(row), dma(col), dma(col)]
        self.peers = [(k, 0) for k in range(1, axis.rows)] + [(0, j) for j in range(1, axis.cols)]
        self.bytes = block.size * 2

    def bind(self, ins, outs, scratch):
        (self.src,), (self.dst,) = ins, outs
        self.keep, self.row_out, self.row_in, self.col_out, self.col_in = scratch

    def place(self, dev, c):
        return self.dst.at[dev, c] if self.outer else self.dst.at[c, dev]

    def along(self, k, c):
        axis = self.axis
        return pltpu.make_async_remote_copy(
            src_ref=self.src.at[c],
            dst_ref=self.place(axis.at(0, 0), c),
            send_sem=self.row_out.at[k - 1, c],
            recv_sem=self.row_in.at[k - 1, c],
            **axis.to(k, 0),
        )

    def across(self, k, j, c):
        axis = self.axis
        spot = self.place(axis.at((axis.rows - k) % axis.rows, 0), c)
        return pltpu.make_async_remote_copy(
            src_ref=self.src.at[c] if k == 0 else spot,
            dst_ref=spot,
            send_sem=self.col_out.at[j - 1, k, c],
            recv_sem=self.col_in.at[j - 1, k, c],
            **axis.to(0, j),
        )

    def own(self, c):
        return pltpu.make_async_copy(
            self.src.at[c], self.place(self.axis.at(0, 0), c), self.keep.at[c]
        )

    def start(self):
        for c in range(self.chunks):
            for k in range(1, self.axis.rows):
                self.along(k, c).start()
        for c in range(self.chunks):
            for j in range(1, self.axis.cols):
                self.across(0, j, c).start()
            self.own(c).start()

    def middle(self, part, parts):
        for c in range(self.chunks * part // parts, self.chunks * (part + 1) // parts):
            for k in range(1, self.axis.rows):
                self.along(k, c).wait_recv()
                for j in range(1, self.axis.cols):
                    self.across(k, j, c).start()

    def finish(self):
        for c in range(self.chunks):
            for k in range(1, self.axis.rows):
                self.along(k, c).wait_send()
            for k in range(self.axis.rows):
                for j in range(1, self.axis.cols):
                    self.across(k, j, c).wait()
            self.own(c).wait()


class Exchange:
    def __init__(self, axis, array, shape, source, target):
        self.axis, self.inputs = axis, [array]
        self.outputs = [jax.ShapeDtypeStruct(shape, array.dtype)]
        self.source, self.target = source, target
        n = axis.size
        self.scratch = [dma, dma((n - 1,)), dma((n - 1,))]
        self.peers = [(k, j) for k in range(axis.rows) for j in range(axis.cols)][1:]
        self.bytes = array.size

    def bind(self, ins, outs, scratch):
        (self.src,), (self.dst,) = ins, outs
        self.keep, self.out_sem, self.in_sem = scratch

    def copy(self, i):
        axis, (k, j) = self.axis, self.peers[i]
        return pltpu.make_async_remote_copy(
            src_ref=self.source(self.src, axis.at(k, j)),
            dst_ref=self.target(self.dst, axis.at(0, 0)),
            send_sem=self.out_sem.at[i],
            recv_sem=self.in_sem.at[i],
            **axis.to(k, j),
        )

    def own(self):
        me = self.axis.at(0, 0)
        return pltpu.make_async_copy(self.source(self.src, me), self.target(self.dst, me), self.keep)

    def start(self):
        self.own().start()
        for i in reversed(range(len(self.peers))):
            self.copy(i).start()

    def middle(self, part, parts):
        pass

    def finish(self):
        for i in reversed(range(len(self.peers))):
            self.copy(i).wait()
        self.own().wait()


class Scatter:
    def __init__(self, axis, parts, outer, dtype):
        self.axis, self.outer, self.dtype, self.inputs = axis, outer, dtype, [parts]
        self.chunks = parts.shape[1 if outer else 0]
        block = (self.chunks,) + parts.shape[2:]
        self.outputs = [jax.ShapeDtypeStruct(block, dtype)]
        rows, others, held = axis.rows, axis.cols - 1, max(axis.rows - 1, 1)
        row, col = (held, self.chunks), (others, rows, self.chunks)
        self.scratch = [
            pltpu.VMEM((rows,) + block, bf16),
            pltpu.VMEM((others, rows) + block, bf16),
            pltpu.VMEM((held,) + block, bf16),
            pltpu.VMEM((held,) + block, bf16),
            pltpu.VMEM(block, dtype),
            dma((rows, self.chunks)),
            dma(col),
            dma(col),
            dma(row),
            dma(row),
            dma((self.chunks,)),
        ]
        self.peers = [(k, 0) for k in range(1, rows)] + [(0, j) for j in range(1, axis.cols)]
        self.order = [(k, c) for k in list(range(1, rows)) + [0] for c in range(self.chunks)]
        self.bytes = parts.size // axis.size * 2

    def bind(self, ins, outs, scratch):
        (self.src,), (self.dst,) = ins, outs
        self.mine, self.met, self.sent, self.come, self.result = scratch[:5]
        self.load, self.col_out, self.col_in, self.row_out, self.row_in, self.store = scratch[5:]

    def terms(self, dev, c):
        return self.src.at[dev, c] if self.outer else self.src.at[c, dev]

    def read(self, k, c):
        return pltpu.make_async_copy(
            self.terms(self.axis.at(k, 0), c), self.mine.at[k, c], self.load.at[k, c]
        )

    def across(self, k, j, c):
        return pltpu.make_async_remote_copy(
            src_ref=self.terms(self.axis.at(k, j), c),
            dst_ref=self.met.at[j - 1, k, c],
            send_sem=self.col_out.at[j - 1, k, c],
            recv_sem=self.col_in.at[j - 1, k, c],
            **self.axis.to(0, j),
        )

    def along(self, k, c):
        return pltpu.make_async_remote_copy(
            src_ref=self.sent.at[k - 1, c],
            dst_ref=self.come.at[k - 1, c],
            send_sem=self.row_out.at[k - 1, c],
            recv_sem=self.row_in.at[k - 1, c],
            **self.axis.to(k, 0),
        )

    def write(self, c):
        return pltpu.make_async_copy(self.result.at[c], self.dst.at[c], self.store.at[c])

    def meet(self, k, c):
        self.read(k, c).wait()
        total = self.mine[k, c].astype(f32)
        for j in range(1, self.axis.cols):
            self.across(k, j, c).wait_recv()
            total = total + self.met[j - 1, k, c].astype(f32)
        return total

    def start(self):
        for k, c in self.order:
            for j in range(1, self.axis.cols):
                self.across(k, j, c).start()
            self.read(k, c).start()

    def middle(self, part, parts):
        steps = [step for step in self.order if step[0]]
        for k, c in steps[len(steps) * part // parts : len(steps) * (part + 1) // parts]:
            self.sent[k - 1, c] = self.meet(k, c).astype(bf16)
            self.along(k, c).start()

    def finish(self):
        for c in range(self.chunks):
            total = self.meet(0, c)
            for k in range(1, self.axis.rows):
                self.along(k, c).wait_recv()
                total = total + self.come[k - 1, c].astype(f32)
            self.result[c] = total.astype(self.dtype)
            self.write(c).start()
        for k, c in self.order:
            for j in range(1, self.axis.cols):
                self.across(k, j, c).wait_send()
            if k:
                self.along(k, c).wait_send()
        for c in range(self.chunks):
            self.write(c).wait()


class Product:
    def __init__(self, left, right, over, tiles):
        self.inputs, self.over = [left, right], over
        self.depth, m, n = left.shape[over[0]], left.shape[1 - over[0]], right.shape[1 - over[1]]
        self.outputs = [jax.ShapeDtypeStruct((m, n), bf16)]
        self.tm, self.tn = min(tiles[0], m), min(tiles[1], n)
        self.grid = (m // self.tm, n // self.tn)
        self.scratch, self.peers, self.bytes = [], [], 0

    def bind(self, ins, outs, scratch):
        self.refs = (*ins, *outs)

    def start(self):
        pass

    def middle(self, part, parts):
        pass

    def finish(self):
        pass

    def compute(self):
        def body(left, right, out):
            out[...] = contract(left[...], right[...], *self.over).astype(bf16)

        def tile(size, over, index):
            if over == 0:
                return pl.BlockSpec((self.depth, size), lambda i, j: (0, (i, j)[index]))
            return pl.BlockSpec((size, self.depth), lambda i, j: ((i, j)[index], 0))

        pltpu.emit_pipeline(
            body,
            grid=self.grid,
            in_specs=[tile(self.tm, self.over[0], 0), tile(self.tn, self.over[1], 1)],
            out_specs=[pl.BlockSpec((self.tm, self.tn), lambda i, j: (i, j))],
        )(*self.refs)


class Net:
    def __init__(self, n_seq, n_fsdp):
        rows = 4 if n_fsdp % 4 == 0 else 1
        self.seq = Axis("seq", n_seq // 2, 2)
        self.fsdp = Axis("fsdp", rows, n_fsdp // rows)
        self.calls = 0

    def run(self, jobs, room=32):
        self.calls += 1
        ins = [array for job in jobs for array in job.inputs]
        outs = [shape for job in jobs for shape in job.outputs]
        scratch = [one for job in jobs for one in job.scratch]
        peers = []
        for job in jobs:
            for peer in job.peers:
                if (job.axis, peer) not in peers:
                    peers.append((job.axis, peer))

        def kernel(*refs):
            at = [0, len(ins), len(ins) + len(outs)]
            for job in jobs:
                taken = []
                for part, count in enumerate(
                    (len(job.inputs), len(job.outputs), len(job.scratch))
                ):
                    taken.append(refs[at[part] : at[part] + count])
                    at[part] += count
                job.bind(*taken)
            barrier = pltpu.get_barrier_semaphore()
            for axis, peer in peers:
                pl.semaphore_signal(barrier, inc=1, **axis.to(*peer))
            pl.semaphore_wait(barrier, len(peers))
            for job in jobs:
                job.start()
            parts = 4
            for part in range(parts):
                for job in jobs:
                    job.middle(part, parts)
            for job in jobs:
                if isinstance(job, Product):
                    job.compute()
            for job in jobs:
                job.finish()

        anywhere = pl.BlockSpec(memory_space=pl.ANY)
        return pl.pallas_call(
            kernel,
            in_specs=[anywhere] * len(ins),
            out_specs=[anywhere] * len(outs),
            out_shape=outs,
            scratch_shapes=scratch,
            compiler_params=pltpu.CompilerParams(
                collective_id=self.calls, has_side_effects=True, vmem_limit_bytes=room << 20
            ),
            cost_estimate=pl.CostEstimate(
                flops=0, bytes_accessed=60 * max(job.bytes for job in jobs), transcendentals=0
            ),
            name="net",
        )(*ins)


def own_columns(weight, me, groups, count, each):
    shard = weight.shape[0]
    per = weight.shape[1] // (groups * count * each)
    if each % 128:
        cut = weight.reshape(shard, groups, count, per, each)
        cut = lax.dynamic_index_in_dim(cut, me, 3, keepdims=False)
        return [cut[:, g].reshape(shard, count * each) for g in range(groups)]

    def kernel(me_ref, *refs):
        for g in range(groups):
            refs[groups + g][...] = refs[g][...]

    def source(g):
        return pl.BlockSpec((shard, each), lambda i, me_ref: (0, (g * count + i) * per + me_ref[0]))

    return pl.pallas_call(
        kernel,
        grid_spec=pltpu.PrefetchScalarGridSpec(
            num_scalar_prefetch=1,
            grid=(count,),
            in_specs=[source(g) for g in range(groups)],
            out_specs=[pl.BlockSpec((shard, each), lambda i, me_ref: (0, i))] * groups,
        ),
        out_shape=[jax.ShapeDtypeStruct((shard, count * each), weight.dtype)] * groups,
        name="own_columns",
    )(me.reshape(1), *([weight] * groups))


def spread_columns(pieces, count, each, block_rows):
    devices, rows, _ = pieces[0].shape
    groups = len(pieces)
    if each % 128:
        cut = jnp.stack(pieces).reshape(groups, devices, rows, count, each)
        return jnp.transpose(cut, (2, 0, 3, 1, 4)).reshape(rows, -1).astype(f32)
    wide = devices * each

    def kernel(in_ref, *refs):
        for j in range(devices):
            refs[-1][:, j * each : (j + 1) * each] = in_ref[j].astype(f32)

    out = None
    for g, piece in enumerate(pieces):
        out = pl.pallas_call(
            kernel,
            grid=(count, rows // block_rows),
            in_specs=[pl.BlockSpec((devices, block_rows, each), lambda i, r: (0, r, i))]
            + ([] if out is None else [pl.BlockSpec(memory_space=pl.ANY)]),
            out_specs=pl.BlockSpec((block_rows, wide), lambda i, r, g=g: (r, g * count + i)),
            out_shape=jax.ShapeDtypeStruct((rows, groups * count * wide), f32),
            input_output_aliases={} if out is None else {1: 0},
            name="spread_columns",
        )(*([piece] if out is None else [piece, out]))
    return out


def mm(left, right):
    return jnp.dot(left, right, preferred_element_type=f32)


def mm_nt(left, right):
    return lax.dot_general(left, right, (((1,), (1,)), ((), ())), preferred_element_type=f32)


def mm_tn(left, right):
    return lax.dot_general(left, right, (((0,), (0,)), ((), ())), preferred_element_type=f32)


def make_body(n_seq, n_fsdp):
    def body(
        tokens,
        cotangent,
        w_qkv,
        w_out,
        w_gate_up,
        w_down,
        gain_attn,
        gain_ffn,
        gate_bias,
        memory_in,
        norms_in,
        resets,
        depth,
    ):
        _, segs, local, width = tokens.shape
        heads = gate_bias.shape[0]
        hdim = width // heads
        my_heads = heads // n_seq
        my_width = width // n_seq
        seg = local * n_seq
        rows = segs * local
        total_rows = segs * seg
        shard = w_qkv.shape[0]
        hidden_shard = w_down.shape[0]
        my_hidden = hidden_shard // n_seq
        out_rows = shard // n_seq
        net = Net(n_seq, n_fsdp)
        me = lax.axis_index("seq")

        (qkv_own,) = own_columns(w_qkv, me, 1, 3, my_width)
        gate_own, up_own = own_columns(w_gate_up, me, 2, n_fsdp, my_hidden)
        down_own = lax.dynamic_slice(w_down, (me * my_hidden, 0), (my_hidden, width))
        out_own = lax.dynamic_slice(w_out, (me * out_rows, 0), (out_rows, width))

        x_flat = tokens.reshape(rows, width).astype(f32)
        r_one = rms(x_flat)
        h_one_own = (r_one * gain_attn).astype(bf16)
        grad_y = cotangent.reshape(rows, width)

        def gather_rows(block):
            return lax.all_gather(block, "fsdp", axis=0, tiled=True)

        def token_parts(value):
            return value.reshape(segs, n_seq, local, width)

        def gather_own(value):
            return Gather(net.seq, value.reshape(segs, local, width), False)

        w_g = gather_rows(gate_own)
        h_one, grad_y_all, w_o, w_q = net.run(
            [
                gather_own(h_one_own),
                gather_own(grad_y),
                Gather(net.fsdp, out_own.reshape(1, out_rows, width), True),
                Gather(net.fsdp, qkv_own.reshape(4, shard // 4, 3 * my_width), True),
            ]
        )
        h_one = h_one.reshape(total_rows, width)
        grad_y_all = grad_y_all.reshape(total_rows, width)
        w_q = w_q.reshape(width, 3 * my_width)
        w_u = gather_rows(tie(up_own, w_q))

        qkv = mm(h_one, w_q).astype(bf16)
        gate = jax.nn.sigmoid(lax.dynamic_slice(gate_bias, (me * my_heads,), (my_heads,)))
        memory = lax.dynamic_slice(memory_in[0], (me * my_heads, 0, 0), (my_heads, hdim, hdim))
        norms = lax.dynamic_slice(norms_in[0], (me * my_heads, 0), (my_heads, hdim))
        attn_heads, lse, mems, nrms = attention_forward(qkv, gate, resets[0], memory, norms, segs)

        half = width // 2
        w_d_left = gather_rows(tie(down_own[:, :half], attn_heads))

        def columns_of(ref, i):
            return ref.at[:, :, pl.ds(pl.multiple_of(i * my_width, my_width), my_width)]

        def tokens_of(ref, i):
            return ref.at[:, i]

        attn, whole_o, w_d_right = net.run(
            [
                Exchange(
                    net.seq,
                    attn_heads.reshape(segs, n_seq, local, my_width),
                    (segs, local, width),
                    tokens_of,
                    columns_of,
                ),
                Gather(net.seq, w_o.reshape(n_fsdp, out_rows, width), False),
                Gather(net.fsdp, down_own[:, half:].reshape(4, my_hidden // 4, half), True),
            ]
        )
        attn = attn.reshape(rows, width)
        whole_o = whole_o.reshape(width, width)
        x_one = x_flat + mm(attn, whole_o)
        r_two = rms(x_one)
        h_two_own = (r_two * gain_ffn).astype(bf16)
        (h_two,) = net.run([gather_own(h_two_own)])
        h_two = h_two.reshape(total_rows, width)
        gate_part = mm(h_two, w_g).astype(bf16)
        up_part = mm(h_two, w_u).astype(bf16)
        hidden = swiglu(gate_part.astype(f32), up_part.astype(f32)).astype(bf16)

        w_d = jnp.concatenate([w_d_left, w_d_right.reshape(-1, half)], axis=1)

        def scatter_rows(parts):
            return lax.psum_scatter(parts, "fsdp", scatter_dimension=0, tiled=True)

        down_parts = mm_tn(hidden, grad_y_all).astype(bf16)
        down_term = scatter_rows(down_parts)
        grad_hidden = mm_nt(tie(grad_y_all, down_parts), w_d)
        _, swiglu_back = jax.vjp(swiglu, gate_part.astype(f32), up_part.astype(f32))
        grad_gate, grad_up = swiglu_back(grad_hidden)
        grad_gate, grad_up = grad_gate.astype(bf16), grad_up.astype(bf16)
        gate_parts = mm_tn(h_two, grad_gate).astype(bf16)
        gate_term = scatter_rows(gate_parts)
        grad_gate, grad_up, _ = lax.optimization_barrier((grad_gate, grad_up, gate_parts))
        grad_h_two = (mm_nt(grad_gate, w_g) + mm_nt(grad_up, w_u)).astype(bf16)
        grad_h_two, up_parts = net.run(
            [
                Scatter(net.seq, token_parts(grad_h_two), False, f32),
                Product(h_two, grad_up, (0, 0), (1024, 512)),
            ],
            56,
        )
        up_term = scatter_rows(up_parts)
        grad_h_two = grad_h_two.reshape(rows, width)

        gain_ffn_term = jnp.sum(grad_h_two * r_two, axis=0)
        _, norm_two_back = jax.vjp(rms, x_one)
        grad_x_one = grad_y.astype(f32) + norm_two_back(grad_h_two * gain_ffn)[0]
        grad_o = grad_x_one.astype(bf16)

        grad_attn_parts = mm_nt(grad_o, whole_o).astype(bf16)
        grad_attn, output = net.run(
            [
                Exchange(
                    net.seq,
                    grad_attn_parts.reshape(segs, local, width),
                    (segs, n_seq, local, my_width),
                    columns_of,
                    tokens_of,
                ),
                Product(hidden, w_d, (1, 0), (1024, 512)),
            ],
            56,
        )
        grad_attn = grad_attn.reshape(total_rows, my_width)
        grads_q, grads_k, grads_v, bias_terms = attention_backward(
            qkv, grad_attn, gate, resets[0], depth, lse, mems, nrms, segs
        )
        grad_qkv_rows = jnp.concatenate([grads_q, grads_k, grads_v], axis=1)
        out_parts = mm_tn(attn, tie(grad_o, grads_q)).astype(bf16)
        out_sum, qkv_parts, grad_h_one = net.run(
            [
                Scatter(net.seq, out_parts.reshape(n_fsdp, n_seq, out_rows, width), False, bf16),
                Product(h_one, grad_qkv_rows, (0, 0), (1024, 512)),
                Product(grad_qkv_rows, w_q, (1, 1), (1024, 512)),
            ],
            56,
        )
        grad_h_one, output, qkv_term, out_term, down_all = net.run(
            [
                Scatter(net.seq, token_parts(grad_h_one), False, f32),
                Scatter(net.seq, token_parts(output), False, f32),
                Scatter(
                    net.fsdp, qkv_parts.reshape(n_fsdp, 4, shard // 4, 3 * my_width), True, bf16
                ),
                Scatter(net.fsdp, out_sum[:, None], True, bf16),
                Gather(net.seq, down_term[None], True),
            ],
            56,
        )
        grad_h_one = grad_h_one.reshape(rows, width)
        output = (x_one + output.reshape(rows, width)).astype(bf16).reshape(tokens.shape)
        qkv_term = qkv_term.reshape(shard, 3 * my_width)
        out_term = out_term.reshape(out_rows, width)
        gain_attn_term = jnp.sum(grad_h_one * r_one, axis=0)
        _, norm_one_back = jax.vjp(rms, x_flat)
        grad_x = grad_x_one + norm_one_back(grad_h_one * gain_attn)[0]
        input_grad = grad_x.astype(bf16).reshape(tokens.shape)

        qkv_all, out_all, gate_all = net.run(
            [Gather(net.seq, term[None], True) for term in (qkv_term, out_term, gate_term)]
        )
        (up_all,) = net.run([Gather(net.seq, up_term[None], True)])
        down_all = down_all.reshape(hidden_shard, width).astype(f32)
        out_all = out_all.reshape(shard, width).astype(f32)
        gate_up_all = spread_columns([gate_all[:, 0], up_all[:, 0]], n_fsdp, my_hidden, shard)
        qkv_all = spread_columns([qkv_all[:, 0]], 3, my_width, shard // 2)

        bias_all = lax.dynamic_update_slice(
            jnp.zeros((heads,), f32), bias_terms[:, 0, 0], (me * my_heads,)
        )
        small = jnp.concatenate([gain_attn_term, gain_ffn_term, bias_all])
        for axis, n in (("seq", n_seq), ("fsdp", n_fsdp)):
            k = 1
            while k < n:
                small = small + lax.ppermute(small, axis, [(i, i ^ k) for i in range(n)])
                k *= 2
        return (
            output,
            input_grad,
            qkv_all,
            out_all,
            gate_up_all,
            down_all,
            small[:width],
            small[width : 2 * width],
            small[2 * width :],
        )

    return body


def solution(mesh):
    rows = P("fsdp", None)
    tokens = P("fsdp", None, "seq", None)
    body = make_body(mesh.shape["seq"], mesh.shape["fsdp"])
    return jax.shard_map(
        body,
        mesh=mesh,
        in_specs=(
            tokens,
            tokens,
            rows,
            rows,
            rows,
            rows,
            P(),
            P(),
            P(),
            P("fsdp", None, None, None),
            P("fsdp", None, None),
            rows,
            P("fsdp"),
        ),
        out_specs=(tokens, tokens, rows, rows, rows, rows, P(), P(), P()),
        check_vma=False,
    )
```

```python
import functools

import jax
import jax.numpy as jnp
from jax import lax
from jax.experimental import pallas as pl
from jax.experimental.pallas import tpu as pltpu
from jax.sharding import PartitionSpec as P

norm_eps = 1e-05
bf16 = jnp.bfloat16
f32 = jnp.float32


def rms(value_rows_segment):
    return value_rows_segment * lax.rsqrt(
        jnp.mean(value_rows_segment * value_rows_segment, axis=-1, keepdims=True) + norm_eps
    )


def swiglu(gate_part, up_part):
    return jax.nn.silu(gate_part) * up_part


def feature(value_rows_segment):
    return jnp.where(
        value_rows_segment > 0,
        value_rows_segment + 1.0,
        jnp.exp(jnp.minimum(value_rows_segment, 0.0)),
    )


def contract(left, right, left_dim, right_dim):
    return lax.dot_general(
        left, right, (((left_dim,), (right_dim,)), ((), ())), preferred_element_type=f32
    )


def split(value):
    high = value.astype(bf16)
    return high, (value - high.astype(f32)).astype(bf16)


def fine(left, right, left_dim, right_dim):
    lh, ll = left
    rh, rl = right
    return (
        contract(lh, rl, left_dim, right_dim)
        + contract(ll, rh, left_dim, right_dim)
        + contract(lh, rh, left_dim, right_dim)
    )


LOG2E = 1.4426950408889634


def scores_of(key, query, block, i):
    n = (i + 1) * block
    sc = contract(key[:n], query, 1, 1)
    rows = lax.broadcasted_iota(jnp.int32, (block, block), 0)
    cols = lax.broadcasted_iota(jnp.int32, (block, block), 1)
    last = jnp.where(rows <= cols, sc[n - block :], -1e30)
    if i == 0:
        return last
    return jnp.concatenate([sc[: n - block], last], axis=0)


def forward_kernel(
    block, segs, gate, resets, q_ref, k_ref, v_ref, m_ref, z_ref, a_ref, lse_ref, mem_ref, nrm_ref, mem, nrm
):
    h, s = pl.program_id(0), pl.program_id(1)
    seg, hdim = q_ref.shape
    scale = LOG2E / hdim**0.5

    @pl.when(s == 0)
    def _():
        mem[...] = m_ref[0]
        nrm[...] = z_ref[0]

    @pl.when(s > 0)
    def _():
        @pl.when(resets[jnp.maximum(s - 1, 0)] > 0)
        def _():
            mem[...] = jnp.zeros_like(mem)
            nrm[...] = jnp.ones_like(nrm)

    mem_ref[0, 0] = mem[...]
    nrm_ref[0, 0] = nrm[...]
    g = gate[h]
    mem_parts = split(mem[...])
    key, value = k_ref[...], v_ref[...]
    value_t = value.T
    for i in range(seg // block):
        rows = slice(i * block, (i + 1) * block)
        query = q_ref[rows, :]
        sc = scores_of(key, query, block, i)
        top = jnp.max(sc, axis=0, keepdims=True)
        weights = jnp.exp2((sc - top) * scale)
        total = jnp.sum(weights, axis=0, keepdims=True)
        lse_ref[0, 0, :, rows] = top * scale + jnp.log2(total)
        adot_t = contract(value_t[:, : (i + 1) * block], weights.astype(bf16), 1, 0)
        adot_t = adot_t * ((1.0 - g) / total)
        sq = feature(query.astype(f32))
        amem = fine(split(sq), mem_parts, 1, 0) * (
            g / jnp.sum(sq * nrm[...], axis=1, keepdims=True)
        )
        a_ref[rows, :] = (amem + adot_t.T).astype(bf16)

    @pl.when(s + 1 < segs)
    def _():
        sk = feature(key.astype(f32))
        sk_parts = split(sk)
        recall = fine(sk_parts, mem_parts, 1, 0) / jnp.sum(sk * nrm[...], axis=1, keepdims=True)
        delta = split(value.astype(f32) - recall)
        mem[...] = mem[...] + fine(sk_parts, delta, 0, 0)
        nrm[...] = nrm[...] + jnp.sum(sk, axis=0, keepdims=True)


def specs(seg, hdim, heads, back, segs):
    def at(part):
        return pl.BlockSpec(
            (seg, hdim), lambda h, t: ((segs - 1 - t) if back else t, part * heads + h)
        )

    return at


def attention_forward(qkv, gate, resets, memory, norms, segs):
    total_rows, cols = qkv.shape
    heads, hdim, _ = memory.shape
    seg = total_rows // segs
    at = specs(seg, hdim, heads, False, segs)
    return pl.pallas_call(
        functools.partial(forward_kernel, min(256, seg), segs),
        grid=(heads, segs),
        in_specs=[
            pl.BlockSpec(memory_space=pltpu.SMEM),
            pl.BlockSpec(memory_space=pltpu.SMEM),
            at(0),
            at(1),
            at(2),
            pl.BlockSpec((1, hdim, hdim), lambda h, t: (h, 0, 0)),
            pl.BlockSpec((1, 1, hdim), lambda h, t: (h, 0, 0)),
        ],
        out_specs=[
            at(0),
            pl.BlockSpec((1, 1, 1, seg), lambda h, t: (h, t, 0, 0)),
            pl.BlockSpec((1, 1, hdim, hdim), lambda h, t: (h, t, 0, 0)),
            pl.BlockSpec((1, 1, 1, hdim), lambda h, t: (h, t, 0, 0)),
        ],
        out_shape=[
            jax.ShapeDtypeStruct((total_rows, heads * hdim), bf16),
            jax.ShapeDtypeStruct((heads, segs, 1, seg), f32),
            jax.ShapeDtypeStruct((heads, segs, hdim, hdim), f32),
            jax.ShapeDtypeStruct((heads, segs, 1, hdim), f32),
        ],
        scratch_shapes=[pltpu.VMEM((hdim, hdim), f32), pltpu.VMEM((1, hdim), f32)],
        compiler_params=pltpu.CompilerParams(vmem_limit_bytes=48 << 20),
        cost_estimate=pl.CostEstimate(
            flops=30 * total_rows * seg * heads * hdim // 8,
            bytes_accessed=4 * total_rows * cols,
            transcendentals=total_rows * seg * heads // 2,
        ),
        name="attention_forward",
    )(gate, resets, qkv, qkv, qkv, memory, norms.reshape(heads, 1, hdim))


def backward_kernel(
    block, segs, gate, resets, depth, q_ref, k_ref, v_ref, da_ref, lse_ref, mem_ref, nrm_ref,
    dq_ref, dk_ref, dv_ref, bias_ref, dm, dz, dk_att, dv_att,
):
    h, t = pl.program_id(0), pl.program_id(1)
    s = segs - 1 - t
    seg, hdim = q_ref.shape
    scale = 1.0 / hdim**0.5
    g = gate[h]

    @pl.when(t == 0)
    def _():
        dm[...] = jnp.zeros_like(dm)
        dz[...] = jnp.zeros_like(dz)
        bias_ref[...] = jnp.zeros_like(bias_ref)

    dk_att[...] = jnp.zeros_like(dk_att)
    dv_att[...] = jnp.zeros_like(dv_att)
    mem, nrm = mem_ref[0, 0], nrm_ref[0, 0]
    mem_parts = split(mem)
    key, value = k_ref[...], v_ref[...]
    key_t = key.T
    term = jnp.zeros((1, 1), f32)
    m_next = jnp.zeros((hdim, hdim), f32)
    z_next = jnp.zeros((1, hdim), f32)
    for i in range(seg // block):
        n = (i + 1) * block
        rows = slice(i * block, n)
        query = q_ref[rows, :]
        sc = scores_of(key, query, block, i)
        probs = jnp.exp2(sc * (scale * LOG2E) - lse_ref[0, 0, :, rows])
        grad_mix = da_ref[rows, :].astype(f32)
        grad_adot = ((1.0 - g) * grad_mix).astype(bf16)
        grad_p = contract(value[:n], grad_adot, 1, 1)
        row = jnp.sum(probs * grad_p, axis=0, keepdims=True)
        grad_s = (probs * (grad_p - row)).astype(bf16)
        dk_att[:n, :] += contract(grad_s, query, 1, 0)
        dv_att[:n, :] += contract(probs.astype(bf16), grad_adot, 1, 0)
        dq = contract(key_t[:, :n], grad_s, 1, 0).T * scale

        qf = query.astype(f32)
        sq = feature(qf)
        slope = jnp.where(qf > 0, 1.0, sq)
        sq_parts = split(sq)
        inverse = 1.0 / jnp.sum(sq * nrm, axis=1, keepdims=True)
        amem = fine(sq_parts, mem_parts, 1, 0) * inverse
        mixed = jnp.sum(grad_mix * amem, axis=1, keepdims=True)
        term = term + (g * (1.0 - g)) * jnp.sum(mixed, axis=0, keepdims=True)
        term = term - g * jnp.sum(row, axis=1, keepdims=True)
        d_top = split(grad_mix * (g * inverse))
        d_low = -(g * mixed) * inverse
        d_sq = fine(d_top, mem_parts, 1, 1) + d_low * nrm
        dq_ref[rows, :] = (dq + d_sq * slope).astype(bf16)
        m_next = m_next + fine(sq_parts, d_top, 0, 0)
        z_next = z_next + jnp.sum(sq * d_low, axis=0, keepdims=True)
    bias_ref[...] += jnp.broadcast_to(term[None], bias_ref.shape)
    dk_ref[...] = (dk_att[...] * scale).astype(bf16)
    dv_ref[...] = dv_att[...].astype(bf16)

    @pl.when(s + 1 < segs)
    def _():
        dm_now, dz_now = dm[...], dz[...]
        dm_parts = split(dm_now)
        kf = key.astype(f32)
        sk = feature(kf)
        slope = jnp.where(kf > 0, 1.0, sk)
        sk_parts = split(sk)
        inverse = 1.0 / jnp.sum(sk * nrm, axis=1, keepdims=True)
        recall = fine(sk_parts, mem_parts, 1, 0) * inverse
        delta = value.astype(f32) - recall
        d_delta = fine(sk_parts, dm_parts, 1, 0)
        d_top = split(-d_delta * inverse)
        d_low = jnp.sum(d_delta * recall, axis=1, keepdims=True) * inverse
        d_sk = (
            fine(split(delta), dm_parts, 1, 1)
            + dz_now
            + fine(d_top, mem_parts, 1, 1)
            + d_low * nrm
        )
        dk_ref[...] = (dk_att[...] * scale + d_sk * slope).astype(bf16)
        dv_ref[...] = (dv_att[...] + d_delta).astype(bf16)
        dm[...] = dm_now + fine(sk_parts, d_top, 0, 0)
        dz[...] = dz_now + jnp.sum(sk * d_low, axis=0, keepdims=True)

    @pl.when(s > 0)
    def _():
        cut = (resets[jnp.maximum(s - 1, 0)] > 0) | (lax.rem(s, depth[0]) == 0)
        dm[...] = jnp.where(cut, 0.0, dm[...] + m_next)
        dz[...] = jnp.where(cut, 0.0, dz[...] + z_next)


def attention_backward(qkv, grad_attn, gate, resets, depth, lse, mems, nrms, segs):
    total_rows, cols = qkv.shape
    heads, _, hdim, _ = mems.shape
    seg = total_rows // segs
    at = specs(seg, hdim, heads, True, segs)
    smem = pl.BlockSpec(memory_space=pltpu.SMEM)
    grad = jax.ShapeDtypeStruct((total_rows, heads * hdim), bf16)
    return pl.pallas_call(
        functools.partial(backward_kernel, min(256, seg), segs),
        grid=(heads, segs),
        in_specs=[
            smem,
            smem,
            smem,
            at(0),
            at(1),
            at(2),
            at(0),
            pl.BlockSpec((1, 1, 1, seg), lambda h, t: (h, segs - 1 - t, 0, 0)),
            pl.BlockSpec((1, 1, hdim, hdim), lambda h, t: (h, segs - 1 - t, 0, 0)),
            pl.BlockSpec((1, 1, 1, hdim), lambda h, t: (h, segs - 1 - t, 0, 0)),
        ],
        out_specs=[at(0), at(0), at(0), pl.BlockSpec((1, 8, hdim), lambda h, t: (h, 0, 0))],
        out_shape=[grad, grad, grad, jax.ShapeDtypeStruct((heads, 8, hdim), f32)],
        scratch_shapes=[
            pltpu.VMEM((hdim, hdim), f32),
            pltpu.VMEM((1, hdim), f32),
            pltpu.VMEM((seg, hdim), f32),
            pltpu.VMEM((seg, hdim), f32),
        ],
        compiler_params=pltpu.CompilerParams(vmem_limit_bytes=48 << 20),
        cost_estimate=pl.CostEstimate(
            flops=60 * total_rows * seg * heads * hdim // 8,
            bytes_accessed=4 * total_rows * cols,
            transcendentals=total_rows * seg * heads // 2,
        ),
        name="attention_backward",
    )(gate, resets, depth, qkv, qkv, qkv, grad_attn, lse, mems, nrms)


def tie(value, *others):
    return lax.optimization_barrier((value,) + others)[0]


MESH = pl.DeviceIdType.MESH
dma = pltpu.SemaphoreType.DMA


class Axis:
    def __init__(self, name, rows, cols):
        self.name, self.rows, self.cols = name, rows, cols
        self.size = rows * cols

    def at(self, down, right):
        me = lax.axis_index(self.name)
        row, col = me // self.cols, lax.rem(me, self.cols)
        return lax.rem(row + down, self.rows) * self.cols + lax.rem(col + right, self.cols)

    def to(self, down, right):
        return {"device_id": {self.name: self.at(down, right)}, "device_id_type": MESH}


class Gather:
    def __init__(self, axis, block, outer):
        self.axis, self.outer, self.inputs = axis, outer, [block]
        n, self.chunks = axis.size, block.shape[0]
        lead = (n, self.chunks) if outer else (self.chunks, n)
        self.outputs = [jax.ShapeDtypeStruct(lead + block.shape[1:], block.dtype)]
        held, others = max(axis.rows - 1, 1), axis.cols - 1
        row, col = (held, self.chunks), (others, axis.rows, self.chunks)
        self.scratch = [dma((self.chunks,)), dma(row), dma(row), dma(col), dma(col)]
        self.peers = [(k, 0) for k in range(1, axis.rows)] + [(0, j) for j in range(1, axis.cols)]
        self.bytes = block.size * 2

    def bind(self, ins, outs, scratch):
        (self.src,), (self.dst,) = ins, outs
        self.keep, self.row_out, self.row_in, self.col_out, self.col_in = scratch

    def place(self, dev, c):
        return self.dst.at[dev, c] if self.outer else self.dst.at[c, dev]

    def along(self, k, c):
        axis = self.axis
        return pltpu.make_async_remote_copy(
            src_ref=self.src.at[c],
            dst_ref=self.place(axis.at(0, 0), c),
            send_sem=self.row_out.at[k - 1, c],
            recv_sem=self.row_in.at[k - 1, c],
            **axis.to(k, 0),
        )

    def across(self, k, j, c):
        axis = self.axis
        spot = self.place(axis.at((axis.rows - k) % axis.rows, 0), c)
        return pltpu.make_async_remote_copy(
            src_ref=self.src.at[c] if k == 0 else spot,
            dst_ref=spot,
            send_sem=self.col_out.at[j - 1, k, c],
            recv_sem=self.col_in.at[j - 1, k, c],
            **axis.to(0, j),
        )

    def own(self, c):
        return pltpu.make_async_copy(
            self.src.at[c], self.place(self.axis.at(0, 0), c), self.keep.at[c]
        )

    def start(self):
        for c in range(self.chunks):
            for k in range(1, self.axis.rows):
                self.along(k, c).start()
        for c in range(self.chunks):
            for j in range(1, self.axis.cols):
                self.across(0, j, c).start()
            self.own(c).start()

    def middle(self, part, parts):
        for c in range(self.chunks * part // parts, self.chunks * (part + 1) // parts):
            for k in range(1, self.axis.rows):
                self.along(k, c).wait_recv()
                for j in range(1, self.axis.cols):
                    self.across(k, j, c).start()

    def finish(self):
        for c in range(self.chunks):
            for k in range(1, self.axis.rows):
                self.along(k, c).wait_send()
            for k in range(self.axis.rows):
                for j in range(1, self.axis.cols):
                    self.across(k, j, c).wait()
            self.own(c).wait()


class Exchange:
    def __init__(self, axis, array, shape, source, target):
        self.axis, self.inputs = axis, [array]
        self.outputs = [jax.ShapeDtypeStruct(shape, array.dtype)]
        self.source, self.target = source, target
        n = axis.size
        self.scratch = [dma, dma((n - 1,)), dma((n - 1,))]
        self.peers = [(k, j) for k in range(axis.rows) for j in range(axis.cols)][1:]
        self.bytes = array.size

    def bind(self, ins, outs, scratch):
        (self.src,), (self.dst,) = ins, outs
        self.keep, self.out_sem, self.in_sem = scratch

    def copy(self, i):
        axis, (k, j) = self.axis, self.peers[i]
        return pltpu.make_async_remote_copy(
            src_ref=self.source(self.src, axis.at(k, j)),
            dst_ref=self.target(self.dst, axis.at(0, 0)),
            send_sem=self.out_sem.at[i],
            recv_sem=self.in_sem.at[i],
            **axis.to(k, j),
        )

    def own(self):
        me = self.axis.at(0, 0)
        return pltpu.make_async_copy(self.source(self.src, me), self.target(self.dst, me), self.keep)

    def start(self):
        self.own().start()
        for i in reversed(range(len(self.peers))):
            self.copy(i).start()

    def middle(self, part, parts):
        pass

    def finish(self):
        for i in reversed(range(len(self.peers))):
            self.copy(i).wait()
        self.own().wait()


class Scatter:
    def __init__(self, axis, parts, outer, dtype, ahead=None):
        self.axis, self.outer, self.dtype, self.inputs = axis, outer, dtype, [parts]
        self.chunks = parts.shape[1 if outer else 0]
        block = (self.chunks,) + parts.shape[2:]
        self.outputs = [jax.ShapeDtypeStruct(block, dtype)]
        rows, others, held = axis.rows, axis.cols - 1, max(axis.rows - 1, 1)
        row, col = (held, self.chunks), (others, rows, self.chunks)
        self.scratch = [
            pltpu.VMEM((rows,) + block, bf16),
            pltpu.VMEM((others, rows) + block, bf16),
            pltpu.VMEM((held,) + block, bf16),
            pltpu.VMEM((held,) + block, bf16),
            pltpu.VMEM(block, dtype),
            dma((rows, self.chunks)),
            dma(col),
            dma(col),
            dma(row),
            dma(row),
            dma((self.chunks,)),
        ]
        self.peers = [(k, 0) for k in range(1, rows)] + [(0, j) for j in range(1, axis.cols)]
        self.order = [(k, c) for k in list(range(1, rows)) + [0] for c in range(self.chunks)]
        self.ahead = min(ahead or len(self.order), len(self.order))
        self.bytes = parts.size // axis.size * 2

    def bind(self, ins, outs, scratch):
        (self.src,), (self.dst,) = ins, outs
        self.mine, self.met, self.sent, self.come, self.result = scratch[:5]
        self.load, self.col_out, self.col_in, self.row_out, self.row_in, self.store = scratch[5:]

    def terms(self, dev, c):
        return self.src.at[dev, c] if self.outer else self.src.at[c, dev]

    def read(self, k, c):
        return pltpu.make_async_copy(
            self.terms(self.axis.at(k, 0), c), self.mine.at[k, c], self.load.at[k, c]
        )

    def across(self, k, j, c):
        return pltpu.make_async_remote_copy(
            src_ref=self.terms(self.axis.at(k, j), c),
            dst_ref=self.met.at[j - 1, k, c],
            send_sem=self.col_out.at[j - 1, k, c],
            recv_sem=self.col_in.at[j - 1, k, c],
            **self.axis.to(0, j),
        )

    def along(self, k, c):
        return pltpu.make_async_remote_copy(
            src_ref=self.sent.at[k - 1, c],
            dst_ref=self.come.at[k - 1, c],
            send_sem=self.row_out.at[k - 1, c],
            recv_sem=self.row_in.at[k - 1, c],
            **self.axis.to(k, 0),
        )

    def write(self, c):
        return pltpu.make_async_copy(self.result.at[c], self.dst.at[c], self.store.at[c])

    def leave(self, i):
        if i < len(self.order):
            k, c = self.order[i]
            for j in range(1, self.axis.cols):
                self.across(k, j, c).start()

    def meet(self, k, c):
        self.read(k, c).wait()
        total = self.mine[k, c].astype(f32)
        for j in range(1, self.axis.cols):
            self.across(k, j, c).wait_recv()
            total = total + self.met[j - 1, k, c].astype(f32)
        self.leave(self.order.index((k, c)) + self.ahead)
        return total

    def start(self):
        for i, (k, c) in enumerate(self.order):
            if i < self.ahead:
                self.leave(i)
            self.read(k, c).start()

    def middle(self, part, parts):
        steps = [step for step in self.order if step[0]]
        for k, c in steps[len(steps) * part // parts : len(steps) * (part + 1) // parts]:
            self.sent[k - 1, c] = self.meet(k, c).astype(bf16)
            self.along(k, c).start()

    def finish(self):
        for c in range(self.chunks):
            total = self.meet(0, c)
            for k in range(1, self.axis.rows):
                self.along(k, c).wait_recv()
                total = total + self.come[k - 1, c].astype(f32)
            self.result[c] = total.astype(self.dtype)
            self.write(c).start()
        for k, c in self.order:
            for j in range(1, self.axis.cols):
                self.across(k, j, c).wait_send()
            if k:
                self.along(k, c).wait_send()
        for c in range(self.chunks):
            self.write(c).wait()


class Product:
    def __init__(self, pairs, over, tiles, rows=None):
        self.inputs, self.over = [matrix for pair in pairs for matrix in pair], over
        left, right = pairs[0]
        self.depth, n = left.shape[over[0]], right.shape[1 - over[1]]
        first, m = rows or (0, left.shape[1 - over[0]])
        self.outputs = [jax.ShapeDtypeStruct((m, n), bf16)]
        self.tm, self.tn = min(tiles[0], m), min(tiles[1], n)
        self.grid, self.skip = (m // self.tm, n // self.tn), first // self.tm
        self.scratch, self.peers, self.bytes = [], [], 0

    def bind(self, ins, outs, scratch):
        self.refs = (*ins, *outs)

    def start(self):
        pass

    def middle(self, part, parts):
        pass

    def finish(self):
        pass

    def compute(self):
        def body(*refs):
            total = contract(refs[0][...], refs[1][...], *self.over)
            for i in range(2, len(refs) - 1, 2):
                total = total + contract(refs[i][...], refs[i + 1][...], *self.over)
            refs[-1][...] = total.astype(bf16)

        def tile(size, over, index):
            def at(i, j):
                return (i + self.skip, j)[index]

            if over == 0:
                return pl.BlockSpec((self.depth, size), lambda i, j: (0, at(i, j)))
            return pl.BlockSpec((size, self.depth), lambda i, j: (at(i, j), 0))

        pair = [tile(self.tm, self.over[0], 0), tile(self.tn, self.over[1], 1)]
        pltpu.emit_pipeline(
            body,
            grid=self.grid,
            in_specs=pair * (len(self.inputs) // 2),
            out_specs=[pl.BlockSpec((self.tm, self.tn), lambda i, j: (i, j))],
        )(*self.refs)


class Net:
    def __init__(self, n_seq, n_fsdp):
        rows = 4 if n_fsdp % 4 == 0 else 1
        self.seq = Axis("seq", n_seq // 2, 2)
        self.fsdp = Axis("fsdp", rows, n_fsdp // rows)
        self.calls = 0

    def run(self, jobs, room=32):
        self.calls += 1
        ins = [array for job in jobs for array in job.inputs]
        outs = [shape for job in jobs for shape in job.outputs]
        scratch = [one for job in jobs for one in job.scratch]
        peers = []
        for job in jobs:
            for peer in job.peers:
                if (job.axis, peer) not in peers:
                    peers.append((job.axis, peer))

        def kernel(*refs):
            at = [0, len(ins), len(ins) + len(outs)]
            for job in jobs:
                taken = []
                for part, count in enumerate(
                    (len(job.inputs), len(job.outputs), len(job.scratch))
                ):
                    taken.append(refs[at[part] : at[part] + count])
                    at[part] += count
                job.bind(*taken)
            barrier = pltpu.get_barrier_semaphore()
            for axis, peer in peers:
                pl.semaphore_signal(barrier, inc=1, **axis.to(*peer))
            pl.semaphore_wait(barrier, len(peers))
            for job in jobs:
                job.start()
            parts = 4
            for part in range(parts):
                for job in jobs:
                    job.middle(part, parts)
            for job in jobs:
                if isinstance(job, Product):
                    job.compute()
            for job in jobs:
                job.finish()

        anywhere = pl.BlockSpec(memory_space=pl.ANY)
        return pl.pallas_call(
            kernel,
            in_specs=[anywhere] * len(ins),
            out_specs=[anywhere] * len(outs),
            out_shape=outs,
            scratch_shapes=scratch,
            compiler_params=pltpu.CompilerParams(
                collective_id=self.calls, has_side_effects=True, vmem_limit_bytes=room << 20
            ),
            cost_estimate=pl.CostEstimate(
                flops=0, bytes_accessed=12 * max(job.bytes for job in jobs), transcendentals=0
            ),
            name="net",
        )(*ins)


def own_columns(weight, me, groups, count, each):
    shard = weight.shape[0]
    per = weight.shape[1] // (groups * count * each)
    if each % 128:
        cut = weight.reshape(shard, groups, count, per, each)
        cut = lax.dynamic_index_in_dim(cut, me, 3, keepdims=False)
        return [cut[:, g].reshape(shard, count * each) for g in range(groups)]

    def kernel(me_ref, *refs):
        for g in range(groups):
            refs[groups + g][...] = refs[g][...]

    def source(g):
        return pl.BlockSpec((shard, each), lambda i, me_ref: (0, (g * count + i) * per + me_ref[0]))

    return pl.pallas_call(
        kernel,
        grid_spec=pltpu.PrefetchScalarGridSpec(
            num_scalar_prefetch=1,
            grid=(count,),
            in_specs=[source(g) for g in range(groups)],
            out_specs=[pl.BlockSpec((shard, each), lambda i, me_ref: (0, i))] * groups,
        ),
        out_shape=[jax.ShapeDtypeStruct((shard, count * each), weight.dtype)] * groups,
        name="own_columns",
    )(me.reshape(1), *([weight] * groups))


def spread_columns(arrays, groups, group, count, each, block_rows):
    devices, rows, _ = arrays[0].shape
    wide = devices * each

    def kernel(in_ref, *refs):
        for j in range(devices):
            refs[-1][:, j * each : (j + 1) * each] = in_ref[j].astype(f32)

    return pl.pallas_call(
        kernel,
        grid=(count, rows // block_rows),
        in_specs=[pl.BlockSpec((devices, block_rows, each), lambda i, r: (0, r, i))]
        + [pl.BlockSpec(memory_space=pl.ANY)] * (len(arrays) - 1),
        out_specs=pl.BlockSpec((block_rows, wide), lambda i, r: (r, group * count + i)),
        out_shape=jax.ShapeDtypeStruct((rows, groups * count * wide), f32),
        input_output_aliases={1: 0} if len(arrays) > 1 else {},
        name="spread_columns",
    )(*arrays)


def mm(left, right):
    return jnp.dot(left, right, preferred_element_type=f32)


def mm_nt(left, right):
    return lax.dot_general(left, right, (((1,), (1,)), ((), ())), preferred_element_type=f32)


def mm_tn(left, right):
    return lax.dot_general(left, right, (((0,), (0,)), ((), ())), preferred_element_type=f32)


def make_body(n_seq, n_fsdp):
    def body(
        tokens,
        cotangent,
        w_qkv,
        w_out,
        w_gate_up,
        w_down,
        gain_attn,
        gain_ffn,
        gate_bias,
        memory_in,
        norms_in,
        resets,
        depth,
    ):
        _, segs, local, width = tokens.shape
        heads = gate_bias.shape[0]
        hdim = width // heads
        my_heads = heads // n_seq
        my_width = width // n_seq
        seg = local * n_seq
        rows = segs * local
        total_rows = segs * seg
        shard = w_qkv.shape[0]
        hidden_shard = w_down.shape[0]
        my_hidden = hidden_shard // n_seq
        out_rows = shard // n_seq
        net = Net(n_seq, n_fsdp)
        me = lax.axis_index("seq")

        (qkv_own,) = own_columns(w_qkv, me, 1, 3, my_width)
        gate_own, up_own = own_columns(w_gate_up, me, 2, n_fsdp, my_hidden)
        down_own = lax.dynamic_slice(w_down, (me * my_hidden, 0), (my_hidden, width))
        out_own = lax.dynamic_slice(w_out, (me * out_rows, 0), (out_rows, width))

        x_flat = tokens.reshape(rows, width).astype(f32)
        r_one = rms(x_flat)
        h_one_own = (r_one * gain_attn).astype(bf16)
        grad_y = cotangent.reshape(rows, width)

        def gather_rows(block):
            return lax.all_gather(block, "fsdp", axis=0, tiled=True)

        def token_parts(value):
            return value.reshape(segs, n_seq, local, width)

        def gather_own(value):
            return Gather(net.seq, value.reshape(segs, local, width), False)

        w_g = gather_rows(gate_own)
        h_one, grad_y_all, w_o, w_q = net.run(
            [
                gather_own(h_one_own),
                gather_own(grad_y),
                Gather(net.fsdp, out_own.reshape(1, out_rows, width), True),
                Gather(net.fsdp, qkv_own.reshape(4, shard // 4, 3 * my_width), True),
            ]
        )
        h_one = h_one.reshape(total_rows, width)
        grad_y_all = grad_y_all.reshape(total_rows, width)
        w_q = w_q.reshape(width, 3 * my_width)
        w_u = gather_rows(tie(up_own, w_q))

        qkv = mm(h_one, w_q).astype(bf16)
        gate = jax.nn.sigmoid(lax.dynamic_slice(gate_bias, (me * my_heads,), (my_heads,)))
        memory = lax.dynamic_slice(memory_in[0], (me * my_heads, 0, 0), (my_heads, hdim, hdim))
        norms = lax.dynamic_slice(norms_in[0], (me * my_heads, 0), (my_heads, hdim))
        attn_heads, lse, mems, nrms = attention_forward(qkv, gate, resets[0], memory, norms, segs)

        half = width // 2
        w_d = gather_rows(tie(down_own, attn_heads))

        def columns_of(ref, i):
            return ref.at[:, :, pl.ds(pl.multiple_of(i * my_width, my_width), my_width)]

        def tokens_of(ref, i):
            return ref.at[:, i]

        attn, whole_o = net.run(
            [
                Exchange(
                    net.seq,
                    attn_heads.reshape(segs, n_seq, local, my_width),
                    (segs, local, width),
                    tokens_of,
                    columns_of,
                ),
                Gather(net.seq, w_o.reshape(n_fsdp, out_rows, width), False),
            ]
        )
        attn = attn.reshape(rows, width)
        whole_o = whole_o.reshape(width, width)
        x_one = x_flat + mm(attn, whole_o)
        r_two = rms(x_one)
        h_two_own = (r_two * gain_ffn).astype(bf16)
        (h_two,) = net.run([gather_own(h_two_own)])
        h_two = h_two.reshape(total_rows, width)
        gate_part = mm(h_two, w_g).astype(bf16)
        up_part = mm(h_two, w_u).astype(bf16)
        hidden = swiglu(gate_part.astype(f32), up_part.astype(f32)).astype(bf16)

        def scatter_rows(parts):
            return lax.psum_scatter(parts, "fsdp", scatter_dimension=0, tiled=True)

        down_parts = mm_tn(hidden, grad_y_all).astype(bf16)
        down_term = scatter_rows(down_parts)
        grad_hidden = mm_nt(tie(grad_y_all, down_parts), w_d)
        _, swiglu_back = jax.vjp(swiglu, gate_part.astype(f32), up_part.astype(f32))
        grad_gate, grad_up = swiglu_back(grad_hidden)
        grad_gate, grad_up = grad_gate.astype(bf16), grad_up.astype(bf16)

        def output_terms(s):
            return Product([(hidden, w_d)], (1, 0), (512, 512), (s * seg, seg))

        def h_two_terms(s):
            pairs = [(grad_gate, w_g), (grad_up, w_u)]
            return Product(pairs, (1, 1), (512, 512), (s * seg, seg))

        gate_product = Product([(h_two, grad_gate)], (0, 0), (1024, 512))
        up_product = Product([(h_two, grad_up)], (0, 0), (1024, 512))
        beside = [[output_terms(s)] for s in range(1, segs)]
        beside += [[h_two_terms(s)] for s in range(segs)] + [[up_product]]
        beside[0].append(gate_product)
        terms = mm(hidden[:seg], tie(w_d, grad_up)).astype(bf16)
        sums, gate_parts = [], None
        for products in beside:
            parts = terms.reshape(n_seq, 2, local // 2, width)
            results = net.run([Scatter(net.seq, parts, True, f32)] + products, 56)
            sums.append(results[0])
            terms = results[1]
            if products[-1] is gate_product:
                gate_parts = results[-1]
                gate_term = scatter_rows(gate_parts)
        up_parts = terms
        up_term = scatter_rows(up_parts)
        output = jnp.stack(sums[:segs]).reshape(rows, width)
        grad_h_two = jnp.stack(sums[segs:]).reshape(rows, width)

        gain_ffn_term = jnp.sum(grad_h_two * r_two, axis=0)
        _, norm_two_back = jax.vjp(rms, x_one)
        grad_x_one = grad_y.astype(f32) + norm_two_back(grad_h_two * gain_ffn)[0]
        grad_o = grad_x_one.astype(bf16)

        grad_attn_parts = mm_nt(grad_o, whole_o).astype(bf16)
        grad_attn, out_parts = net.run(
            [
                Exchange(
                    net.seq,
                    grad_attn_parts.reshape(segs, local, width),
                    (segs, n_seq, local, my_width),
                    columns_of,
                    tokens_of,
                ),
                Product([(attn, grad_o)], (0, 0), (1024, 512)),
            ],
            56,
        )
        grad_attn = tie(grad_attn.reshape(total_rows, my_width), down_term)
        grads_q, grads_k, grads_v, bias_terms = attention_backward(
            qkv, grad_attn, gate, resets[0], depth, lse, mems, nrms, segs
        )
        grad_qkv_rows = jnp.concatenate([grads_q, grads_k, grads_v], axis=1)
        out_sum, qkv_parts, grad_h_one = net.run(
            [
                Scatter(net.seq, out_parts.reshape(n_fsdp, n_seq, out_rows, width), False, bf16),
                Product([(h_one, grad_qkv_rows)], (0, 0), (1024, 512)),
                Product([(grad_qkv_rows, w_q)], (1, 1), (1024, 512)),
            ],
            56,
        )
        grad_h_one, qkv_term, out_term, down_all, gate_all = net.run(
            [
                Scatter(net.seq, token_parts(grad_h_one), False, f32),
                Scatter(
                    net.fsdp, qkv_parts.reshape(n_fsdp, 4, shard // 4, 3 * my_width), True, bf16, 5
                ),
                Scatter(net.fsdp, out_sum[:, None], True, bf16, 2),
                Gather(net.seq, down_term[None], True),
                Gather(net.seq, gate_term[None], True),
            ],
            56,
        )
        grad_h_one = grad_h_one.reshape(rows, width)
        output = (x_one + output).astype(bf16).reshape(tokens.shape)
        qkv_term = qkv_term.reshape(shard, 3 * my_width)
        out_term = out_term.reshape(out_rows, width)
        gain_attn_term = jnp.sum(grad_h_one * r_one, axis=0)
        _, norm_one_back = jax.vjp(rms, x_flat)
        grad_x = grad_x_one + norm_one_back(grad_h_one * gain_attn)[0]
        input_grad = grad_x.astype(bf16).reshape(tokens.shape)

        bias_all = lax.dynamic_update_slice(
            jnp.zeros((heads,), f32), bias_terms[:, 0, 0], (me * my_heads,)
        )
        small = jnp.concatenate([gain_attn_term, gain_ffn_term, bias_all])
        wide = -(-small.shape[0] // 1024) * 128
        small = jnp.pad(small, (0, 8 * wide - small.shape[0])).reshape(1, 8, wide)

        qkv_all, out_all, small = net.run(
            [
                Gather(net.seq, qkv_term[None], True),
                Gather(net.seq, out_term[None], True),
                Gather(net.seq, small, True),
            ]
        )
        down_all = down_all.reshape(hidden_shard, width).astype(f32)
        out_all = out_all.reshape(shard, width).astype(f32)
        qkv_all = spread_columns([qkv_all[:, 0]], 1, 0, 3, my_width, shard // 2)
        aligned = my_hidden % 128 == 0
        gate_up_all = gate_all[:, 0]
        if aligned:
            gate_up_all = spread_columns([gate_up_all], 2, 0, n_fsdp, my_hidden, shard)
        up_term = tie(
            up_term, down_all, out_all, qkv_all, gate_up_all, output, input_grad, small
        )
        up_all, small = net.run(
            [
                Gather(net.seq, up_term[None], True),
                Gather(net.fsdp, jnp.sum(small, axis=0), True),
            ]
        )
        small = jnp.sum(small, axis=0).reshape(-1)
        if aligned:
            last = [up_all[:, 0], gate_up_all]
            gate_up_all = spread_columns(last, 2, 1, n_fsdp, my_hidden, shard)
        else:
            cut = jnp.stack([gate_up_all, up_all[:, 0]])
            cut = cut.reshape(2, n_seq, shard, n_fsdp, my_hidden)
            gate_up_all = jnp.transpose(cut, (2, 0, 3, 1, 4)).reshape(shard, -1).astype(f32)

        return (
            output,
            input_grad,
            qkv_all,
            out_all,
            gate_up_all,
            down_all,
            small[:width],
            small[width : 2 * width],
            small[2 * width : 2 * width + heads],
        )

    return body


def solution(mesh):
    rows = P("fsdp", None)
    tokens = P("fsdp", None, "seq", None)
    body = make_body(mesh.shape["seq"], mesh.shape["fsdp"])
    return jax.shard_map(
        body,
        mesh=mesh,
        in_specs=(
            tokens,
            tokens,
            rows,
            rows,
            rows,
            rows,
            P(),
            P(),
            P(),
            P("fsdp", None, None, None),
            P("fsdp", None, None),
            rows,
            P("fsdp"),
        ),
        out_specs=(tokens, tokens, rows, rows, rows, rows, P(), P(), P()),
        check_vma=False,
    )
```

```python
import functools

import jax
import jax.numpy as jnp
from jax import lax
from jax.experimental import pallas as pl
from jax.experimental.pallas import tpu as pltpu
from jax.sharding import PartitionSpec as P

norm_eps = 1e-05
bf16 = jnp.bfloat16
f32 = jnp.float32


def rms(value_rows_segment):
    return value_rows_segment * lax.rsqrt(
        jnp.mean(value_rows_segment * value_rows_segment, axis=-1, keepdims=True) + norm_eps
    )


def swiglu(gate_part, up_part):
    return jax.nn.silu(gate_part) * up_part


def feature(value_rows_segment):
    return jnp.where(
        value_rows_segment > 0,
        value_rows_segment + 1.0,
        jnp.exp(jnp.minimum(value_rows_segment, 0.0)),
    )


def contract(left, right, left_dim, right_dim):
    return lax.dot_general(
        left, right, (((left_dim,), (right_dim,)), ((), ())), preferred_element_type=f32
    )


def split(value):
    high = value.astype(bf16)
    return high, (value - high.astype(f32)).astype(bf16)


def fine(left, right, left_dim, right_dim):
    lh, ll = left
    rh, rl = right
    return (
        contract(lh, rl, left_dim, right_dim)
        + contract(ll, rh, left_dim, right_dim)
        + contract(lh, rh, left_dim, right_dim)
    )


LOG2E = 1.4426950408889634


def scores_of(key, query, block, i):
    n = (i + 1) * block
    sc = contract(key[:n], query, 1, 1)
    rows = lax.broadcasted_iota(jnp.int32, (block, block), 0)
    cols = lax.broadcasted_iota(jnp.int32, (block, block), 1)
    last = jnp.where(rows <= cols, sc[n - block :], -1e30)
    if i == 0:
        return last
    return jnp.concatenate([sc[: n - block], last], axis=0)


def forward_kernel(
    block, segs, gate, resets, q_ref, k_ref, v_ref, m_ref, z_ref, a_ref, lse_ref, mem_ref, nrm_ref, mem, nrm
):
    h, s = pl.program_id(0), pl.program_id(1)
    seg, hdim = q_ref.shape
    scale = LOG2E / hdim**0.5

    @pl.when(s == 0)
    def _():
        mem[...] = m_ref[0]
        nrm[...] = z_ref[0]

    @pl.when(s > 0)
    def _():
        @pl.when(resets[jnp.maximum(s - 1, 0)] > 0)
        def _():
            mem[...] = jnp.zeros_like(mem)
            nrm[...] = jnp.ones_like(nrm)

    mem_ref[0, 0] = mem[...]
    nrm_ref[0, 0] = nrm[...]
    g = gate[h]
    mem_parts = split(mem[...])
    key, value = k_ref[...], v_ref[...]
    value_t = value.T
    for i in range(seg // block):
        rows = slice(i * block, (i + 1) * block)
        query = q_ref[rows, :]
        sc = scores_of(key, query, block, i)
        top = jnp.max(sc, axis=0, keepdims=True)
        weights = jnp.exp2((sc - top) * scale)
        total = jnp.sum(weights, axis=0, keepdims=True)
        lse_ref[0, 0, :, rows] = top * scale + jnp.log2(total)
        adot_t = contract(value_t[:, : (i + 1) * block], weights.astype(bf16), 1, 0)
        adot_t = adot_t * ((1.0 - g) / total)
        sq = feature(query.astype(f32))
        amem = fine(split(sq), mem_parts, 1, 0) * (
            g / jnp.sum(sq * nrm[...], axis=1, keepdims=True)
        )
        a_ref[rows, :] = (amem + adot_t.T).astype(bf16)

    @pl.when(s + 1 < segs)
    def _():
        sk = feature(key.astype(f32))
        sk_parts = split(sk)
        recall = fine(sk_parts, mem_parts, 1, 0) / jnp.sum(sk * nrm[...], axis=1, keepdims=True)
        delta = split(value.astype(f32) - recall)
        mem[...] = mem[...] + fine(sk_parts, delta, 0, 0)
        nrm[...] = nrm[...] + jnp.sum(sk, axis=0, keepdims=True)


def specs(seg, hdim, heads, back, segs):
    def at(part):
        return pl.BlockSpec(
            (seg, hdim), lambda h, t: ((segs - 1 - t) if back else t, part * heads + h)
        )

    return at


def attention_forward(qkv, gate, resets, memory, norms, segs):
    total_rows, cols = qkv.shape
    heads, hdim, _ = memory.shape
    seg = total_rows // segs
    at = specs(seg, hdim, heads, False, segs)
    return pl.pallas_call(
        functools.partial(forward_kernel, min(256, seg), segs),
        grid=(heads, segs),
        in_specs=[
            pl.BlockSpec(memory_space=pltpu.SMEM),
            pl.BlockSpec(memory_space=pltpu.SMEM),
            at(0),
            at(1),
            at(2),
            pl.BlockSpec((1, hdim, hdim), lambda h, t: (h, 0, 0)),
            pl.BlockSpec((1, 1, hdim), lambda h, t: (h, 0, 0)),
        ],
        out_specs=[
            at(0),
            pl.BlockSpec((1, 1, 1, seg), lambda h, t: (h, t, 0, 0)),
            pl.BlockSpec((1, 1, hdim, hdim), lambda h, t: (h, t, 0, 0)),
            pl.BlockSpec((1, 1, 1, hdim), lambda h, t: (h, t, 0, 0)),
        ],
        out_shape=[
            jax.ShapeDtypeStruct((total_rows, heads * hdim), bf16),
            jax.ShapeDtypeStruct((heads, segs, 1, seg), f32),
            jax.ShapeDtypeStruct((heads, segs, hdim, hdim), f32),
            jax.ShapeDtypeStruct((heads, segs, 1, hdim), f32),
        ],
        scratch_shapes=[pltpu.VMEM((hdim, hdim), f32), pltpu.VMEM((1, hdim), f32)],
        compiler_params=pltpu.CompilerParams(vmem_limit_bytes=48 << 20),
        cost_estimate=pl.CostEstimate(
            flops=30 * total_rows * seg * heads * hdim // 8,
            bytes_accessed=4 * total_rows * cols,
            transcendentals=total_rows * seg * heads // 2,
        ),
        name="attention_forward",
    )(gate, resets, qkv, qkv, qkv, memory, norms.reshape(heads, 1, hdim))


def backward_kernel(
    block, segs, gate, resets, depth, q_ref, k_ref, v_ref, da_ref, lse_ref, mem_ref, nrm_ref,
    dq_ref, dk_ref, dv_ref, bias_ref, dm, dz, dk_att, dv_att,
):
    h, t = pl.program_id(0), pl.program_id(1)
    s = segs - 1 - t
    seg, hdim = q_ref.shape
    scale = 1.0 / hdim**0.5
    g = gate[h]

    @pl.when(t == 0)
    def _():
        dm[...] = jnp.zeros_like(dm)
        dz[...] = jnp.zeros_like(dz)
        bias_ref[...] = jnp.zeros_like(bias_ref)

    dk_att[...] = jnp.zeros_like(dk_att)
    dv_att[...] = jnp.zeros_like(dv_att)
    mem, nrm = mem_ref[0, 0], nrm_ref[0, 0]
    mem_parts = split(mem)
    key, value = k_ref[...], v_ref[...]
    key_t = key.T
    term = jnp.zeros((1, 1), f32)
    m_next = jnp.zeros((hdim, hdim), f32)
    z_next = jnp.zeros((1, hdim), f32)
    for i in range(seg // block):
        n = (i + 1) * block
        rows = slice(i * block, n)
        query = q_ref[rows, :]
        sc = scores_of(key, query, block, i)
        probs = jnp.exp2(sc * (scale * LOG2E) - lse_ref[0, 0, :, rows])
        grad_mix = da_ref[rows, :].astype(f32)
        grad_adot = ((1.0 - g) * grad_mix).astype(bf16)
        grad_p = contract(value[:n], grad_adot, 1, 1)
        row = jnp.sum(probs * grad_p, axis=0, keepdims=True)
        grad_s = (probs * (grad_p - row)).astype(bf16)
        dk_att[:n, :] += contract(grad_s, query, 1, 0)
        dv_att[:n, :] += contract(probs.astype(bf16), grad_adot, 1, 0)
        dq = contract(key_t[:, :n], grad_s, 1, 0).T * scale

        qf = query.astype(f32)
        sq = feature(qf)
        slope = jnp.where(qf > 0, 1.0, sq)
        sq_parts = split(sq)
        inverse = 1.0 / jnp.sum(sq * nrm, axis=1, keepdims=True)
        amem = fine(sq_parts, mem_parts, 1, 0) * inverse
        mixed = jnp.sum(grad_mix * amem, axis=1, keepdims=True)
        term = term + (g * (1.0 - g)) * jnp.sum(mixed, axis=0, keepdims=True)
        term = term - g * jnp.sum(row, axis=1, keepdims=True)
        d_top = split(grad_mix * (g * inverse))
        d_low = -(g * mixed) * inverse
        d_sq = fine(d_top, mem_parts, 1, 1) + d_low * nrm
        dq_ref[rows, :] = (dq + d_sq * slope).astype(bf16)
        m_next = m_next + fine(sq_parts, d_top, 0, 0)
        z_next = z_next + jnp.sum(sq * d_low, axis=0, keepdims=True)
    bias_ref[...] += jnp.broadcast_to(term[None], bias_ref.shape)
    dk_ref[...] = (dk_att[...] * scale).astype(bf16)
    dv_ref[...] = dv_att[...].astype(bf16)

    @pl.when(s + 1 < segs)
    def _():
        dm_now, dz_now = dm[...], dz[...]
        dm_parts = split(dm_now)
        kf = key.astype(f32)
        sk = feature(kf)
        slope = jnp.where(kf > 0, 1.0, sk)
        sk_parts = split(sk)
        inverse = 1.0 / jnp.sum(sk * nrm, axis=1, keepdims=True)
        recall = fine(sk_parts, mem_parts, 1, 0) * inverse
        delta = value.astype(f32) - recall
        d_delta = fine(sk_parts, dm_parts, 1, 0)
        d_top = split(-d_delta * inverse)
        d_low = jnp.sum(d_delta * recall, axis=1, keepdims=True) * inverse
        d_sk = (
            fine(split(delta), dm_parts, 1, 1)
            + dz_now
            + fine(d_top, mem_parts, 1, 1)
            + d_low * nrm
        )
        dk_ref[...] = (dk_att[...] * scale + d_sk * slope).astype(bf16)
        dv_ref[...] = (dv_att[...] + d_delta).astype(bf16)
        dm[...] = dm_now + fine(sk_parts, d_top, 0, 0)
        dz[...] = dz_now + jnp.sum(sk * d_low, axis=0, keepdims=True)

    @pl.when(s > 0)
    def _():
        cut = (resets[jnp.maximum(s - 1, 0)] > 0) | (lax.rem(s, depth[0]) == 0)
        dm[...] = jnp.where(cut, 0.0, dm[...] + m_next)
        dz[...] = jnp.where(cut, 0.0, dz[...] + z_next)


def attention_backward(qkv, grad_attn, gate, resets, depth, lse, mems, nrms, segs):
    total_rows, cols = qkv.shape
    heads, _, hdim, _ = mems.shape
    seg = total_rows // segs
    at = specs(seg, hdim, heads, True, segs)
    smem = pl.BlockSpec(memory_space=pltpu.SMEM)
    grad = jax.ShapeDtypeStruct((total_rows, heads * hdim), bf16)
    return pl.pallas_call(
        functools.partial(backward_kernel, min(256, seg), segs),
        grid=(heads, segs),
        in_specs=[
            smem,
            smem,
            smem,
            at(0),
            at(1),
            at(2),
            at(0),
            pl.BlockSpec((1, 1, 1, seg), lambda h, t: (h, segs - 1 - t, 0, 0)),
            pl.BlockSpec((1, 1, hdim, hdim), lambda h, t: (h, segs - 1 - t, 0, 0)),
            pl.BlockSpec((1, 1, 1, hdim), lambda h, t: (h, segs - 1 - t, 0, 0)),
        ],
        out_specs=[at(0), at(0), at(0), pl.BlockSpec((1, 8, hdim), lambda h, t: (h, 0, 0))],
        out_shape=[grad, grad, grad, jax.ShapeDtypeStruct((heads, 8, hdim), f32)],
        scratch_shapes=[
            pltpu.VMEM((hdim, hdim), f32),
            pltpu.VMEM((1, hdim), f32),
            pltpu.VMEM((seg, hdim), f32),
            pltpu.VMEM((seg, hdim), f32),
        ],
        compiler_params=pltpu.CompilerParams(vmem_limit_bytes=48 << 20),
        cost_estimate=pl.CostEstimate(
            flops=60 * total_rows * seg * heads * hdim // 8,
            bytes_accessed=4 * total_rows * cols,
            transcendentals=total_rows * seg * heads // 2,
        ),
        name="attention_backward",
    )(gate, resets, depth, qkv, qkv, qkv, grad_attn, lse, mems, nrms)


def ring_order(n):
    if n % 4 or n < 8:
        return list(range(n))
    wide = n // 4
    walk = []
    for r in range(4):
        cols = range(1, wide) if r % 2 == 0 else range(wide - 1, 0, -1)
        walk += [r * wide + c for c in cols]
    return walk + [r * wide for r in reversed(range(4))]


def reorder(value, order, axis):
    size = value.shape[axis] // len(order)
    return jnp.concatenate(
        [lax.slice_in_dim(value, i * size, (i + 1) * size, axis=axis) for i in order], axis=axis
    )


def tie(value, *others):
    return lax.optimization_barrier((value,) + others)[0]


MESH = pl.DeviceIdType.MESH
dma = pltpu.SemaphoreType.DMA


class Axis:
    def __init__(self, name, rows, cols):
        self.name, self.rows, self.cols = name, rows, cols
        self.size = rows * cols

    def at(self, down, right):
        me = lax.axis_index(self.name)
        row, col = me // self.cols, lax.rem(me, self.cols)
        return lax.rem(row + down, self.rows) * self.cols + lax.rem(col + right, self.cols)

    def to(self, down, right):
        return {"device_id": {self.name: self.at(down, right)}, "device_id_type": MESH}


class Gather:
    def __init__(self, axis, block, outer):
        self.axis, self.outer, self.inputs = axis, outer, [block]
        n, self.chunks = axis.size, block.shape[0]
        lead = (n, self.chunks) if outer else (self.chunks, n)
        self.outputs = [jax.ShapeDtypeStruct(lead + block.shape[1:], block.dtype)]
        held, others = max(axis.rows - 1, 1), axis.cols - 1
        row, col = (held, self.chunks), (others, axis.rows, self.chunks)
        self.scratch = [dma((self.chunks,)), dma(row), dma(row), dma(col), dma(col)]
        self.peers = [(k, 0) for k in range(1, axis.rows)] + [(0, j) for j in range(1, axis.cols)]
        self.bytes = block.size * 2

    def bind(self, ins, outs, scratch):
        (self.src,), (self.dst,) = ins, outs
        self.keep, self.row_out, self.row_in, self.col_out, self.col_in = scratch

    def place(self, dev, c):
        return self.dst.at[dev, c] if self.outer else self.dst.at[c, dev]

    def along(self, k, c):
        axis = self.axis
        return pltpu.make_async_remote_copy(
            src_ref=self.src.at[c],
            dst_ref=self.place(axis.at(0, 0), c),
            send_sem=self.row_out.at[k - 1, c],
            recv_sem=self.row_in.at[k - 1, c],
            **axis.to(k, 0),
        )

    def across(self, k, j, c):
        axis = self.axis
        spot = self.place(axis.at((axis.rows - k) % axis.rows, 0), c)
        return pltpu.make_async_remote_copy(
            src_ref=self.src.at[c] if k == 0 else spot,
            dst_ref=spot,
            send_sem=self.col_out.at[j - 1, k, c],
            recv_sem=self.col_in.at[j - 1, k, c],
            **axis.to(0, j),
        )

    def own(self, c):
        return pltpu.make_async_copy(
            self.src.at[c], self.place(self.axis.at(0, 0), c), self.keep.at[c]
        )

    def start(self):
        for c in range(self.chunks):
            for k in range(1, self.axis.rows):
                self.along(k, c).start()
        for c in range(self.chunks):
            for j in range(1, self.axis.cols):
                self.across(0, j, c).start()
            self.own(c).start()

    def middle(self, part, parts):
        for c in range(self.chunks * part // parts, self.chunks * (part + 1) // parts):
            for k in range(1, self.axis.rows):
                self.along(k, c).wait_recv()
                for j in range(1, self.axis.cols):
                    self.across(k, j, c).start()

    def finish(self):
        for c in range(self.chunks):
            for k in range(1, self.axis.rows):
                self.along(k, c).wait_send()
            for k in range(self.axis.rows):
                for j in range(1, self.axis.cols):
                    self.across(k, j, c).wait()
            self.own(c).wait()


class Exchange:
    def __init__(self, axis, array, shape, source, target):
        self.axis, self.inputs = axis, [array]
        self.outputs = [jax.ShapeDtypeStruct(shape, array.dtype)]
        self.source, self.target = source, target
        n = axis.size
        self.scratch = [dma, dma((n - 1,)), dma((n - 1,))]
        self.peers = [(k, j) for k in range(axis.rows) for j in range(axis.cols)][1:]
        self.bytes = array.size

    def bind(self, ins, outs, scratch):
        (self.src,), (self.dst,) = ins, outs
        self.keep, self.out_sem, self.in_sem = scratch

    def copy(self, i):
        axis, (k, j) = self.axis, self.peers[i]
        return pltpu.make_async_remote_copy(
            src_ref=self.source(self.src, axis.at(k, j)),
            dst_ref=self.target(self.dst, axis.at(0, 0)),
            send_sem=self.out_sem.at[i],
            recv_sem=self.in_sem.at[i],
            **axis.to(k, j),
        )

    def own(self):
        me = self.axis.at(0, 0)
        return pltpu.make_async_copy(self.source(self.src, me), self.target(self.dst, me), self.keep)

    def start(self):
        self.own().start()
        for i in reversed(range(len(self.peers))):
            self.copy(i).start()

    def middle(self, part, parts):
        pass

    def finish(self):
        for i in reversed(range(len(self.peers))):
            self.copy(i).wait()
        self.own().wait()


class Scatter:
    def __init__(self, axis, parts, outer, dtype, ahead=None):
        self.axis, self.outer, self.dtype, self.inputs = axis, outer, dtype, [parts]
        self.chunks = parts.shape[1 if outer else 0]
        block = (self.chunks,) + parts.shape[2:]
        self.outputs = [jax.ShapeDtypeStruct(block, dtype)]
        rows, others, held = axis.rows, axis.cols - 1, max(axis.rows - 1, 1)
        row, col = (held, self.chunks), (others, rows, self.chunks)
        self.scratch = [
            pltpu.VMEM((rows,) + block, bf16),
            pltpu.VMEM((others, rows) + block, bf16),
            pltpu.VMEM((held,) + block, bf16),
            pltpu.VMEM((held,) + block, bf16),
            pltpu.VMEM(block, dtype),
            dma((rows, self.chunks)),
            dma(col),
            dma(col),
            dma(row),
            dma(row),
            dma((self.chunks,)),
        ]
        self.peers = [(k, 0) for k in range(1, rows)] + [(0, j) for j in range(1, axis.cols)]
        self.order = [(k, c) for k in list(range(1, rows)) + [0] for c in range(self.chunks)]
        self.ahead = min(ahead or len(self.order), len(self.order))
        self.bytes = parts.size // axis.size * 2

    def bind(self, ins, outs, scratch):
        (self.src,), (self.dst,) = ins, outs
        self.mine, self.met, self.sent, self.come, self.result = scratch[:5]
        self.load, self.col_out, self.col_in, self.row_out, self.row_in, self.store = scratch[5:]

    def terms(self, dev, c):
        return self.src.at[dev, c] if self.outer else self.src.at[c, dev]

    def read(self, k, c):
        return pltpu.make_async_copy(
            self.terms(self.axis.at(k, 0), c), self.mine.at[k, c], self.load.at[k, c]
        )

    def across(self, k, j, c):
        return pltpu.make_async_remote_copy(
            src_ref=self.terms(self.axis.at(k, j), c),
            dst_ref=self.met.at[j - 1, k, c],
            send_sem=self.col_out.at[j - 1, k, c],
            recv_sem=self.col_in.at[j - 1, k, c],
            **self.axis.to(0, j),
        )

    def along(self, k, c):
        return pltpu.make_async_remote_copy(
            src_ref=self.sent.at[k - 1, c],
            dst_ref=self.come.at[k - 1, c],
            send_sem=self.row_out.at[k - 1, c],
            recv_sem=self.row_in.at[k - 1, c],
            **self.axis.to(k, 0),
        )

    def write(self, c):
        return pltpu.make_async_copy(self.result.at[c], self.dst.at[c], self.store.at[c])

    def leave(self, i):
        if i < len(self.order):
            k, c = self.order[i]
            for j in range(1, self.axis.cols):
                self.across(k, j, c).start()

    def meet(self, k, c):
        self.read(k, c).wait()
        total = self.mine[k, c].astype(f32)
        for j in range(1, self.axis.cols):
            self.across(k, j, c).wait_recv()
            total = total + self.met[j - 1, k, c].astype(f32)
        self.leave(self.order.index((k, c)) + self.ahead)
        return total

    def start(self):
        for i, (k, c) in enumerate(self.order):
            if i < self.ahead:
                self.leave(i)
            self.read(k, c).start()

    def middle(self, part, parts):
        steps = [step for step in self.order if step[0]]
        for k, c in steps[len(steps) * part // parts : len(steps) * (part + 1) // parts]:
            self.sent[k - 1, c] = self.meet(k, c).astype(bf16)
            self.along(k, c).start()

    def finish(self):
        for c in range(self.chunks):
            total = self.meet(0, c)
            for k in range(1, self.axis.rows):
                self.along(k, c).wait_recv()
                total = total + self.come[k - 1, c].astype(f32)
            self.result[c] = total.astype(self.dtype)
            self.write(c).start()
        for k, c in self.order:
            for j in range(1, self.axis.cols):
                self.across(k, j, c).wait_send()
            if k:
                self.along(k, c).wait_send()
        for c in range(self.chunks):
            self.write(c).wait()


class Product:
    def __init__(self, pairs, over, tiles, rows=None):
        self.inputs, self.over = [matrix for pair in pairs for matrix in pair], over
        left, right = pairs[0]
        self.depth, n = left.shape[over[0]], right.shape[1 - over[1]]
        first, m = rows or (0, left.shape[1 - over[0]])
        self.outputs = [jax.ShapeDtypeStruct((m, n), bf16)]
        self.tm, self.tn = min(tiles[0], m), min(tiles[1], n)
        self.grid, self.skip = (m // self.tm, n // self.tn), first // self.tm
        self.scratch, self.peers, self.bytes = [], [], 0

    def bind(self, ins, outs, scratch):
        self.refs = (*ins, *outs)

    def start(self):
        pass

    def middle(self, part, parts):
        pass

    def finish(self):
        pass

    def compute(self):
        def body(*refs):
            total = contract(refs[0][...], refs[1][...], *self.over)
            for i in range(2, len(refs) - 1, 2):
                total = total + contract(refs[i][...], refs[i + 1][...], *self.over)
            refs[-1][...] = total.astype(bf16)

        def tile(size, over, index):
            def at(i, j):
                return (i + self.skip, j)[index]

            if over == 0:
                return pl.BlockSpec((self.depth, size), lambda i, j: (0, at(i, j)))
            return pl.BlockSpec((size, self.depth), lambda i, j: (at(i, j), 0))

        pair = [tile(self.tm, self.over[0], 0), tile(self.tn, self.over[1], 1)]
        pltpu.emit_pipeline(
            body,
            grid=self.grid,
            in_specs=pair * (len(self.inputs) // 2),
            out_specs=[pl.BlockSpec((self.tm, self.tn), lambda i, j: (i, j))],
        )(*self.refs)


class Net:
    def __init__(self, n_seq, n_fsdp):
        rows = 4 if n_fsdp % 4 == 0 else 1
        self.seq = Axis("seq", n_seq // 2, 2)
        self.fsdp = Axis("fsdp", rows, n_fsdp // rows)
        self.calls = 0

    def run(self, jobs, room=32):
        self.calls += 1
        ins = [array for job in jobs for array in job.inputs]
        outs = [shape for job in jobs for shape in job.outputs]
        scratch = [one for job in jobs for one in job.scratch]
        peers = []
        for job in jobs:
            for peer in job.peers:
                if (job.axis, peer) not in peers:
                    peers.append((job.axis, peer))

        def kernel(*refs):
            at = [0, len(ins), len(ins) + len(outs)]
            for job in jobs:
                taken = []
                for part, count in enumerate(
                    (len(job.inputs), len(job.outputs), len(job.scratch))
                ):
                    taken.append(refs[at[part] : at[part] + count])
                    at[part] += count
                job.bind(*taken)
            barrier = pltpu.get_barrier_semaphore()
            for axis, peer in peers:
                pl.semaphore_signal(barrier, inc=1, **axis.to(*peer))
            pl.semaphore_wait(barrier, len(peers))
            for job in jobs:
                job.start()
            parts = 4
            for part in range(parts):
                for job in jobs:
                    job.middle(part, parts)
            for job in jobs:
                if isinstance(job, Product):
                    job.compute()
            for job in jobs:
                job.finish()

        anywhere = pl.BlockSpec(memory_space=pl.ANY)
        return pl.pallas_call(
            kernel,
            in_specs=[anywhere] * len(ins),
            out_specs=[anywhere] * len(outs),
            out_shape=outs,
            scratch_shapes=scratch,
            compiler_params=pltpu.CompilerParams(
                collective_id=self.calls, has_side_effects=True, vmem_limit_bytes=room << 20
            ),
            cost_estimate=pl.CostEstimate(
                flops=0, bytes_accessed=12 * max(job.bytes for job in jobs), transcendentals=0
            ),
            name="net",
        )(*ins)


def own_columns(weight, me, groups, order, each):
    shard, count = weight.shape[0], len(order)
    per = weight.shape[1] // (groups * count * each)
    if each % 128:
        cut = weight.reshape(shard, groups, count, per, each)
        cut = lax.dynamic_index_in_dim(cut, me, 3, keepdims=False)
        return [reorder(cut[:, g], order, 1).reshape(shard, count * each) for g in range(groups)]

    def kernel(me_ref, order_ref, *refs):
        for g in range(groups):
            refs[groups + g][...] = refs[g][...]

    def source(g):
        def at(i, me_ref, order_ref):
            return 0, (g * count + order_ref[i]) * per + me_ref[0]

        return pl.BlockSpec((shard, each), at)

    return pl.pallas_call(
        kernel,
        grid_spec=pltpu.PrefetchScalarGridSpec(
            num_scalar_prefetch=2,
            grid=(count,),
            in_specs=[source(g) for g in range(groups)],
            out_specs=[pl.BlockSpec((shard, each), lambda i, *refs: (0, i))] * groups,
        ),
        out_shape=[jax.ShapeDtypeStruct((shard, count * each), weight.dtype)] * groups,
        name="own_columns",
    )(me.reshape(1), jnp.array(order, jnp.int32), *([weight] * groups))


def spread_columns(arrays, groups, group, order, each, block_rows):
    devices, rows, _ = arrays[0].shape
    wide, count = devices * each, len(order)

    def kernel(order_ref, in_ref, *refs):
        for j in range(devices):
            refs[-1][:, j * each : (j + 1) * each] = in_ref[j].astype(f32)

    return pl.pallas_call(
        kernel,
        grid_spec=pltpu.PrefetchScalarGridSpec(
            num_scalar_prefetch=1,
            grid=(count, rows // block_rows),
            in_specs=[
                pl.BlockSpec((devices, block_rows, each), lambda i, r, order_ref: (0, r, i))
            ]
            + [pl.BlockSpec(memory_space=pl.ANY)] * (len(arrays) - 1),
            out_specs=pl.BlockSpec(
                (block_rows, wide), lambda i, r, order_ref: (r, group * count + order_ref[i])
            ),
        ),
        out_shape=jax.ShapeDtypeStruct((rows, groups * count * wide), f32),
        input_output_aliases={2: 0} if len(arrays) > 1 else {},
        name="spread_columns",
    )(jnp.array(order, jnp.int32), *arrays)


def mm(left, right):
    return jnp.dot(left, right, preferred_element_type=f32)


def mm_nt(left, right):
    return lax.dot_general(left, right, (((1,), (1,)), ((), ())), preferred_element_type=f32)


def mm_tn(left, right):
    return lax.dot_general(left, right, (((0,), (0,)), ((), ())), preferred_element_type=f32)


def make_body(n_seq, n_fsdp):
    def body(
        tokens,
        cotangent,
        w_qkv,
        w_out,
        w_gate_up,
        w_down,
        gain_attn,
        gain_ffn,
        gate_bias,
        memory_in,
        norms_in,
        resets,
        depth,
    ):
        _, segs, local, width = tokens.shape
        heads = gate_bias.shape[0]
        hdim = width // heads
        my_heads = heads // n_seq
        my_width = width // n_seq
        seg = local * n_seq
        rows = segs * local
        total_rows = segs * seg
        shard = w_qkv.shape[0]
        hidden_shard = w_down.shape[0]
        my_hidden = hidden_shard // n_seq
        out_rows = shard // n_seq
        net = Net(n_seq, n_fsdp)
        me = lax.axis_index("seq")

        ring = ring_order(n_fsdp)
        back = [ring.index(i) for i in range(n_fsdp)]
        (qkv_own,) = own_columns(w_qkv, me, 1, range(3), my_width)
        gate_own, up_own = own_columns(w_gate_up, me, 2, ring, my_hidden)
        down_own = lax.dynamic_slice(w_down, (me * my_hidden, 0), (my_hidden, width))
        out_own = lax.dynamic_slice(w_out, (me * out_rows, 0), (out_rows, width))

        x_flat = tokens.reshape(rows, width).astype(f32)
        r_one = rms(x_flat)
        h_one_own = reorder((r_one * gain_attn).astype(bf16), ring, 1)
        grad_y = cotangent.reshape(rows, width)

        def gather_rows(block):
            return lax.all_gather(block, "fsdp", axis=0, tiled=True, axis_index_groups=[ring])

        def token_parts(value):
            return value.reshape(segs, n_seq, local, width)

        def gather_own(value):
            return Gather(net.seq, value.reshape(segs, local, width), False)

        w_o = gather_rows(tie(out_own, h_one_own))
        w_q = gather_rows(tie(qkv_own, h_one_own))
        (h_one,) = net.run([gather_own(h_one_own)])
        h_one = h_one.reshape(total_rows, width)
        w_g = gather_rows(tie(gate_own, h_one))
        w_o = reorder(tie(w_o, h_one), back, 0)
        (whole_o,) = net.run([Gather(net.seq, w_o.reshape(n_fsdp, out_rows, width), False)])
        whole_o = whole_o.reshape(width, width)
        w_u = gather_rows(tie(up_own, whole_o))

        qkv = mm(h_one, w_q).astype(bf16)
        gate = jax.nn.sigmoid(lax.dynamic_slice(gate_bias, (me * my_heads,), (my_heads,)))
        memory = lax.dynamic_slice(memory_in[0], (me * my_heads, 0, 0), (my_heads, hdim, hdim))
        norms = lax.dynamic_slice(norms_in[0], (me * my_heads, 0), (my_heads, hdim))
        attn_heads, lse, mems, nrms = attention_forward(qkv, gate, resets[0], memory, norms, segs)

        half = width // 2
        w_d = gather_rows(tie(down_own, attn_heads))

        def columns_of(ref, i):
            return ref.at[:, :, pl.ds(pl.multiple_of(i * my_width, my_width), my_width)]

        def tokens_of(ref, i):
            return ref.at[:, i]

        (attn,) = net.run(
            [
                Exchange(
                    net.seq,
                    attn_heads.reshape(segs, n_seq, local, my_width),
                    (segs, local, width),
                    tokens_of,
                    columns_of,
                ),
            ]
        )
        attn = attn.reshape(rows, width)
        x_one = x_flat + mm(attn, whole_o)
        r_two = rms(x_one)
        h_two_own = reorder((r_two * gain_ffn).astype(bf16), ring, 1)
        (h_two,) = net.run([gather_own(h_two_own)])
        h_two = h_two.reshape(total_rows, width)
        grad_y_all, gate_part = net.run(
            [gather_own(tie(grad_y, h_two)), Product([(h_two, w_g)], (1, 0), (1024, 512))], 56
        )
        grad_y_all = grad_y_all.reshape(total_rows, width)
        up_part = mm(h_two, w_u).astype(bf16)
        hidden = swiglu(gate_part.astype(f32), up_part.astype(f32)).astype(bf16)

        def scatter_rows(parts):
            return lax.psum_scatter(
                parts, "fsdp", scatter_dimension=0, tiled=True, axis_index_groups=[ring]
            )

        down_parts = mm_tn(hidden, grad_y_all).astype(bf16)
        down_term = scatter_rows(down_parts)
        grad_hidden = mm_nt(tie(grad_y_all, down_parts), w_d)
        _, swiglu_back = jax.vjp(swiglu, gate_part.astype(f32), up_part.astype(f32))
        grad_gate, grad_up = swiglu_back(grad_hidden)
        grad_gate, grad_up = grad_gate.astype(bf16), grad_up.astype(bf16)

        def output_terms(s):
            return Product([(hidden, w_d)], (1, 0), (512, 512), (s * seg, seg))

        def h_two_terms(s):
            pairs = [(grad_gate, w_g), (grad_up, w_u)]
            return Product(pairs, (1, 1), (512, 512), (s * seg, seg))

        gate_product = Product([(h_two, grad_gate)], (0, 0), (1024, 512))
        up_product = Product([(h_two, grad_up)], (0, 0), (1024, 512))
        beside = [[output_terms(s)] for s in range(1, segs)]
        beside += [[h_two_terms(s)] for s in range(segs)] + [[up_product]]
        beside[0].append(gate_product)
        terms = mm(hidden[:seg], tie(w_d, grad_up)).astype(bf16)
        sums, gate_parts = [], None
        for products in beside:
            parts = terms.reshape(n_seq, 2, local // 2, width)
            results = net.run([Scatter(net.seq, parts, True, f32)] + products, 56)
            sums.append(results[0])
            terms = results[1]
            if products[-1] is gate_product:
                gate_parts = results[-1]
                gate_term = scatter_rows(gate_parts)
        up_parts = terms
        up_term = scatter_rows(up_parts)
        output = jnp.stack(sums[:segs]).reshape(rows, width)
        grad_h_two = reorder(jnp.stack(sums[segs:]).reshape(rows, width), back, 1)

        gain_ffn_term = jnp.sum(grad_h_two * r_two, axis=0)
        _, norm_two_back = jax.vjp(rms, x_one)
        grad_x_one = grad_y.astype(f32) + norm_two_back(grad_h_two * gain_ffn)[0]
        grad_o = grad_x_one.astype(bf16)

        grad_attn_parts = mm_nt(grad_o, whole_o).astype(bf16)
        grad_attn, out_parts = net.run(
            [
                Exchange(
                    net.seq,
                    grad_attn_parts.reshape(segs, local, width),
                    (segs, n_seq, local, my_width),
                    columns_of,
                    tokens_of,
                ),
                Product([(attn, grad_o)], (0, 0), (1024, 512)),
            ],
            56,
        )
        grad_attn = tie(grad_attn.reshape(total_rows, my_width), down_term)
        grads_q, grads_k, grads_v, bias_terms = attention_backward(
            qkv, grad_attn, gate, resets[0], depth, lse, mems, nrms, segs
        )
        grad_qkv_rows = jnp.concatenate([grads_q, grads_k, grads_v], axis=1)
        out_parts = tie(out_parts, gate_term)
        out_sum, qkv_parts, grad_h_one = net.run(
            [
                Scatter(net.seq, out_parts.reshape(n_fsdp, n_seq, out_rows, width), False, bf16),
                Product([(h_one, grad_qkv_rows)], (0, 0), (1024, 512)),
                Product([(grad_qkv_rows, w_q)], (1, 1), (1024, 512)),
            ],
            56,
        )
        qkv_term = scatter_rows(qkv_parts)
        grad_h_one, out_term, down_all, gate_all, up_all = net.run(
            [
                Scatter(net.seq, token_parts(tie(grad_h_one, up_term)), False, f32),
                Scatter(net.fsdp, out_sum[:, None], True, bf16, 2),
                Gather(net.seq, down_term[None], True),
                Gather(net.seq, gate_term[None], True),
                Gather(net.seq, up_term[None], True),
            ],
            56,
        )
        grad_h_one = reorder(grad_h_one.reshape(rows, width), back, 1)
        output = (x_one + output).astype(bf16).reshape(tokens.shape)
        gain_attn_term = jnp.sum(grad_h_one * r_one, axis=0)
        _, norm_one_back = jax.vjp(rms, x_flat)
        grad_x = grad_x_one + norm_one_back(grad_h_one * gain_attn)[0]
        input_grad = grad_x.astype(bf16).reshape(tokens.shape)

        bias_all = lax.dynamic_update_slice(
            jnp.zeros((heads,), f32), bias_terms[:, 0, 0], (me * my_heads,)
        )
        small = jnp.concatenate([gain_attn_term, gain_ffn_term, bias_all])
        wide = -(-small.shape[0] // 1024) * 128
        small = jnp.pad(small, (0, 8 * wide - small.shape[0])).reshape(1, 8, wide)

        down_all = down_all.reshape(hidden_shard, width).astype(f32)
        aligned = my_hidden % 128 == 0
        if aligned:
            gate_up_all = spread_columns([gate_all[:, 0]], 2, 0, ring, my_hidden, shard)
            gate_up_all = spread_columns([up_all[:, 0], gate_up_all], 2, 1, ring, my_hidden, shard)
        else:
            cut = jnp.stack([gate_all, up_all]).reshape(2, n_seq, shard, n_fsdp, my_hidden)
            cut = reorder(cut, back, 3)
            gate_up_all = jnp.transpose(cut, (2, 0, 3, 1, 4)).reshape(shard, -1).astype(f32)
        qkv_term = tie(qkv_term, down_all, gate_up_all, output, input_grad)
        (small,) = net.run([Gather(net.fsdp, small, True)])
        qkv_all, out_all, small = net.run(
            [
                Gather(net.seq, qkv_term[None], True),
                Gather(net.seq, out_term, True),
                Gather(net.seq, jnp.sum(small, axis=0), True),
            ]
        )
        small = jnp.sum(small, axis=0).reshape(-1)
        out_all = out_all.reshape(shard, width).astype(f32)
        qkv_all = spread_columns([qkv_all[:, 0]], 1, 0, range(3), my_width, shard // 2)

        return (
            output,
            input_grad,
            qkv_all,
            out_all,
            gate_up_all,
            down_all,
            small[:width],
            small[width : 2 * width],
            small[2 * width : 2 * width + heads],
        )

    return body


def solution(mesh):
    rows = P("fsdp", None)
    tokens = P("fsdp", None, "seq", None)
    body = make_body(mesh.shape["seq"], mesh.shape["fsdp"])
    return jax.shard_map(
        body,
        mesh=mesh,
        in_specs=(
            tokens,
            tokens,
            rows,
            rows,
            rows,
            rows,
            P(),
            P(),
            P(),
            P("fsdp", None, None, None),
            P("fsdp", None, None),
            rows,
            P("fsdp"),
        ),
        out_specs=(tokens, tokens, rows, rows, rows, rows, P(), P(), P()),
        check_vma=False,
    )
```

```python
import functools

import jax
import jax.numpy as jnp
from jax import lax
from jax.experimental import pallas as pl
from jax.experimental.pallas import tpu as pltpu
from jax.sharding import PartitionSpec as P

norm_eps = 1e-05
bf16 = jnp.bfloat16
f32 = jnp.float32


def rms(value_rows_segment):
    return value_rows_segment * lax.rsqrt(
        jnp.mean(value_rows_segment * value_rows_segment, axis=-1, keepdims=True) + norm_eps
    )


def swiglu(gate_part, up_part):
    return jax.nn.silu(gate_part) * up_part


def feature(value_rows_segment):
    return jnp.where(
        value_rows_segment > 0,
        value_rows_segment + 1.0,
        jnp.exp(jnp.minimum(value_rows_segment, 0.0)),
    )


def contract(left, right, left_dim, right_dim):
    return lax.dot_general(
        left, right, (((left_dim,), (right_dim,)), ((), ())), preferred_element_type=f32
    )


def split(value):
    high = value.astype(bf16)
    return high, (value - high.astype(f32)).astype(bf16)


def fine(left, right, left_dim, right_dim):
    lh, ll = left
    rh, rl = right
    return (
        contract(lh, rl, left_dim, right_dim)
        + contract(ll, rh, left_dim, right_dim)
        + contract(lh, rh, left_dim, right_dim)
    )


LOG2E = 1.4426950408889634


def scores_of(key, query, block, i):
    n = (i + 1) * block
    sc = contract(key[:n], query, 1, 1)
    rows = lax.broadcasted_iota(jnp.int32, (block, block), 0)
    cols = lax.broadcasted_iota(jnp.int32, (block, block), 1)
    last = jnp.where(rows <= cols, sc[n - block :], -1e30)
    if i == 0:
        return last
    return jnp.concatenate([sc[: n - block], last], axis=0)


def forward_kernel(
    block, segs, gate, resets, q_ref, k_ref, v_ref, m_ref, z_ref, a_ref, lse_ref, mem_ref, nrm_ref, mem, nrm
):
    h, s = pl.program_id(0), pl.program_id(1)
    seg, hdim = q_ref.shape
    scale = LOG2E / hdim**0.5

    @pl.when(s == 0)
    def _():
        mem[...] = m_ref[0]
        nrm[...] = z_ref[0]

    @pl.when(s > 0)
    def _():
        @pl.when(resets[jnp.maximum(s - 1, 0)] > 0)
        def _():
            mem[...] = jnp.zeros_like(mem)
            nrm[...] = jnp.ones_like(nrm)

    mem_ref[0, 0] = mem[...]
    nrm_ref[0, 0] = nrm[...]
    g = gate[h]
    mem_parts = split(mem[...])
    key, value = k_ref[...], v_ref[...]
    value_t = value.T
    for i in range(seg // block):
        rows = slice(i * block, (i + 1) * block)
        query = q_ref[rows, :]
        sc = scores_of(key, query, block, i)
        top = jnp.max(sc, axis=0, keepdims=True)
        weights = jnp.exp2((sc - top) * scale)
        total = jnp.sum(weights, axis=0, keepdims=True)
        lse_ref[0, 0, :, rows] = top * scale + jnp.log2(total)
        adot_t = contract(value_t[:, : (i + 1) * block], weights.astype(bf16), 1, 0)
        adot_t = adot_t * ((1.0 - g) / total)
        sq = feature(query.astype(f32))
        amem = fine(split(sq), mem_parts, 1, 0) * (
            g / jnp.sum(sq * nrm[...], axis=1, keepdims=True)
        )
        a_ref[rows, :] = (amem + adot_t.T).astype(bf16)

    @pl.when(s + 1 < segs)
    def _():
        sk = feature(key.astype(f32))
        sk_parts = split(sk)
        recall = fine(sk_parts, mem_parts, 1, 0) / jnp.sum(sk * nrm[...], axis=1, keepdims=True)
        delta = split(value.astype(f32) - recall)
        mem[...] = mem[...] + fine(sk_parts, delta, 0, 0)
        nrm[...] = nrm[...] + jnp.sum(sk, axis=0, keepdims=True)


def specs(seg, hdim, heads, back, segs):
    def at(part):
        return pl.BlockSpec(
            (seg, hdim), lambda h, t: ((segs - 1 - t) if back else t, part * heads + h)
        )

    return at


def attention_forward(qkv, gate, resets, memory, norms, segs):
    total_rows, cols = qkv.shape
    heads, hdim, _ = memory.shape
    seg = total_rows // segs
    at = specs(seg, hdim, heads, False, segs)
    return pl.pallas_call(
        functools.partial(forward_kernel, min(256, seg), segs),
        grid=(heads, segs),
        in_specs=[
            pl.BlockSpec(memory_space=pltpu.SMEM),
            pl.BlockSpec(memory_space=pltpu.SMEM),
            at(0),
            at(1),
            at(2),
            pl.BlockSpec((1, hdim, hdim), lambda h, t: (h, 0, 0)),
            pl.BlockSpec((1, 1, hdim), lambda h, t: (h, 0, 0)),
        ],
        out_specs=[
            at(0),
            pl.BlockSpec((1, 1, 1, seg), lambda h, t: (h, t, 0, 0)),
            pl.BlockSpec((1, 1, hdim, hdim), lambda h, t: (h, t, 0, 0)),
            pl.BlockSpec((1, 1, 1, hdim), lambda h, t: (h, t, 0, 0)),
        ],
        out_shape=[
            jax.ShapeDtypeStruct((total_rows, heads * hdim), bf16),
            jax.ShapeDtypeStruct((heads, segs, 1, seg), f32),
            jax.ShapeDtypeStruct((heads, segs, hdim, hdim), f32),
            jax.ShapeDtypeStruct((heads, segs, 1, hdim), f32),
        ],
        scratch_shapes=[pltpu.VMEM((hdim, hdim), f32), pltpu.VMEM((1, hdim), f32)],
        compiler_params=pltpu.CompilerParams(vmem_limit_bytes=48 << 20),
        cost_estimate=pl.CostEstimate(
            flops=30 * total_rows * seg * heads * hdim // 8,
            bytes_accessed=4 * total_rows * cols,
            transcendentals=total_rows * seg * heads // 2,
        ),
        name="attention_forward",
    )(gate, resets, qkv, qkv, qkv, memory, norms.reshape(heads, 1, hdim))


def backward_kernel(
    block, segs, gate, resets, depth, q_ref, k_ref, v_ref, da_ref, lse_ref, mem_ref, nrm_ref,
    dq_ref, dk_ref, dv_ref, bias_ref, dm, dz, dk_att, dv_att,
):
    h, t = pl.program_id(0), pl.program_id(1)
    s = segs - 1 - t
    seg, hdim = q_ref.shape
    scale = 1.0 / hdim**0.5
    g = gate[h]

    @pl.when(t == 0)
    def _():
        dm[...] = jnp.zeros_like(dm)
        dz[...] = jnp.zeros_like(dz)
        bias_ref[...] = jnp.zeros_like(bias_ref)

    dk_att[...] = jnp.zeros_like(dk_att)
    dv_att[...] = jnp.zeros_like(dv_att)
    mem, nrm = mem_ref[0, 0], nrm_ref[0, 0]
    mem_parts = split(mem)
    key, value = k_ref[...], v_ref[...]
    key_t = key.T
    term = jnp.zeros((1, 1), f32)
    m_next = jnp.zeros((hdim, hdim), f32)
    z_next = jnp.zeros((1, hdim), f32)
    for i in range(seg // block):
        n = (i + 1) * block
        rows = slice(i * block, n)
        query = q_ref[rows, :]
        sc = scores_of(key, query, block, i)
        probs = jnp.exp2(sc * (scale * LOG2E) - lse_ref[0, 0, :, rows])
        grad_mix = da_ref[rows, :].astype(f32)
        grad_adot = ((1.0 - g) * grad_mix).astype(bf16)
        grad_p = contract(value[:n], grad_adot, 1, 1)
        row = jnp.sum(probs * grad_p, axis=0, keepdims=True)
        grad_s = (probs * (grad_p - row)).astype(bf16)
        dk_att[:n, :] += contract(grad_s, query, 1, 0)
        dv_att[:n, :] += contract(probs.astype(bf16), grad_adot, 1, 0)
        dq = contract(key_t[:, :n], grad_s, 1, 0).T * scale

        qf = query.astype(f32)
        sq = feature(qf)
        slope = jnp.where(qf > 0, 1.0, sq)
        sq_parts = split(sq)
        inverse = 1.0 / jnp.sum(sq * nrm, axis=1, keepdims=True)
        amem = fine(sq_parts, mem_parts, 1, 0) * inverse
        mixed = jnp.sum(grad_mix * amem, axis=1, keepdims=True)
        term = term + (g * (1.0 - g)) * jnp.sum(mixed, axis=0, keepdims=True)
        term = term - g * jnp.sum(row, axis=1, keepdims=True)
        d_top = split(grad_mix * (g * inverse))
        d_low = -(g * mixed) * inverse
        d_sq = fine(d_top, mem_parts, 1, 1) + d_low * nrm
        dq_ref[rows, :] = (dq + d_sq * slope).astype(bf16)
        m_next = m_next + fine(sq_parts, d_top, 0, 0)
        z_next = z_next + jnp.sum(sq * d_low, axis=0, keepdims=True)
    bias_ref[...] += jnp.broadcast_to(term[None], bias_ref.shape)
    dk_ref[...] = (dk_att[...] * scale).astype(bf16)
    dv_ref[...] = dv_att[...].astype(bf16)

    @pl.when(s + 1 < segs)
    def _():
        dm_now, dz_now = dm[...], dz[...]
        dm_parts = split(dm_now)
        kf = key.astype(f32)
        sk = feature(kf)
        slope = jnp.where(kf > 0, 1.0, sk)
        sk_parts = split(sk)
        inverse = 1.0 / jnp.sum(sk * nrm, axis=1, keepdims=True)
        recall = fine(sk_parts, mem_parts, 1, 0) * inverse
        delta = value.astype(f32) - recall
        d_delta = fine(sk_parts, dm_parts, 1, 0)
        d_top = split(-d_delta * inverse)
        d_low = jnp.sum(d_delta * recall, axis=1, keepdims=True) * inverse
        d_sk = (
            fine(split(delta), dm_parts, 1, 1)
            + dz_now
            + fine(d_top, mem_parts, 1, 1)
            + d_low * nrm
        )
        dk_ref[...] = (dk_att[...] * scale + d_sk * slope).astype(bf16)
        dv_ref[...] = (dv_att[...] + d_delta).astype(bf16)
        dm[...] = dm_now + fine(sk_parts, d_top, 0, 0)
        dz[...] = dz_now + jnp.sum(sk * d_low, axis=0, keepdims=True)

    @pl.when(s > 0)
    def _():
        cut = (resets[jnp.maximum(s - 1, 0)] > 0) | (lax.rem(s, depth[0]) == 0)
        dm[...] = jnp.where(cut, 0.0, dm[...] + m_next)
        dz[...] = jnp.where(cut, 0.0, dz[...] + z_next)


def attention_backward(qkv, grad_attn, gate, resets, depth, lse, mems, nrms, segs):
    total_rows, cols = qkv.shape
    heads, _, hdim, _ = mems.shape
    seg = total_rows // segs
    at = specs(seg, hdim, heads, True, segs)
    smem = pl.BlockSpec(memory_space=pltpu.SMEM)
    grad = jax.ShapeDtypeStruct((total_rows, heads * hdim), bf16)
    return pl.pallas_call(
        functools.partial(backward_kernel, min(256, seg), segs),
        grid=(heads, segs),
        in_specs=[
            smem,
            smem,
            smem,
            at(0),
            at(1),
            at(2),
            at(0),
            pl.BlockSpec((1, 1, 1, seg), lambda h, t: (h, segs - 1 - t, 0, 0)),
            pl.BlockSpec((1, 1, hdim, hdim), lambda h, t: (h, segs - 1 - t, 0, 0)),
            pl.BlockSpec((1, 1, 1, hdim), lambda h, t: (h, segs - 1 - t, 0, 0)),
        ],
        out_specs=[at(0), at(0), at(0), pl.BlockSpec((1, 8, hdim), lambda h, t: (h, 0, 0))],
        out_shape=[grad, grad, grad, jax.ShapeDtypeStruct((heads, 8, hdim), f32)],
        scratch_shapes=[
            pltpu.VMEM((hdim, hdim), f32),
            pltpu.VMEM((1, hdim), f32),
            pltpu.VMEM((seg, hdim), f32),
            pltpu.VMEM((seg, hdim), f32),
        ],
        compiler_params=pltpu.CompilerParams(vmem_limit_bytes=48 << 20),
        cost_estimate=pl.CostEstimate(
            flops=60 * total_rows * seg * heads * hdim // 8,
            bytes_accessed=4 * total_rows * cols,
            transcendentals=total_rows * seg * heads // 2,
        ),
        name="attention_backward",
    )(gate, resets, depth, qkv, qkv, qkv, grad_attn, lse, mems, nrms)


def ring_order(n):
    if n % 4 or n < 8:
        return list(range(n))
    wide = n // 4
    walk = []
    for r in range(4):
        cols = range(1, wide) if r % 2 == 0 else range(wide - 1, 0, -1)
        walk += [r * wide + c for c in cols]
    return walk + [r * wide for r in reversed(range(4))]


def reorder(value, order, axis):
    size = value.shape[axis] // len(order)
    return jnp.concatenate(
        [lax.slice_in_dim(value, i * size, (i + 1) * size, axis=axis) for i in order], axis=axis
    )


def move_blocks(value, order, axis):
    n = len(order)
    block = (value.shape[0] // n, value.shape[1]) if axis == 0 else (value.shape[0], value.shape[1] // n)

    def kernel(order_ref, in_ref, out_ref):
        out_ref[...] = in_ref[...]

    def at(i):
        return (i, 0) if axis == 0 else (0, i)

    return pl.pallas_call(
        kernel,
        grid_spec=pltpu.PrefetchScalarGridSpec(
            num_scalar_prefetch=1,
            grid=(n,),
            in_specs=[pl.BlockSpec(block, lambda i, order_ref: at(order_ref[i]))],
            out_specs=pl.BlockSpec(block, lambda i, order_ref: at(i)),
        ),
        out_shape=jax.ShapeDtypeStruct(value.shape, value.dtype),
        name="move_blocks",
    )(jnp.array(order, jnp.int32), value)


def tie(value, *others):
    return lax.optimization_barrier((value,) + others)[0]


MESH = pl.DeviceIdType.MESH
dma = pltpu.SemaphoreType.DMA


class Axis:
    def __init__(self, name, rows, cols):
        self.name, self.rows, self.cols = name, rows, cols
        self.size = rows * cols

    def at(self, down, right):
        me = lax.axis_index(self.name)
        row, col = me // self.cols, lax.rem(me, self.cols)
        return lax.rem(row + down, self.rows) * self.cols + lax.rem(col + right, self.cols)

    def to(self, down, right):
        return {"device_id": {self.name: self.at(down, right)}, "device_id_type": MESH}


class Gather:
    def __init__(self, axis, block, outer):
        self.axis, self.outer, self.inputs = axis, outer, [block]
        n, self.chunks = axis.size, block.shape[0]
        lead = (n, self.chunks) if outer else (self.chunks, n)
        self.outputs = [jax.ShapeDtypeStruct(lead + block.shape[1:], block.dtype)]
        held, others = max(axis.rows - 1, 1), axis.cols - 1
        row, col = (held, self.chunks), (others, axis.rows, self.chunks)
        self.scratch = [dma((self.chunks,)), dma(row), dma(row), dma(col), dma(col)]
        self.peers = [(k, 0) for k in range(1, axis.rows)] + [(0, j) for j in range(1, axis.cols)]
        self.bytes = block.size * 2

    def bind(self, ins, outs, scratch):
        (self.src,), (self.dst,) = ins, outs
        self.keep, self.row_out, self.row_in, self.col_out, self.col_in = scratch

    def place(self, dev, c):
        return self.dst.at[dev, c] if self.outer else self.dst.at[c, dev]

    def along(self, k, c):
        axis = self.axis
        return pltpu.make_async_remote_copy(
            src_ref=self.src.at[c],
            dst_ref=self.place(axis.at(0, 0), c),
            send_sem=self.row_out.at[k - 1, c],
            recv_sem=self.row_in.at[k - 1, c],
            **axis.to(k, 0),
        )

    def across(self, k, j, c):
        axis = self.axis
        spot = self.place(axis.at((axis.rows - k) % axis.rows, 0), c)
        return pltpu.make_async_remote_copy(
            src_ref=self.src.at[c] if k == 0 else spot,
            dst_ref=spot,
            send_sem=self.col_out.at[j - 1, k, c],
            recv_sem=self.col_in.at[j - 1, k, c],
            **axis.to(0, j),
        )

    def own(self, c):
        return pltpu.make_async_copy(
            self.src.at[c], self.place(self.axis.at(0, 0), c), self.keep.at[c]
        )

    def start(self):
        for c in range(self.chunks):
            for k in range(1, self.axis.rows):
                self.along(k, c).start()
        for c in range(self.chunks):
            for j in range(1, self.axis.cols):
                self.across(0, j, c).start()
            self.own(c).start()

    def middle(self, part, parts):
        for c in range(self.chunks * part // parts, self.chunks * (part + 1) // parts):
            for k in range(1, self.axis.rows):
                self.along(k, c).wait_recv()
                for j in range(1, self.axis.cols):
                    self.across(k, j, c).start()

    def finish(self):
        for c in range(self.chunks):
            for k in range(1, self.axis.rows):
                self.along(k, c).wait_send()
            for k in range(self.axis.rows):
                for j in range(1, self.axis.cols):
                    self.across(k, j, c).wait()
            self.own(c).wait()


class Exchange:
    def __init__(self, axis, array, shape, source, target):
        self.axis, self.inputs = axis, [array]
        self.outputs = [jax.ShapeDtypeStruct(shape, array.dtype)]
        self.source, self.target = source, target
        n = axis.size
        self.scratch = [dma, dma((n - 1,)), dma((n - 1,))]
        self.peers = [(k, j) for k in range(axis.rows) for j in range(axis.cols)][1:]
        self.bytes = array.size

    def bind(self, ins, outs, scratch):
        (self.src,), (self.dst,) = ins, outs
        self.keep, self.out_sem, self.in_sem = scratch

    def copy(self, i):
        axis, (k, j) = self.axis, self.peers[i]
        return pltpu.make_async_remote_copy(
            src_ref=self.source(self.src, axis.at(k, j)),
            dst_ref=self.target(self.dst, axis.at(0, 0)),
            send_sem=self.out_sem.at[i],
            recv_sem=self.in_sem.at[i],
            **axis.to(k, j),
        )

    def own(self):
        me = self.axis.at(0, 0)
        return pltpu.make_async_copy(self.source(self.src, me), self.target(self.dst, me), self.keep)

    def start(self):
        self.own().start()
        for i in reversed(range(len(self.peers))):
            self.copy(i).start()

    def middle(self, part, parts):
        pass

    def finish(self):
        for i in reversed(range(len(self.peers))):
            self.copy(i).wait()
        self.own().wait()


class Scatter:
    def __init__(self, axis, parts, outer, dtype, ahead=None):
        self.axis, self.outer, self.dtype, self.inputs = axis, outer, dtype, [parts]
        self.chunks = parts.shape[1 if outer else 0]
        block = (self.chunks,) + parts.shape[2:]
        self.outputs = [jax.ShapeDtypeStruct(block, dtype)]
        rows, others, held = axis.rows, axis.cols - 1, max(axis.rows - 1, 1)
        row, col = (held, self.chunks), (others, rows, self.chunks)
        self.scratch = [
            pltpu.VMEM((rows,) + block, bf16),
            pltpu.VMEM((others, rows) + block, bf16),
            pltpu.VMEM((held,) + block, bf16),
            pltpu.VMEM((held,) + block, bf16),
            pltpu.VMEM(block, dtype),
            dma((rows, self.chunks)),
            dma(col),
            dma(col),
            dma(row),
            dma(row),
            dma((self.chunks,)),
        ]
        self.peers = [(k, 0) for k in range(1, rows)] + [(0, j) for j in range(1, axis.cols)]
        self.order = [(k, c) for k in list(range(1, rows)) + [0] for c in range(self.chunks)]
        self.ahead = min(ahead or len(self.order), len(self.order))
        self.bytes = parts.size // axis.size * 2

    def bind(self, ins, outs, scratch):
        (self.src,), (self.dst,) = ins, outs
        self.mine, self.met, self.sent, self.come, self.result = scratch[:5]
        self.load, self.col_out, self.col_in, self.row_out, self.row_in, self.store = scratch[5:]

    def terms(self, dev, c):
        return self.src.at[dev, c] if self.outer else self.src.at[c, dev]

    def read(self, k, c):
        return pltpu.make_async_copy(
            self.terms(self.axis.at(k, 0), c), self.mine.at[k, c], self.load.at[k, c]
        )

    def across(self, k, j, c):
        return pltpu.make_async_remote_copy(
            src_ref=self.terms(self.axis.at(k, j), c),
            dst_ref=self.met.at[j - 1, k, c],
            send_sem=self.col_out.at[j - 1, k, c],
            recv_sem=self.col_in.at[j - 1, k, c],
            **self.axis.to(0, j),
        )

    def along(self, k, c):
        return pltpu.make_async_remote_copy(
            src_ref=self.sent.at[k - 1, c],
            dst_ref=self.come.at[k - 1, c],
            send_sem=self.row_out.at[k - 1, c],
            recv_sem=self.row_in.at[k - 1, c],
            **self.axis.to(k, 0),
        )

    def write(self, c):
        return pltpu.make_async_copy(self.result.at[c], self.dst.at[c], self.store.at[c])

    def leave(self, i):
        if i < len(self.order):
            k, c = self.order[i]
            for j in range(1, self.axis.cols):
                self.across(k, j, c).start()

    def meet(self, k, c):
        self.read(k, c).wait()
        total = self.mine[k, c].astype(f32)
        for j in range(1, self.axis.cols):
            self.across(k, j, c).wait_recv()
            total = total + self.met[j - 1, k, c].astype(f32)
        self.leave(self.order.index((k, c)) + self.ahead)
        return total

    def start(self):
        for i, (k, c) in enumerate(self.order):
            if i < self.ahead:
                self.leave(i)
            self.read(k, c).start()

    def middle(self, part, parts):
        steps = [step for step in self.order if step[0]]
        for k, c in steps[len(steps) * part // parts : len(steps) * (part + 1) // parts]:
            self.sent[k - 1, c] = self.meet(k, c).astype(bf16)
            self.along(k, c).start()

    def finish(self):
        for c in range(self.chunks):
            total = self.meet(0, c)
            for k in range(1, self.axis.rows):
                self.along(k, c).wait_recv()
                total = total + self.come[k - 1, c].astype(f32)
            self.result[c] = total.astype(self.dtype)
            self.write(c).start()
        for k, c in self.order:
            for j in range(1, self.axis.cols):
                self.across(k, j, c).wait_send()
            if k:
                self.along(k, c).wait_send()
        for c in range(self.chunks):
            self.write(c).wait()


class Product:
    def __init__(self, pairs, over, tiles, rows=None):
        self.inputs, self.over = [matrix for pair in pairs for matrix in pair], over
        left, right = pairs[0]
        self.depth, n = left.shape[over[0]], right.shape[1 - over[1]]
        first, m = rows or (0, left.shape[1 - over[0]])
        self.outputs = [jax.ShapeDtypeStruct((m, n), bf16)]
        self.tm, self.tn = min(tiles[0], m), min(tiles[1], n)
        self.grid, self.skip = (m // self.tm, n // self.tn), first // self.tm
        self.scratch, self.peers, self.bytes = [], [], 0

    def bind(self, ins, outs, scratch):
        self.refs = (*ins, *outs)

    def start(self):
        pass

    def middle(self, part, parts):
        pass

    def finish(self):
        pass

    def compute(self):
        def body(*refs):
            total = contract(refs[0][...], refs[1][...], *self.over)
            for i in range(2, len(refs) - 1, 2):
                total = total + contract(refs[i][...], refs[i + 1][...], *self.over)
            refs[-1][...] = total.astype(bf16)

        def tile(size, over, index):
            def at(i, j):
                return (i + self.skip, j)[index]

            if over == 0:
                return pl.BlockSpec((self.depth, size), lambda i, j: (0, at(i, j)))
            return pl.BlockSpec((size, self.depth), lambda i, j: (at(i, j), 0))

        pair = [tile(self.tm, self.over[0], 0), tile(self.tn, self.over[1], 1)]
        pltpu.emit_pipeline(
            body,
            grid=self.grid,
            in_specs=pair * (len(self.inputs) // 2),
            out_specs=[pl.BlockSpec((self.tm, self.tn), lambda i, j: (i, j))],
        )(*self.refs)


class Net:
    def __init__(self, n_seq, n_fsdp):
        rows = 4 if n_fsdp % 4 == 0 else 1
        self.seq = Axis("seq", n_seq // 2, 2)
        self.fsdp = Axis("fsdp", rows, n_fsdp // rows)
        self.calls = 0

    def run(self, jobs, room=32):
        self.calls += 1
        ins = [array for job in jobs for array in job.inputs]
        outs = [shape for job in jobs for shape in job.outputs]
        scratch = [one for job in jobs for one in job.scratch]
        peers = []
        for job in jobs:
            for peer in job.peers:
                if (job.axis, peer) not in peers:
                    peers.append((job.axis, peer))

        def kernel(*refs):
            at = [0, len(ins), len(ins) + len(outs)]
            for job in jobs:
                taken = []
                for part, count in enumerate(
                    (len(job.inputs), len(job.outputs), len(job.scratch))
                ):
                    taken.append(refs[at[part] : at[part] + count])
                    at[part] += count
                job.bind(*taken)
            barrier = pltpu.get_barrier_semaphore()
            for axis, peer in peers:
                pl.semaphore_signal(barrier, inc=1, **axis.to(*peer))
            pl.semaphore_wait(barrier, len(peers))
            for job in jobs:
                job.start()
            products = [job for job in jobs if not job.peers]
            late = [job for job in jobs if products and isinstance(job, Gather)]
            parts = 4
            for some in ([job for job in jobs if job not in late], late):
                for part in range(parts):
                    for job in some:
                        job.middle(part, parts)
                if some is not late:
                    for job in products:
                        job.compute()
            for job in jobs:
                job.finish()

        anywhere = pl.BlockSpec(memory_space=pl.ANY)
        return pl.pallas_call(
            kernel,
            in_specs=[anywhere] * len(ins),
            out_specs=[anywhere] * len(outs),
            out_shape=outs,
            scratch_shapes=scratch,
            compiler_params=pltpu.CompilerParams(
                collective_id=self.calls, has_side_effects=True, vmem_limit_bytes=room << 20
            ),
            cost_estimate=pl.CostEstimate(
                flops=0, bytes_accessed=12 * max(job.bytes for job in jobs), transcendentals=0
            ),
            name="net",
        )(*ins)


def own_columns(weight, me, groups, order, each):
    shard, count = weight.shape[0], len(order)
    per = weight.shape[1] // (groups * count * each)
    if each % 128:
        cut = weight.reshape(shard, groups, count, per, each)
        cut = lax.dynamic_index_in_dim(cut, me, 3, keepdims=False)
        return [reorder(cut[:, g], order, 1).reshape(shard, count * each) for g in range(groups)]

    def kernel(me_ref, order_ref, *refs):
        for g in range(groups):
            refs[groups + g][...] = refs[g][...]

    def source(g):
        def at(i, me_ref, order_ref):
            return 0, (g * count + order_ref[i]) * per + me_ref[0]

        return pl.BlockSpec((shard, each), at)

    return pl.pallas_call(
        kernel,
        grid_spec=pltpu.PrefetchScalarGridSpec(
            num_scalar_prefetch=2,
            grid=(count,),
            in_specs=[source(g) for g in range(groups)],
            out_specs=[pl.BlockSpec((shard, each), lambda i, *refs: (0, i))] * groups,
        ),
        out_shape=[jax.ShapeDtypeStruct((shard, count * each), weight.dtype)] * groups,
        name="own_columns",
    )(me.reshape(1), jnp.array(order, jnp.int32), *([weight] * groups))


def spread_columns(arrays, groups, group, order, each, block_rows):
    devices, rows, _ = arrays[0].shape
    wide, count = devices * each, len(order)

    def kernel(order_ref, in_ref, *refs):
        for j in range(devices):
            refs[-1][:, j * each : (j + 1) * each] = in_ref[j].astype(f32)

    return pl.pallas_call(
        kernel,
        grid_spec=pltpu.PrefetchScalarGridSpec(
            num_scalar_prefetch=1,
            grid=(count, rows // block_rows),
            in_specs=[
                pl.BlockSpec((devices, block_rows, each), lambda i, r, order_ref: (0, r, i))
            ]
            + [pl.BlockSpec(memory_space=pl.ANY)] * (len(arrays) - 1),
            out_specs=pl.BlockSpec(
                (block_rows, wide), lambda i, r, order_ref: (r, group * count + order_ref[i])
            ),
        ),
        out_shape=jax.ShapeDtypeStruct((rows, groups * count * wide), f32),
        input_output_aliases={2: 0} if len(arrays) > 1 else {},
        name="spread_columns",
    )(jnp.array(order, jnp.int32), *arrays)


def mm(left, right):
    return jnp.dot(left, right, preferred_element_type=f32)


def mm_nt(left, right):
    return lax.dot_general(left, right, (((1,), (1,)), ((), ())), preferred_element_type=f32)


def mm_tn(left, right):
    return lax.dot_general(left, right, (((0,), (0,)), ((), ())), preferred_element_type=f32)


def make_body(n_seq, n_fsdp):
    def body(
        tokens,
        cotangent,
        w_qkv,
        w_out,
        w_gate_up,
        w_down,
        gain_attn,
        gain_ffn,
        gate_bias,
        memory_in,
        norms_in,
        resets,
        depth,
    ):
        _, segs, local, width = tokens.shape
        heads = gate_bias.shape[0]
        hdim = width // heads
        my_heads = heads // n_seq
        my_width = width // n_seq
        seg = local * n_seq
        rows = segs * local
        total_rows = segs * seg
        shard = w_qkv.shape[0]
        hidden_shard = w_down.shape[0]
        my_hidden = hidden_shard // n_seq
        out_rows = shard // n_seq
        net = Net(n_seq, n_fsdp)
        me = lax.axis_index("seq")

        ring = ring_order(n_fsdp)
        back = [ring.index(i) for i in range(n_fsdp)]
        (qkv_own,) = own_columns(w_qkv, me, 1, range(3), my_width)
        gate_own, up_own = own_columns(w_gate_up, me, 2, ring, my_hidden)
        down_own = lax.dynamic_slice(w_down, (me * my_hidden, 0), (my_hidden, width))
        out_own = lax.dynamic_slice(w_out, (me * out_rows, 0), (out_rows, width))

        x_flat = tokens.reshape(rows, width).astype(f32)
        r_one = rms(x_flat)
        h_one_own = reorder((r_one * gain_attn).astype(bf16), ring, 1)
        grad_y = cotangent.reshape(rows, width)

        def gather_rows(block):
            return lax.all_gather(block, "fsdp", axis=0, tiled=True, axis_index_groups=[ring])

        def token_parts(value):
            return value.reshape(segs, n_seq, local, width)

        def gather_own(value):
            return Gather(net.seq, value.reshape(segs, local, width), False)

        w_o = gather_rows(tie(out_own, h_one_own))
        w_q = gather_rows(tie(qkv_own, h_one_own))
        (h_one,) = net.run([gather_own(h_one_own)])
        h_one = h_one.reshape(total_rows, width)
        w_g = gather_rows(tie(gate_own, h_one))
        w_o = move_blocks(tie(w_o, h_one), back, 0)
        (whole_o,) = net.run([Gather(net.seq, w_o.reshape(n_fsdp, out_rows, width), False)])
        whole_o = whole_o.reshape(width, width)
        w_u = gather_rows(tie(up_own, whole_o))

        qkv = mm(h_one, w_q).astype(bf16)
        gate = jax.nn.sigmoid(lax.dynamic_slice(gate_bias, (me * my_heads,), (my_heads,)))
        memory = lax.dynamic_slice(memory_in[0], (me * my_heads, 0, 0), (my_heads, hdim, hdim))
        norms = lax.dynamic_slice(norms_in[0], (me * my_heads, 0), (my_heads, hdim))
        attn_heads, lse, mems, nrms = attention_forward(qkv, gate, resets[0], memory, norms, segs)

        half = width // 2
        w_d = gather_rows(tie(down_own, attn_heads))

        def columns_of(ref, i):
            return ref.at[:, :, pl.ds(pl.multiple_of(i * my_width, my_width), my_width)]

        def tokens_of(ref, i):
            return ref.at[:, i]

        (attn,) = net.run(
            [
                Exchange(
                    net.seq,
                    attn_heads.reshape(segs, n_seq, local, my_width),
                    (segs, local, width),
                    tokens_of,
                    columns_of,
                ),
            ]
        )
        attn = attn.reshape(rows, width)
        x_one = x_flat + mm(attn, whole_o)
        r_two = rms(x_one)
        h_two_own = reorder((r_two * gain_ffn).astype(bf16), ring, 1)
        (h_two,) = net.run([gather_own(h_two_own)])
        h_two = h_two.reshape(total_rows, width)
        grad_y_all, gate_part = net.run(
            [gather_own(tie(grad_y, h_two)), Product([(h_two, w_g)], (1, 0), (1024, 512))], 56
        )
        grad_y_all = grad_y_all.reshape(total_rows, width)
        up_part = mm(h_two, w_u).astype(bf16)
        hidden = swiglu(gate_part.astype(f32), up_part.astype(f32)).astype(bf16)

        def scatter_rows(parts):
            return lax.psum_scatter(
                parts, "fsdp", scatter_dimension=0, tiled=True, axis_index_groups=[ring]
            )

        down_parts = mm_tn(hidden, grad_y_all).astype(bf16)
        down_term = scatter_rows(down_parts)
        grad_hidden = mm_nt(tie(grad_y_all, down_parts), w_d)
        _, swiglu_back = jax.vjp(swiglu, gate_part.astype(f32), up_part.astype(f32))
        grad_gate, grad_up = swiglu_back(grad_hidden)
        grad_gate, grad_up = grad_gate.astype(bf16), grad_up.astype(bf16)

        def output_terms(s):
            return Product([(hidden, w_d)], (1, 0), (512, 512), (s * seg, seg))

        def h_two_terms(s):
            pairs = [(grad_gate, w_g), (grad_up, w_u)]
            return Product(pairs, (1, 1), (512, 512), (s * seg, seg))

        gate_product = Product([(h_two, grad_gate)], (0, 0), (1024, 512))
        up_product = Product([(h_two, grad_up)], (0, 0), (1024, 512))
        beside = [[output_terms(s)] for s in range(1, segs)]
        beside += [[h_two_terms(s)] for s in range(segs)] + [[up_product]]
        beside[0].append(gate_product)
        terms = mm(hidden[:seg], tie(w_d, grad_up)).astype(bf16)
        sums, gate_parts = [], None
        for products in beside:
            parts = terms.reshape(n_seq, 2, local // 2, width)
            results = net.run([Scatter(net.seq, parts, True, f32)] + products, 56)
            sums.append(results[0])
            terms = results[1]
            if products[-1] is gate_product:
                gate_parts = results[-1]
                gate_term = scatter_rows(gate_parts)
        up_parts = terms
        up_term = scatter_rows(up_parts)
        output = jnp.stack(sums[:segs]).reshape(rows, width)
        grad_h_two = reorder(jnp.stack(sums[segs:]).reshape(rows, width), back, 1)

        gain_ffn_term = jnp.sum(grad_h_two * r_two, axis=0)
        _, norm_two_back = jax.vjp(rms, x_one)
        grad_x_one = grad_y.astype(f32) + norm_two_back(grad_h_two * gain_ffn)[0]
        grad_o = grad_x_one.astype(bf16)

        grad_attn_parts = mm_nt(grad_o, whole_o).astype(bf16)
        grad_attn, out_parts = net.run(
            [
                Exchange(
                    net.seq,
                    grad_attn_parts.reshape(segs, local, width),
                    (segs, n_seq, local, my_width),
                    columns_of,
                    tokens_of,
                ),
                Product([(attn, grad_o)], (0, 0), (1024, 512)),
            ],
            56,
        )
        grad_attn = tie(grad_attn.reshape(total_rows, my_width), down_term)
        grads_q, grads_k, grads_v, bias_terms = attention_backward(
            qkv, grad_attn, gate, resets[0], depth, lse, mems, nrms, segs
        )
        grad_qkv_rows = jnp.concatenate([grads_q, grads_k, grads_v], axis=1)
        out_parts = tie(out_parts, gate_term)
        out_sum, qkv_parts, grad_h_one = net.run(
            [
                Scatter(net.seq, out_parts.reshape(n_fsdp, n_seq, out_rows, width), False, bf16),
                Product([(h_one, grad_qkv_rows)], (0, 0), (1024, 512)),
                Product([(grad_qkv_rows, w_q)], (1, 1), (1024, 512)),
            ],
            56,
        )
        qkv_term = scatter_rows(qkv_parts)
        grad_h_one, out_term, down_all, gate_all, up_all = net.run(
            [
                Scatter(net.seq, token_parts(tie(grad_h_one, up_term)), False, f32),
                Scatter(net.fsdp, out_sum[:, None], True, bf16, 2),
                Gather(net.seq, down_term[None], True),
                Gather(net.seq, gate_term[None], True),
                Gather(net.seq, up_term[None], True),
            ],
            56,
        )
        grad_h_one = move_blocks(grad_h_one.reshape(rows, width), back, 1)
        output = (x_one + output).astype(bf16).reshape(tokens.shape)
        gain_attn_term = jnp.sum(grad_h_one * r_one, axis=0)
        _, norm_one_back = jax.vjp(rms, x_flat)
        grad_x = grad_x_one + norm_one_back(grad_h_one * gain_attn)[0]
        input_grad = grad_x.astype(bf16).reshape(tokens.shape)

        bias_all = lax.dynamic_update_slice(
            jnp.zeros((heads,), f32), bias_terms[:, 0, 0], (me * my_heads,)
        )
        small = jnp.concatenate([gain_attn_term, gain_ffn_term, bias_all])
        wide = -(-small.shape[0] // 1024) * 128
        small = jnp.pad(small, (0, 8 * wide - small.shape[0])).reshape(1, 8, wide)

        down_all = down_all.reshape(hidden_shard, width).astype(f32)
        aligned = my_hidden % 128 == 0
        if aligned:
            gate_up_all = spread_columns([gate_all[:, 0]], 2, 0, ring, my_hidden, shard)
            gate_up_all = spread_columns([up_all[:, 0], gate_up_all], 2, 1, ring, my_hidden, shard)
        else:
            cut = jnp.stack([gate_all, up_all]).reshape(2, n_seq, shard, n_fsdp, my_hidden)
            cut = reorder(cut, back, 3)
            gate_up_all = jnp.transpose(cut, (2, 0, 3, 1, 4)).reshape(shard, -1).astype(f32)
        qkv_all = lax.all_gather(tie(qkv_term, grad_h_one), "seq", axis=0)
        out_all = lax.all_gather(out_term.reshape(out_rows, width), "seq", axis=0)
        (small,) = net.run([Gather(net.fsdp, small, True)])
        (small,) = net.run([Gather(net.seq, jnp.sum(small, axis=0), True)])
        small = jnp.sum(small, axis=0).reshape(-1)
        out_all = out_all.reshape(shard, width).astype(f32)
        qkv_all = tie(qkv_all, down_all, gate_up_all, output, input_grad, small)
        qkv_all = spread_columns([qkv_all], 1, 0, range(3), my_width, shard // 2)

        return (
            output,
            input_grad,
            qkv_all,
            out_all,
            gate_up_all,
            down_all,
            small[:width],
            small[width : 2 * width],
            small[2 * width : 2 * width + heads],
        )

    return body


def solution(mesh):
    rows = P("fsdp", None)
    tokens = P("fsdp", None, "seq", None)
    body = make_body(mesh.shape["seq"], mesh.shape["fsdp"])
    return jax.shard_map(
        body,
        mesh=mesh,
        in_specs=(
            tokens,
            tokens,
            rows,
            rows,
            rows,
            rows,
            P(),
            P(),
            P(),
            P("fsdp", None, None, None),
            P("fsdp", None, None),
            rows,
            P("fsdp"),
        ),
        out_specs=(tokens, tokens, rows, rows, rows, rows, P(), P(), P()),
        check_vma=False,
    )
```

```python
import functools

import jax
import jax.numpy as jnp
from jax import lax
from jax.experimental import pallas as pl
from jax.experimental.pallas import tpu as pltpu
from jax.sharding import PartitionSpec as P

norm_eps = 1e-05
bf16 = jnp.bfloat16
f32 = jnp.float32


def rms(value_rows_segment):
    return value_rows_segment * lax.rsqrt(
        jnp.mean(value_rows_segment * value_rows_segment, axis=-1, keepdims=True) + norm_eps
    )


def swiglu(gate_part, up_part):
    return jax.nn.silu(gate_part) * up_part


def feature(value_rows_segment):
    return jnp.where(
        value_rows_segment > 0,
        value_rows_segment + 1.0,
        jnp.exp(jnp.minimum(value_rows_segment, 0.0)),
    )


def contract(left, right, left_dim, right_dim):
    return lax.dot_general(
        left, right, (((left_dim,), (right_dim,)), ((), ())), preferred_element_type=f32
    )


def split(value):
    high = value.astype(bf16)
    return high, (value - high.astype(f32)).astype(bf16)


def fine(left, right, left_dim, right_dim):
    lh, ll = left
    rh, rl = right
    return (
        contract(lh, rl, left_dim, right_dim)
        + contract(ll, rh, left_dim, right_dim)
        + contract(lh, rh, left_dim, right_dim)
    )


LOG2E = 1.4426950408889634


def scores_of(key, query, block, i):
    n = (i + 1) * block
    sc = contract(key[:n], query, 1, 1)
    rows = lax.broadcasted_iota(jnp.int32, (block, block), 0)
    cols = lax.broadcasted_iota(jnp.int32, (block, block), 1)
    last = jnp.where(rows <= cols, sc[n - block :], -1e30)
    if i == 0:
        return last
    return jnp.concatenate([sc[: n - block], last], axis=0)


def forward_kernel(
    block, segs, gate, resets, q_ref, k_ref, v_ref, m_ref, z_ref, a_ref, lse_ref, mem_ref, nrm_ref, mem, nrm
):
    h, s = pl.program_id(0), pl.program_id(1)
    seg, hdim = q_ref.shape
    scale = LOG2E / hdim**0.5

    @pl.when(s == 0)
    def _():
        mem[...] = m_ref[0]
        nrm[...] = z_ref[0]

    @pl.when(s > 0)
    def _():
        @pl.when(resets[jnp.maximum(s - 1, 0)] > 0)
        def _():
            mem[...] = jnp.zeros_like(mem)
            nrm[...] = jnp.ones_like(nrm)

    mem_ref[0, 0] = mem[...]
    nrm_ref[0, 0] = nrm[...]
    g = gate[h]
    mem_parts = split(mem[...])
    key, value = k_ref[...], v_ref[...]
    value_t = value.T
    for i in range(seg // block):
        rows = slice(i * block, (i + 1) * block)
        query = q_ref[rows, :]
        sc = scores_of(key, query, block, i)
        top = jnp.max(sc, axis=0, keepdims=True)
        weights = jnp.exp2((sc - top) * scale)
        total = jnp.sum(weights, axis=0, keepdims=True)
        lse_ref[0, 0, :, rows] = top * scale + jnp.log2(total)
        adot_t = contract(value_t[:, : (i + 1) * block], weights.astype(bf16), 1, 0)
        adot_t = adot_t * ((1.0 - g) / total)
        sq = feature(query.astype(f32))
        amem = fine(split(sq), mem_parts, 1, 0) * (
            g / jnp.sum(sq * nrm[...], axis=1, keepdims=True)
        )
        a_ref[rows, :] = (amem + adot_t.T).astype(bf16)

    @pl.when(s + 1 < segs)
    def _():
        sk = feature(key.astype(f32))
        sk_parts = split(sk)
        recall = fine(sk_parts, mem_parts, 1, 0) / jnp.sum(sk * nrm[...], axis=1, keepdims=True)
        delta = split(value.astype(f32) - recall)
        mem[...] = mem[...] + fine(sk_parts, delta, 0, 0)
        nrm[...] = nrm[...] + jnp.sum(sk, axis=0, keepdims=True)


def specs(seg, hdim, heads, back, segs):
    def at(part):
        return pl.BlockSpec(
            (seg, hdim), lambda h, t: ((segs - 1 - t) if back else t, part * heads + h)
        )

    return at


def attention_forward(qkv, gate, resets, memory, norms, segs):
    total_rows, cols = qkv.shape
    heads, hdim, _ = memory.shape
    seg = total_rows // segs
    at = specs(seg, hdim, heads, False, segs)
    return pl.pallas_call(
        functools.partial(forward_kernel, min(256, seg), segs),
        grid=(heads, segs),
        in_specs=[
            pl.BlockSpec(memory_space=pltpu.SMEM),
            pl.BlockSpec(memory_space=pltpu.SMEM),
            at(0),
            at(1),
            at(2),
            pl.BlockSpec((1, hdim, hdim), lambda h, t: (h, 0, 0)),
            pl.BlockSpec((1, 1, hdim), lambda h, t: (h, 0, 0)),
        ],
        out_specs=[
            at(0),
            pl.BlockSpec((1, 1, 1, seg), lambda h, t: (h, t, 0, 0)),
            pl.BlockSpec((1, 1, hdim, hdim), lambda h, t: (h, t, 0, 0)),
            pl.BlockSpec((1, 1, 1, hdim), lambda h, t: (h, t, 0, 0)),
        ],
        out_shape=[
            jax.ShapeDtypeStruct((total_rows, heads * hdim), bf16),
            jax.ShapeDtypeStruct((heads, segs, 1, seg), f32),
            jax.ShapeDtypeStruct((heads, segs, hdim, hdim), f32),
            jax.ShapeDtypeStruct((heads, segs, 1, hdim), f32),
        ],
        scratch_shapes=[pltpu.VMEM((hdim, hdim), f32), pltpu.VMEM((1, hdim), f32)],
        compiler_params=pltpu.CompilerParams(vmem_limit_bytes=48 << 20),
        cost_estimate=pl.CostEstimate(
            flops=30 * total_rows * seg * heads * hdim // 8,
            bytes_accessed=4 * total_rows * cols,
            transcendentals=total_rows * seg * heads // 2,
        ),
        name="attention_forward",
    )(gate, resets, qkv, qkv, qkv, memory, norms.reshape(heads, 1, hdim))


def backward_kernel(
    block, segs, gate, resets, depth, q_ref, k_ref, v_ref, da_ref, lse_ref, mem_ref, nrm_ref,
    dq_ref, dk_ref, dv_ref, bias_ref, dm, dz, dk_att, dv_att,
):
    h, t = pl.program_id(0), pl.program_id(1)
    s = segs - 1 - t
    seg, hdim = q_ref.shape
    scale = 1.0 / hdim**0.5
    g = gate[h]

    @pl.when(t == 0)
    def _():
        dm[...] = jnp.zeros_like(dm)
        dz[...] = jnp.zeros_like(dz)
        bias_ref[...] = jnp.zeros_like(bias_ref)

    dk_att[...] = jnp.zeros_like(dk_att)
    dv_att[...] = jnp.zeros_like(dv_att)
    mem, nrm = mem_ref[0, 0], nrm_ref[0, 0]
    mem_parts = split(mem)
    key, value = k_ref[...], v_ref[...]
    key_t = key.T
    term = jnp.zeros((1, 1), f32)
    m_next = jnp.zeros((hdim, hdim), f32)
    z_next = jnp.zeros((1, hdim), f32)
    for i in range(seg // block):
        n = (i + 1) * block
        rows = slice(i * block, n)
        query = q_ref[rows, :]
        sc = scores_of(key, query, block, i)
        probs = jnp.exp2(sc * (scale * LOG2E) - lse_ref[0, 0, :, rows])
        grad_mix = da_ref[rows, :].astype(f32)
        grad_adot = ((1.0 - g) * grad_mix).astype(bf16)
        grad_p = contract(value[:n], grad_adot, 1, 1)
        row = jnp.sum(probs * grad_p, axis=0, keepdims=True)
        grad_s = (probs * (grad_p - row)).astype(bf16)
        dk_att[:n, :] += contract(grad_s, query, 1, 0)
        dv_att[:n, :] += contract(probs.astype(bf16), grad_adot, 1, 0)
        dq = contract(key_t[:, :n], grad_s, 1, 0).T * scale

        qf = query.astype(f32)
        sq = feature(qf)
        slope = jnp.where(qf > 0, 1.0, sq)
        sq_parts = split(sq)
        inverse = 1.0 / jnp.sum(sq * nrm, axis=1, keepdims=True)
        amem = fine(sq_parts, mem_parts, 1, 0) * inverse
        mixed = jnp.sum(grad_mix * amem, axis=1, keepdims=True)
        term = term + (g * (1.0 - g)) * jnp.sum(mixed, axis=0, keepdims=True)
        term = term - g * jnp.sum(row, axis=1, keepdims=True)
        d_top = split(grad_mix * (g * inverse))
        d_low = -(g * mixed) * inverse
        d_sq = fine(d_top, mem_parts, 1, 1) + d_low * nrm
        dq_ref[rows, :] = (dq + d_sq * slope).astype(bf16)
        m_next = m_next + fine(sq_parts, d_top, 0, 0)
        z_next = z_next + jnp.sum(sq * d_low, axis=0, keepdims=True)
    bias_ref[...] += jnp.broadcast_to(term[None], bias_ref.shape)
    dk_ref[...] = (dk_att[...] * scale).astype(bf16)
    dv_ref[...] = dv_att[...].astype(bf16)

    @pl.when(s + 1 < segs)
    def _():
        dm_now, dz_now = dm[...], dz[...]
        dm_parts = split(dm_now)
        kf = key.astype(f32)
        sk = feature(kf)
        slope = jnp.where(kf > 0, 1.0, sk)
        sk_parts = split(sk)
        inverse = 1.0 / jnp.sum(sk * nrm, axis=1, keepdims=True)
        recall = fine(sk_parts, mem_parts, 1, 0) * inverse
        delta = value.astype(f32) - recall
        d_delta = fine(sk_parts, dm_parts, 1, 0)
        d_top = split(-d_delta * inverse)
        d_low = jnp.sum(d_delta * recall, axis=1, keepdims=True) * inverse
        d_sk = (
            fine(split(delta), dm_parts, 1, 1)
            + dz_now
            + fine(d_top, mem_parts, 1, 1)
            + d_low * nrm
        )
        dk_ref[...] = (dk_att[...] * scale + d_sk * slope).astype(bf16)
        dv_ref[...] = (dv_att[...] + d_delta).astype(bf16)
        dm[...] = dm_now + fine(sk_parts, d_top, 0, 0)
        dz[...] = dz_now + jnp.sum(sk * d_low, axis=0, keepdims=True)

    @pl.when(s > 0)
    def _():
        cut = (resets[jnp.maximum(s - 1, 0)] > 0) | (lax.rem(s, depth[0]) == 0)
        dm[...] = jnp.where(cut, 0.0, dm[...] + m_next)
        dz[...] = jnp.where(cut, 0.0, dz[...] + z_next)


def attention_backward(qkv, grad_attn, gate, resets, depth, lse, mems, nrms, segs):
    total_rows, cols = qkv.shape
    heads, _, hdim, _ = mems.shape
    seg = total_rows // segs
    at = specs(seg, hdim, heads, True, segs)
    smem = pl.BlockSpec(memory_space=pltpu.SMEM)
    grad = jax.ShapeDtypeStruct((total_rows, heads * hdim), bf16)
    return pl.pallas_call(
        functools.partial(backward_kernel, min(256, seg), segs),
        grid=(heads, segs),
        in_specs=[
            smem,
            smem,
            smem,
            at(0),
            at(1),
            at(2),
            at(0),
            pl.BlockSpec((1, 1, 1, seg), lambda h, t: (h, segs - 1 - t, 0, 0)),
            pl.BlockSpec((1, 1, hdim, hdim), lambda h, t: (h, segs - 1 - t, 0, 0)),
            pl.BlockSpec((1, 1, 1, hdim), lambda h, t: (h, segs - 1 - t, 0, 0)),
        ],
        out_specs=[at(0), at(0), at(0), pl.BlockSpec((1, 8, hdim), lambda h, t: (h, 0, 0))],
        out_shape=[grad, grad, grad, jax.ShapeDtypeStruct((heads, 8, hdim), f32)],
        scratch_shapes=[
            pltpu.VMEM((hdim, hdim), f32),
            pltpu.VMEM((1, hdim), f32),
            pltpu.VMEM((seg, hdim), f32),
            pltpu.VMEM((seg, hdim), f32),
        ],
        compiler_params=pltpu.CompilerParams(vmem_limit_bytes=48 << 20),
        cost_estimate=pl.CostEstimate(
            flops=60 * total_rows * seg * heads * hdim // 8,
            bytes_accessed=4 * total_rows * cols,
            transcendentals=total_rows * seg * heads // 2,
        ),
        name="attention_backward",
    )(gate, resets, depth, qkv, qkv, qkv, grad_attn, lse, mems, nrms)


def ring_order(n):
    if n % 4 or n < 8:
        return list(range(n))
    wide = n // 4
    walk = []
    for r in range(4):
        cols = range(1, wide) if r % 2 == 0 else range(wide - 1, 0, -1)
        walk += [r * wide + c for c in cols]
    return walk + [r * wide for r in reversed(range(4))]


def reorder(value, order, axis):
    size = value.shape[axis] // len(order)
    return jnp.concatenate(
        [lax.slice_in_dim(value, i * size, (i + 1) * size, axis=axis) for i in order], axis=axis
    )


def move_blocks(value, order, axis):
    n = len(order)
    block = (value.shape[0] // n, value.shape[1]) if axis == 0 else (value.shape[0], value.shape[1] // n)

    def kernel(order_ref, in_ref, out_ref):
        out_ref[...] = in_ref[...]

    def at(i):
        return (i, 0) if axis == 0 else (0, i)

    return pl.pallas_call(
        kernel,
        grid_spec=pltpu.PrefetchScalarGridSpec(
            num_scalar_prefetch=1,
            grid=(n,),
            in_specs=[pl.BlockSpec(block, lambda i, order_ref: at(order_ref[i]))],
            out_specs=pl.BlockSpec(block, lambda i, order_ref: at(i)),
        ),
        out_shape=jax.ShapeDtypeStruct(value.shape, value.dtype),
        name="move_blocks",
    )(jnp.array(order, jnp.int32), value)


def tie(value, *others):
    return lax.optimization_barrier((value,) + others)[0]


MESH = pl.DeviceIdType.MESH
dma = pltpu.SemaphoreType.DMA


class Axis:
    def __init__(self, name, rows, cols):
        self.name, self.rows, self.cols = name, rows, cols
        self.size = rows * cols

    def at(self, down, right):
        me = lax.axis_index(self.name)
        row, col = me // self.cols, lax.rem(me, self.cols)
        return lax.rem(row + down, self.rows) * self.cols + lax.rem(col + right, self.cols)

    def to(self, down, right):
        return {"device_id": {self.name: self.at(down, right)}, "device_id_type": MESH}


class Gather:
    def __init__(self, axis, block, outer):
        self.axis, self.outer, self.inputs = axis, outer, [block]
        n, self.chunks = axis.size, block.shape[0]
        lead = (n, self.chunks) if outer else (self.chunks, n)
        self.outputs = [jax.ShapeDtypeStruct(lead + block.shape[1:], block.dtype)]
        held, others = max(axis.rows - 1, 1), axis.cols - 1
        row, col = (held, self.chunks), (others, axis.rows, self.chunks)
        self.scratch = [dma((self.chunks,)), dma(row), dma(row), dma(col), dma(col)]
        self.peers = [(k, 0) for k in range(1, axis.rows)] + [(0, j) for j in range(1, axis.cols)]
        self.bytes = block.size * 2

    def bind(self, ins, outs, scratch):
        (self.src,), (self.dst,) = ins, outs
        self.keep, self.row_out, self.row_in, self.col_out, self.col_in = scratch

    def place(self, dev, c):
        return self.dst.at[dev, c] if self.outer else self.dst.at[c, dev]

    def along(self, k, c):
        axis = self.axis
        return pltpu.make_async_remote_copy(
            src_ref=self.src.at[c],
            dst_ref=self.place(axis.at(0, 0), c),
            send_sem=self.row_out.at[k - 1, c],
            recv_sem=self.row_in.at[k - 1, c],
            **axis.to(k, 0),
        )

    def across(self, k, j, c):
        axis = self.axis
        spot = self.place(axis.at((axis.rows - k) % axis.rows, 0), c)
        return pltpu.make_async_remote_copy(
            src_ref=self.src.at[c] if k == 0 else spot,
            dst_ref=spot,
            send_sem=self.col_out.at[j - 1, k, c],
            recv_sem=self.col_in.at[j - 1, k, c],
            **axis.to(0, j),
        )

    def own(self, c):
        return pltpu.make_async_copy(
            self.src.at[c], self.place(self.axis.at(0, 0), c), self.keep.at[c]
        )

    def start(self):
        for c in range(self.chunks):
            for k in range(1, self.axis.rows):
                self.along(k, c).start()
        for c in range(self.chunks):
            for j in range(1, self.axis.cols):
                self.across(0, j, c).start()
            self.own(c).start()

    def middle(self, part, parts):
        for c in range(self.chunks * part // parts, self.chunks * (part + 1) // parts):
            for k in range(1, self.axis.rows):
                self.along(k, c).wait_recv()
                for j in range(1, self.axis.cols):
                    self.across(k, j, c).start()

    def finish(self):
        for c in range(self.chunks):
            for k in range(1, self.axis.rows):
                self.along(k, c).wait_send()
            for k in range(self.axis.rows):
                for j in range(1, self.axis.cols):
                    self.across(k, j, c).wait()
            self.own(c).wait()


class Exchange:
    def __init__(self, axis, array, shape, source, target):
        self.axis, self.inputs = axis, [array]
        self.outputs = [jax.ShapeDtypeStruct(shape, array.dtype)]
        self.source, self.target = source, target
        n = axis.size
        self.scratch = [dma, dma((n - 1,)), dma((n - 1,))]
        self.peers = [(k, j) for k in range(axis.rows) for j in range(axis.cols)][1:]
        self.bytes = array.size

    def bind(self, ins, outs, scratch):
        (self.src,), (self.dst,) = ins, outs
        self.keep, self.out_sem, self.in_sem = scratch

    def copy(self, i):
        axis, (k, j) = self.axis, self.peers[i]
        return pltpu.make_async_remote_copy(
            src_ref=self.source(self.src, axis.at(k, j)),
            dst_ref=self.target(self.dst, axis.at(0, 0)),
            send_sem=self.out_sem.at[i],
            recv_sem=self.in_sem.at[i],
            **axis.to(k, j),
        )

    def own(self):
        me = self.axis.at(0, 0)
        return pltpu.make_async_copy(self.source(self.src, me), self.target(self.dst, me), self.keep)

    def start(self):
        self.own().start()
        for i in reversed(range(len(self.peers))):
            self.copy(i).start()

    def middle(self, part, parts):
        pass

    def finish(self):
        for i in reversed(range(len(self.peers))):
            self.copy(i).wait()
        self.own().wait()


class Scatter:
    def __init__(self, axis, parts, outer, dtype, ahead=None):
        self.axis, self.outer, self.dtype, self.inputs = axis, outer, dtype, [parts]
        self.chunks = parts.shape[1 if outer else 0]
        block = (self.chunks,) + parts.shape[2:]
        self.outputs = [jax.ShapeDtypeStruct(block, dtype)]
        rows, others, held = axis.rows, axis.cols - 1, max(axis.rows - 1, 1)
        row, col = (held, self.chunks), (others, rows, self.chunks)
        self.scratch = [
            pltpu.VMEM((rows,) + block, bf16),
            pltpu.VMEM((others, rows) + block, bf16),
            pltpu.VMEM((held,) + block, bf16),
            pltpu.VMEM((held,) + block, bf16),
            pltpu.VMEM(block, dtype),
            dma((rows, self.chunks)),
            dma(col),
            dma(col),
            dma(row),
            dma(row),
            dma((self.chunks,)),
        ]
        self.peers = [(k, 0) for k in range(1, rows)] + [(0, j) for j in range(1, axis.cols)]
        self.order = [(k, c) for k in list(range(1, rows)) + [0] for c in range(self.chunks)]
        self.ahead = min(ahead or len(self.order), len(self.order))
        self.bytes = parts.size // axis.size * 2

    def bind(self, ins, outs, scratch):
        (self.src,), (self.dst,) = ins, outs
        self.mine, self.met, self.sent, self.come, self.result = scratch[:5]
        self.load, self.col_out, self.col_in, self.row_out, self.row_in, self.store = scratch[5:]

    def terms(self, dev, c):
        return self.src.at[dev, c] if self.outer else self.src.at[c, dev]

    def read(self, k, c):
        return pltpu.make_async_copy(
            self.terms(self.axis.at(k, 0), c), self.mine.at[k, c], self.load.at[k, c]
        )

    def across(self, k, j, c):
        return pltpu.make_async_remote_copy(
            src_ref=self.terms(self.axis.at(k, j), c),
            dst_ref=self.met.at[j - 1, k, c],
            send_sem=self.col_out.at[j - 1, k, c],
            recv_sem=self.col_in.at[j - 1, k, c],
            **self.axis.to(0, j),
        )

    def along(self, k, c):
        return pltpu.make_async_remote_copy(
            src_ref=self.sent.at[k - 1, c],
            dst_ref=self.come.at[k - 1, c],
            send_sem=self.row_out.at[k - 1, c],
            recv_sem=self.row_in.at[k - 1, c],
            **self.axis.to(k, 0),
        )

    def write(self, c):
        return pltpu.make_async_copy(self.result.at[c], self.dst.at[c], self.store.at[c])

    def leave(self, i):
        if i < len(self.order):
            k, c = self.order[i]
            for j in range(1, self.axis.cols):
                self.across(k, j, c).start()

    def meet(self, k, c):
        self.read(k, c).wait()
        total = self.mine[k, c].astype(f32)
        for j in range(1, self.axis.cols):
            self.across(k, j, c).wait_recv()
            total = total + self.met[j - 1, k, c].astype(f32)
        self.leave(self.order.index((k, c)) + self.ahead)
        return total

    def start(self):
        for i, (k, c) in enumerate(self.order):
            if i < self.ahead:
                self.leave(i)
            self.read(k, c).start()

    def middle(self, part, parts):
        steps = [step for step in self.order if step[0]]
        for k, c in steps[len(steps) * part // parts : len(steps) * (part + 1) // parts]:
            self.sent[k - 1, c] = self.meet(k, c).astype(bf16)
            self.along(k, c).start()

    def finish(self):
        for c in range(self.chunks):
            total = self.meet(0, c)
            for k in range(1, self.axis.rows):
                self.along(k, c).wait_recv()
                total = total + self.come[k - 1, c].astype(f32)
            self.result[c] = total.astype(self.dtype)
            self.write(c).start()
        for k, c in self.order:
            for j in range(1, self.axis.cols):
                self.across(k, j, c).wait_send()
            if k:
                self.along(k, c).wait_send()
        for c in range(self.chunks):
            self.write(c).wait()


class Product:
    def __init__(self, pairs, over, tiles, rows=None):
        self.inputs, self.over = [matrix for pair in pairs for matrix in pair], over
        left, right = pairs[0]
        self.depth, n = left.shape[over[0]], right.shape[1 - over[1]]
        first, m = rows or (0, left.shape[1 - over[0]])
        self.outputs = [jax.ShapeDtypeStruct((m, n), bf16)]
        self.tm, self.tn = min(tiles[0], m), min(tiles[1], n)
        self.grid, self.skip = (m // self.tm, n // self.tn), first // self.tm
        self.scratch, self.peers, self.bytes = [], [], 0

    def bind(self, ins, outs, scratch):
        self.refs = (*ins, *outs)

    def start(self):
        pass

    def middle(self, part, parts):
        pass

    def finish(self):
        pass

    def compute(self):
        def body(*refs):
            total = contract(refs[0][...], refs[1][...], *self.over)
            for i in range(2, len(refs) - 1, 2):
                total = total + contract(refs[i][...], refs[i + 1][...], *self.over)
            refs[-1][...] = total.astype(bf16)

        def tile(size, over, index):
            def at(i, j):
                return (i + self.skip, j)[index]

            if over == 0:
                return pl.BlockSpec((self.depth, size), lambda i, j: (0, at(i, j)))
            return pl.BlockSpec((size, self.depth), lambda i, j: (at(i, j), 0))

        pair = [tile(self.tm, self.over[0], 0), tile(self.tn, self.over[1], 1)]
        pltpu.emit_pipeline(
            body,
            grid=self.grid,
            in_specs=pair * (len(self.inputs) // 2),
            out_specs=[pl.BlockSpec((self.tm, self.tn), lambda i, j: (i, j))],
        )(*self.refs)


class Net:
    def __init__(self, n_seq, n_fsdp):
        rows = 4 if n_fsdp % 4 == 0 else 1
        self.seq = Axis("seq", n_seq // 2, 2)
        self.fsdp = Axis("fsdp", rows, n_fsdp // rows)
        self.calls = 0

    def run(self, jobs, room=32):
        self.calls += 1
        ins = [array for job in jobs for array in job.inputs]
        outs = [shape for job in jobs for shape in job.outputs]
        scratch = [one for job in jobs for one in job.scratch]
        peers = []
        for job in jobs:
            for peer in job.peers:
                if (job.axis, peer) not in peers:
                    peers.append((job.axis, peer))

        def kernel(*refs):
            at = [0, len(ins), len(ins) + len(outs)]
            for job in jobs:
                taken = []
                for part, count in enumerate(
                    (len(job.inputs), len(job.outputs), len(job.scratch))
                ):
                    taken.append(refs[at[part] : at[part] + count])
                    at[part] += count
                job.bind(*taken)
            barrier = pltpu.get_barrier_semaphore()
            for axis, peer in peers:
                pl.semaphore_signal(barrier, inc=1, **axis.to(*peer))
            pl.semaphore_wait(barrier, len(peers))
            for job in jobs:
                job.start()
            products = [job for job in jobs if not job.peers]
            late = [job for job in jobs if products and isinstance(job, Gather)]
            parts = 4
            for some in ([job for job in jobs if job not in late], late):
                for part in range(parts):
                    for job in some:
                        job.middle(part, parts)
                if some is not late:
                    for job in products:
                        job.compute()
            for job in jobs:
                job.finish()

        anywhere = pl.BlockSpec(memory_space=pl.ANY)
        return pl.pallas_call(
            kernel,
            in_specs=[anywhere] * len(ins),
            out_specs=[anywhere] * len(outs),
            out_shape=outs,
            scratch_shapes=scratch,
            compiler_params=pltpu.CompilerParams(
                collective_id=self.calls, has_side_effects=True, vmem_limit_bytes=room << 20
            ),
            cost_estimate=pl.CostEstimate(
                flops=0, bytes_accessed=12 * max(job.bytes for job in jobs), transcendentals=0
            ),
            name="net",
        )(*ins)


def own_columns(weight, me, groups, order, each):
    shard, count = weight.shape[0], len(order)
    per = weight.shape[1] // (groups * count * each)
    if each % 128:
        cut = weight.reshape(shard, groups, count, per, each)
        cut = lax.dynamic_index_in_dim(cut, me, 3, keepdims=False)
        return [reorder(cut[:, g], order, 1).reshape(shard, count * each) for g in range(groups)]

    def kernel(me_ref, order_ref, *refs):
        for g in range(groups):
            refs[groups + g][...] = refs[g][...]

    def source(g):
        def at(i, me_ref, order_ref):
            return 0, (g * count + order_ref[i]) * per + me_ref[0]

        return pl.BlockSpec((shard, each), at)

    return pl.pallas_call(
        kernel,
        grid_spec=pltpu.PrefetchScalarGridSpec(
            num_scalar_prefetch=2,
            grid=(count,),
            in_specs=[source(g) for g in range(groups)],
            out_specs=[pl.BlockSpec((shard, each), lambda i, *refs: (0, i))] * groups,
        ),
        out_shape=[jax.ShapeDtypeStruct((shard, count * each), weight.dtype)] * groups,
        name="own_columns",
    )(me.reshape(1), jnp.array(order, jnp.int32), *([weight] * groups))


def spread_columns(arrays, groups, group, order, each, block_rows):
    devices, rows, _ = arrays[0].shape
    wide, count = devices * each, len(order)

    def kernel(order_ref, in_ref, *refs):
        for j in range(devices):
            refs[-1][:, j * each : (j + 1) * each] = in_ref[j].astype(f32)

    return pl.pallas_call(
        kernel,
        grid_spec=pltpu.PrefetchScalarGridSpec(
            num_scalar_prefetch=1,
            grid=(count, rows // block_rows),
            in_specs=[
                pl.BlockSpec((devices, block_rows, each), lambda i, r, order_ref: (0, r, i))
            ]
            + [pl.BlockSpec(memory_space=pl.ANY)] * (len(arrays) - 1),
            out_specs=pl.BlockSpec(
                (block_rows, wide), lambda i, r, order_ref: (r, group * count + order_ref[i])
            ),
        ),
        out_shape=jax.ShapeDtypeStruct((rows, groups * count * wide), f32),
        input_output_aliases={2: 0} if len(arrays) > 1 else {},
        name="spread_columns",
    )(jnp.array(order, jnp.int32), *arrays)


def mm(left, right):
    return jnp.dot(left, right, preferred_element_type=f32)


def mm_nt(left, right):
    return lax.dot_general(left, right, (((1,), (1,)), ((), ())), preferred_element_type=f32)


def mm_tn(left, right):
    return lax.dot_general(left, right, (((0,), (0,)), ((), ())), preferred_element_type=f32)


def make_body(n_seq, n_fsdp):
    def body(
        tokens,
        cotangent,
        w_qkv,
        w_out,
        w_gate_up,
        w_down,
        gain_attn,
        gain_ffn,
        gate_bias,
        memory_in,
        norms_in,
        resets,
        depth,
    ):
        _, segs, local, width = tokens.shape
        heads = gate_bias.shape[0]
        hdim = width // heads
        my_heads = heads // n_seq
        my_width = width // n_seq
        seg = local * n_seq
        rows = segs * local
        total_rows = segs * seg
        shard = w_qkv.shape[0]
        hidden_shard = w_down.shape[0]
        my_hidden = hidden_shard // n_seq
        out_rows = shard // n_seq
        net = Net(n_seq, n_fsdp)
        me = lax.axis_index("seq")

        ring = ring_order(n_fsdp)
        back = [ring.index(i) for i in range(n_fsdp)]
        (qkv_own,) = own_columns(w_qkv, me, 1, range(3), my_width)
        gate_own, up_own = own_columns(w_gate_up, me, 2, ring, my_hidden)
        down_own = lax.dynamic_slice(w_down, (me * my_hidden, 0), (my_hidden, width))
        out_own = lax.dynamic_slice(w_out, (me * out_rows, 0), (out_rows, width))

        x_flat = tokens.reshape(rows, width).astype(f32)
        r_one = rms(x_flat)
        h_one_own = reorder((r_one * gain_attn).astype(bf16), ring, 1)
        grad_y = cotangent.reshape(rows, width)

        def gather_rows(block):
            return lax.all_gather(block, "fsdp", axis=0, tiled=True, axis_index_groups=[ring])

        def token_parts(value):
            return value.reshape(segs, n_seq, local, width)

        def gather_own(value):
            return Gather(net.seq, value.reshape(segs, local, width), False)

        w_o = gather_rows(tie(out_own, h_one_own))
        w_q = gather_rows(tie(qkv_own, h_one_own))
        (h_one,) = net.run([gather_own(h_one_own)])
        h_one = h_one.reshape(total_rows, width)
        w_g = gather_rows(tie(gate_own, h_one))
        w_o = move_blocks(tie(w_o, h_one), back, 0)
        (whole_o,) = net.run([Gather(net.seq, w_o.reshape(n_fsdp, out_rows, width), False)])
        whole_o = whole_o.reshape(width, width)
        w_u = gather_rows(tie(up_own, whole_o))

        qkv = mm(h_one, w_q).astype(bf16)
        gate = jax.nn.sigmoid(lax.dynamic_slice(gate_bias, (me * my_heads,), (my_heads,)))
        memory = lax.dynamic_slice(memory_in[0], (me * my_heads, 0, 0), (my_heads, hdim, hdim))
        norms = lax.dynamic_slice(norms_in[0], (me * my_heads, 0), (my_heads, hdim))
        attn_heads, lse, mems, nrms = attention_forward(qkv, gate, resets[0], memory, norms, segs)

        half = width // 2
        w_d = gather_rows(tie(down_own, attn_heads))

        def columns_of(ref, i):
            return ref.at[:, :, pl.ds(pl.multiple_of(i * my_width, my_width), my_width)]

        def tokens_of(ref, i):
            return ref.at[:, i]

        (attn,) = net.run(
            [
                Exchange(
                    net.seq,
                    attn_heads.reshape(segs, n_seq, local, my_width),
                    (segs, local, width),
                    tokens_of,
                    columns_of,
                ),
            ]
        )
        attn = attn.reshape(rows, width)
        x_one = x_flat + mm(attn, whole_o)
        r_two = rms(x_one)
        h_two_own = reorder((r_two * gain_ffn).astype(bf16), ring, 1)
        (h_two,) = net.run([gather_own(h_two_own)])
        h_two = h_two.reshape(total_rows, width)
        grad_y_all, gate_part = net.run(
            [gather_own(tie(grad_y, h_two)), Product([(h_two, w_g)], (1, 0), (1024, 512))], 56
        )
        grad_y_all = grad_y_all.reshape(total_rows, width)
        up_part = mm(h_two, w_u).astype(bf16)
        hidden = swiglu(gate_part.astype(f32), up_part.astype(f32)).astype(bf16)

        def scatter_rows(parts):
            return lax.psum_scatter(
                parts, "fsdp", scatter_dimension=0, tiled=True, axis_index_groups=[ring]
            )

        down_parts = mm_tn(hidden, grad_y_all).astype(bf16)
        down_term = scatter_rows(down_parts)
        grad_hidden = mm_nt(tie(grad_y_all, down_parts), w_d)
        _, swiglu_back = jax.vjp(swiglu, gate_part.astype(f32), up_part.astype(f32))
        grad_gate, grad_up = swiglu_back(grad_hidden)
        grad_gate, grad_up = grad_gate.astype(bf16), grad_up.astype(bf16)

        def output_terms(s):
            return Product([(hidden, w_d)], (1, 0), (512, 512), (s * seg, seg))

        def h_two_terms(s):
            pairs = [(grad_gate, w_g), (grad_up, w_u)]
            return Product(pairs, (1, 1), (512, 512), (s * seg, seg))

        gate_product = Product([(h_two, grad_gate)], (0, 0), (1024, 512))
        up_product = Product([(h_two, grad_up)], (0, 0), (1024, 512))
        beside = [[output_terms(s)] for s in range(1, segs)]
        beside += [[h_two_terms(s)] for s in range(segs)] + [[up_product]]
        beside[0].append(gate_product)
        terms = mm(hidden[:seg], tie(w_d, grad_up)).astype(bf16)
        sums, gate_parts = [], None
        for products in beside:
            parts = terms.reshape(n_seq, 2, local // 2, width)
            results = net.run([Scatter(net.seq, parts, True, f32)] + products, 56)
            sums.append(results[0])
            terms = results[1]
            if products[-1] is gate_product:
                gate_parts = results[-1]
                gate_term = scatter_rows(gate_parts)
        up_parts = terms
        up_term = scatter_rows(up_parts)
        output = jnp.stack(sums[:segs]).reshape(rows, width)
        grad_h_two = reorder(jnp.stack(sums[segs:]).reshape(rows, width), back, 1)

        gain_ffn_term = jnp.sum(grad_h_two * r_two, axis=0)
        _, norm_two_back = jax.vjp(rms, x_one)
        grad_x_one = grad_y.astype(f32) + norm_two_back(grad_h_two * gain_ffn)[0]
        grad_o = grad_x_one.astype(bf16)

        grad_attn_parts = mm_nt(grad_o, whole_o).astype(bf16)
        grad_attn, out_parts = net.run(
            [
                Exchange(
                    net.seq,
                    grad_attn_parts.reshape(segs, local, width),
                    (segs, n_seq, local, my_width),
                    columns_of,
                    tokens_of,
                ),
                Product([(attn, grad_o)], (0, 0), (1024, 512)),
            ],
            56,
        )
        grad_attn = tie(grad_attn.reshape(total_rows, my_width), down_term)
        grads_q, grads_k, grads_v, bias_terms = attention_backward(
            qkv, grad_attn, gate, resets[0], depth, lse, mems, nrms, segs
        )
        grad_qkv_rows = jnp.concatenate([grads_q, grads_k, grads_v], axis=1)
        out_parts = tie(out_parts, gate_term)
        out_sum, qkv_parts, grad_h_one = net.run(
            [
                Scatter(net.seq, out_parts.reshape(n_fsdp, n_seq, out_rows, width), False, bf16),
                Product([(h_one, grad_qkv_rows)], (0, 0), (1024, 512)),
                Product([(grad_qkv_rows, w_q)], (1, 1), (1024, 512)),
            ],
            56,
        )
        qkv_term = scatter_rows(qkv_parts)
        grad_h_one, out_term, down_all, gate_all = net.run(
            [
                Scatter(net.seq, token_parts(tie(grad_h_one, up_term)), False, f32),
                Scatter(net.fsdp, out_sum[:, None], True, bf16, 2),
                Gather(net.seq, down_term[None], True),
                Gather(net.seq, gate_term[None], True),
            ],
            56,
        )
        grad_h_one = move_blocks(grad_h_one.reshape(rows, width), back, 1)
        output = (x_one + output).astype(bf16).reshape(tokens.shape)
        gain_attn_term = jnp.sum(grad_h_one * r_one, axis=0)
        _, norm_one_back = jax.vjp(rms, x_flat)
        grad_x = grad_x_one + norm_one_back(grad_h_one * gain_attn)[0]
        input_grad = grad_x.astype(bf16).reshape(tokens.shape)

        bias_all = lax.dynamic_update_slice(
            jnp.zeros((heads,), f32), bias_terms[:, 0, 0], (me * my_heads,)
        )
        small = jnp.concatenate([gain_attn_term, gain_ffn_term, bias_all])
        wide = -(-small.shape[0] // 1024) * 128
        small = jnp.pad(small, (0, 8 * wide - small.shape[0])).reshape(1, 8, wide)

        down_all = down_all.reshape(hidden_shard, width).astype(f32)
        aligned = my_hidden % 128 == 0
        gate_up_all = gate_all[:, 0]
        if aligned:
            gate_up_all = spread_columns([gate_up_all], 2, 0, ring, my_hidden, shard)
        up_all = lax.all_gather(tie(up_term, grad_h_one), "seq", axis=0)
        qkv_all = lax.all_gather(tie(qkv_term, grad_h_one), "seq", axis=0)
        small, out_all = net.run([Gather(net.fsdp, small, True), Gather(net.seq, out_term, True)])
        (small,) = net.run([Gather(net.seq, jnp.sum(small, axis=0), True)])
        small = jnp.sum(small, axis=0).reshape(-1)
        out_all = out_all.reshape(shard, width).astype(f32)
        done = (down_all, gate_up_all, output, input_grad, small, out_all)
        qkv_all = tie(qkv_all, *done)
        up_all = tie(up_all, *done)
        qkv_all = spread_columns([qkv_all], 1, 0, range(3), my_width, shard // 2)
        if aligned:
            gate_up_all = spread_columns([up_all, gate_up_all], 2, 1, ring, my_hidden, shard)
        else:
            cut = jnp.stack([gate_up_all, up_all]).reshape(2, n_seq, shard, n_fsdp, my_hidden)
            cut = reorder(cut, back, 3)
            gate_up_all = jnp.transpose(cut, (2, 0, 3, 1, 4)).reshape(shard, -1).astype(f32)

        return (
            output,
            input_grad,
            qkv_all,
            out_all,
            gate_up_all,
            down_all,
            small[:width],
            small[width : 2 * width],
            small[2 * width : 2 * width + heads],
        )

    return body


def solution(mesh):
    rows = P("fsdp", None)
    tokens = P("fsdp", None, "seq", None)
    body = make_body(mesh.shape["seq"], mesh.shape["fsdp"])
    return jax.shard_map(
        body,
        mesh=mesh,
        in_specs=(
            tokens,
            tokens,
            rows,
            rows,
            rows,
            rows,
            P(),
            P(),
            P(),
            P("fsdp", None, None, None),
            P("fsdp", None, None),
            rows,
            P("fsdp"),
        ),
        out_specs=(tokens, tokens, rows, rows, rows, rows, P(), P(), P()),
        check_vma=False,
    )
```

```python
import functools

import jax
import jax.numpy as jnp
from jax import lax
from jax.experimental import pallas as pl
from jax.experimental.pallas import tpu as pltpu
from jax.sharding import PartitionSpec as P

norm_eps = 1e-05
bf16 = jnp.bfloat16
f32 = jnp.float32


def rms(value_rows_segment):
    return value_rows_segment * lax.rsqrt(
        jnp.mean(value_rows_segment * value_rows_segment, axis=-1, keepdims=True) + norm_eps
    )


def swiglu(gate_part, up_part):
    return jax.nn.silu(gate_part) * up_part


def feature(value_rows_segment):
    return jnp.where(
        value_rows_segment > 0,
        value_rows_segment + 1.0,
        jnp.exp(jnp.minimum(value_rows_segment, 0.0)),
    )


def contract(left, right, left_dim, right_dim):
    return lax.dot_general(
        left, right, (((left_dim,), (right_dim,)), ((), ())), preferred_element_type=f32
    )


def split(value):
    high = value.astype(bf16)
    return high, (value - high.astype(f32)).astype(bf16)


def fine(left, right, left_dim, right_dim):
    lh, ll = left
    rh, rl = right
    return (
        contract(lh, rl, left_dim, right_dim)
        + contract(ll, rh, left_dim, right_dim)
        + contract(lh, rh, left_dim, right_dim)
    )


LOG2E = 1.4426950408889634


def scores_of(key, query, block, i):
    n = (i + 1) * block
    sc = contract(key[:n], query, 1, 1)
    rows = lax.broadcasted_iota(jnp.int32, (block, block), 0)
    cols = lax.broadcasted_iota(jnp.int32, (block, block), 1)
    last = jnp.where(rows <= cols, sc[n - block :], -1e30)
    if i == 0:
        return last
    return jnp.concatenate([sc[: n - block], last], axis=0)


def forward_kernel(
    block, segs, gate, resets, q_ref, k_ref, v_ref, m_ref, z_ref, a_ref, lse_ref, mem_ref, nrm_ref, mem, nrm
):
    h, s = pl.program_id(0), pl.program_id(1)
    seg, hdim = q_ref.shape
    scale = LOG2E / hdim**0.5

    @pl.when(s == 0)
    def _():
        mem[...] = m_ref[0]
        nrm[...] = z_ref[0]

    @pl.when(s > 0)
    def _():
        @pl.when(resets[jnp.maximum(s - 1, 0)] > 0)
        def _():
            mem[...] = jnp.zeros_like(mem)
            nrm[...] = jnp.ones_like(nrm)

    mem_ref[0, 0] = mem[...]
    nrm_ref[0, 0] = nrm[...]
    g = gate[h]
    mem_parts = split(mem[...])
    key, value = k_ref[...], v_ref[...]
    value_t = value.T
    for i in range(seg // block):
        rows = slice(i * block, (i + 1) * block)
        query = q_ref[rows, :]
        sc = scores_of(key, query, block, i)
        top = jnp.max(sc, axis=0, keepdims=True)
        weights = jnp.exp2((sc - top) * scale)
        total = jnp.sum(weights, axis=0, keepdims=True)
        lse_ref[0, 0, :, rows] = top * scale + jnp.log2(total)
        adot_t = contract(value_t[:, : (i + 1) * block], weights.astype(bf16), 1, 0)
        adot_t = adot_t * ((1.0 - g) / total)
        sq = feature(query.astype(f32))
        amem = fine(split(sq), mem_parts, 1, 0) * (
            g / jnp.sum(sq * nrm[...], axis=1, keepdims=True)
        )
        a_ref[rows, :] = (amem + adot_t.T).astype(bf16)

    @pl.when(s + 1 < segs)
    def _():
        sk = feature(key.astype(f32))
        sk_parts = split(sk)
        recall = fine(sk_parts, mem_parts, 1, 0) / jnp.sum(sk * nrm[...], axis=1, keepdims=True)
        delta = split(value.astype(f32) - recall)
        mem[...] = mem[...] + fine(sk_parts, delta, 0, 0)
        nrm[...] = nrm[...] + jnp.sum(sk, axis=0, keepdims=True)


def specs(seg, hdim, heads, back, segs):
    def at(part):
        return pl.BlockSpec(
            (seg, hdim), lambda h, t: ((segs - 1 - t) if back else t, part * heads + h)
        )

    return at


def attention_forward(qkv, gate, resets, memory, norms, segs):
    total_rows, cols = qkv.shape
    heads, hdim, _ = memory.shape
    seg = total_rows // segs
    at = specs(seg, hdim, heads, False, segs)
    return pl.pallas_call(
        functools.partial(forward_kernel, min(256, seg), segs),
        grid=(heads, segs),
        in_specs=[
            pl.BlockSpec(memory_space=pltpu.SMEM),
            pl.BlockSpec(memory_space=pltpu.SMEM),
            at(0),
            at(1),
            at(2),
            pl.BlockSpec((1, hdim, hdim), lambda h, t: (h, 0, 0)),
            pl.BlockSpec((1, 1, hdim), lambda h, t: (h, 0, 0)),
        ],
        out_specs=[
            at(0),
            pl.BlockSpec((1, 1, 1, seg), lambda h, t: (h, t, 0, 0)),
            pl.BlockSpec((1, 1, hdim, hdim), lambda h, t: (h, t, 0, 0)),
            pl.BlockSpec((1, 1, 1, hdim), lambda h, t: (h, t, 0, 0)),
        ],
        out_shape=[
            jax.ShapeDtypeStruct((total_rows, heads * hdim), bf16),
            jax.ShapeDtypeStruct((heads, segs, 1, seg), f32),
            jax.ShapeDtypeStruct((heads, segs, hdim, hdim), f32),
            jax.ShapeDtypeStruct((heads, segs, 1, hdim), f32),
        ],
        scratch_shapes=[pltpu.VMEM((hdim, hdim), f32), pltpu.VMEM((1, hdim), f32)],
        compiler_params=pltpu.CompilerParams(vmem_limit_bytes=48 << 20),
        cost_estimate=pl.CostEstimate(
            flops=30 * total_rows * seg * heads * hdim // 8,
            bytes_accessed=4 * total_rows * cols,
            transcendentals=total_rows * seg * heads // 2,
        ),
        name="attention_forward",
    )(gate, resets, qkv, qkv, qkv, memory, norms.reshape(heads, 1, hdim))


def backward_kernel(
    block, segs, gate, resets, depth, q_ref, k_ref, v_ref, da_ref, lse_ref, mem_ref, nrm_ref,
    dq_ref, dk_ref, dv_ref, bias_ref, dm, dz, dk_att, dv_att,
):
    h, t = pl.program_id(0), pl.program_id(1)
    s = segs - 1 - t
    seg, hdim = q_ref.shape
    scale = 1.0 / hdim**0.5
    g = gate[h]

    @pl.when(t == 0)
    def _():
        dm[...] = jnp.zeros_like(dm)
        dz[...] = jnp.zeros_like(dz)
        bias_ref[...] = jnp.zeros_like(bias_ref)

    dk_att[...] = jnp.zeros_like(dk_att)
    dv_att[...] = jnp.zeros_like(dv_att)
    mem, nrm = mem_ref[0, 0], nrm_ref[0, 0]
    mem_parts = split(mem)
    key, value = k_ref[...], v_ref[...]
    key_t = key.T
    term = jnp.zeros((1, 1), f32)
    m_next = jnp.zeros((hdim, hdim), f32)
    z_next = jnp.zeros((1, hdim), f32)
    for i in range(seg // block):
        n = (i + 1) * block
        rows = slice(i * block, n)
        query = q_ref[rows, :]
        sc = scores_of(key, query, block, i)
        probs = jnp.exp2(sc * (scale * LOG2E) - lse_ref[0, 0, :, rows])
        grad_mix = da_ref[rows, :].astype(f32)
        grad_adot = ((1.0 - g) * grad_mix).astype(bf16)
        grad_p = contract(value[:n], grad_adot, 1, 1)
        row = jnp.sum(probs * grad_p, axis=0, keepdims=True)
        grad_s = (probs * (grad_p - row)).astype(bf16)
        dk_att[:n, :] += contract(grad_s, query, 1, 0)
        dv_att[:n, :] += contract(probs.astype(bf16), grad_adot, 1, 0)
        dq = contract(key_t[:, :n], grad_s, 1, 0).T * scale

        qf = query.astype(f32)
        sq = feature(qf)
        slope = jnp.where(qf > 0, 1.0, sq)
        sq_parts = split(sq)
        inverse = 1.0 / jnp.sum(sq * nrm, axis=1, keepdims=True)
        amem = fine(sq_parts, mem_parts, 1, 0) * inverse
        mixed = jnp.sum(grad_mix * amem, axis=1, keepdims=True)
        term = term + (g * (1.0 - g)) * jnp.sum(mixed, axis=0, keepdims=True)
        term = term - g * jnp.sum(row, axis=1, keepdims=True)
        d_top = split(grad_mix * (g * inverse))
        d_low = -(g * mixed) * inverse
        d_sq = fine(d_top, mem_parts, 1, 1) + d_low * nrm
        dq_ref[rows, :] = (dq + d_sq * slope).astype(bf16)
        m_next = m_next + fine(sq_parts, d_top, 0, 0)
        z_next = z_next + jnp.sum(sq * d_low, axis=0, keepdims=True)
    bias_ref[...] += jnp.broadcast_to(term[None], bias_ref.shape)
    dk_ref[...] = (dk_att[...] * scale).astype(bf16)
    dv_ref[...] = dv_att[...].astype(bf16)

    @pl.when(s + 1 < segs)
    def _():
        dm_now, dz_now = dm[...], dz[...]
        dm_parts = split(dm_now)
        kf = key.astype(f32)
        sk = feature(kf)
        slope = jnp.where(kf > 0, 1.0, sk)
        sk_parts = split(sk)
        inverse = 1.0 / jnp.sum(sk * nrm, axis=1, keepdims=True)
        recall = fine(sk_parts, mem_parts, 1, 0) * inverse
        delta = value.astype(f32) - recall
        d_delta = fine(sk_parts, dm_parts, 1, 0)
        d_top = split(-d_delta * inverse)
        d_low = jnp.sum(d_delta * recall, axis=1, keepdims=True) * inverse
        d_sk = (
            fine(split(delta), dm_parts, 1, 1)
            + dz_now
            + fine(d_top, mem_parts, 1, 1)
            + d_low * nrm
        )
        dk_ref[...] = (dk_att[...] * scale + d_sk * slope).astype(bf16)
        dv_ref[...] = (dv_att[...] + d_delta).astype(bf16)
        dm[...] = dm_now + fine(sk_parts, d_top, 0, 0)
        dz[...] = dz_now + jnp.sum(sk * d_low, axis=0, keepdims=True)

    @pl.when(s > 0)
    def _():
        cut = (resets[jnp.maximum(s - 1, 0)] > 0) | (lax.rem(s, depth[0]) == 0)
        dm[...] = jnp.where(cut, 0.0, dm[...] + m_next)
        dz[...] = jnp.where(cut, 0.0, dz[...] + z_next)


def attention_backward(qkv, grad_attn, gate, resets, depth, lse, mems, nrms, segs):
    total_rows, cols = qkv.shape
    heads, _, hdim, _ = mems.shape
    seg = total_rows // segs
    at = specs(seg, hdim, heads, True, segs)
    smem = pl.BlockSpec(memory_space=pltpu.SMEM)
    grad = jax.ShapeDtypeStruct((total_rows, heads * hdim), bf16)
    return pl.pallas_call(
        functools.partial(backward_kernel, min(256, seg), segs),
        grid=(heads, segs),
        in_specs=[
            smem,
            smem,
            smem,
            at(0),
            at(1),
            at(2),
            at(0),
            pl.BlockSpec((1, 1, 1, seg), lambda h, t: (h, segs - 1 - t, 0, 0)),
            pl.BlockSpec((1, 1, hdim, hdim), lambda h, t: (h, segs - 1 - t, 0, 0)),
            pl.BlockSpec((1, 1, 1, hdim), lambda h, t: (h, segs - 1 - t, 0, 0)),
        ],
        out_specs=[at(0), at(0), at(0), pl.BlockSpec((1, 8, hdim), lambda h, t: (h, 0, 0))],
        out_shape=[grad, grad, grad, jax.ShapeDtypeStruct((heads, 8, hdim), f32)],
        scratch_shapes=[
            pltpu.VMEM((hdim, hdim), f32),
            pltpu.VMEM((1, hdim), f32),
            pltpu.VMEM((seg, hdim), f32),
            pltpu.VMEM((seg, hdim), f32),
        ],
        compiler_params=pltpu.CompilerParams(vmem_limit_bytes=48 << 20),
        cost_estimate=pl.CostEstimate(
            flops=60 * total_rows * seg * heads * hdim // 8,
            bytes_accessed=4 * total_rows * cols,
            transcendentals=total_rows * seg * heads // 2,
        ),
        name="attention_backward",
    )(gate, resets, depth, qkv, qkv, qkv, grad_attn, lse, mems, nrms)


def ring_order(n):
    if n % 4 or n < 8:
        return list(range(n))
    wide = n // 4
    walk = []
    for r in range(4):
        cols = range(1, wide) if r % 2 == 0 else range(wide - 1, 0, -1)
        walk += [r * wide + c for c in cols]
    return walk + [r * wide for r in reversed(range(4))]


def reorder(value, order, axis):
    size = value.shape[axis] // len(order)
    return jnp.concatenate(
        [lax.slice_in_dim(value, i * size, (i + 1) * size, axis=axis) for i in order], axis=axis
    )


def move_blocks(value, order, axis):
    n = len(order)
    block = (value.shape[0] // n, value.shape[1]) if axis == 0 else (value.shape[0], value.shape[1] // n)

    def kernel(order_ref, in_ref, out_ref):
        out_ref[...] = in_ref[...]

    def at(i):
        return (i, 0) if axis == 0 else (0, i)

    return pl.pallas_call(
        kernel,
        grid_spec=pltpu.PrefetchScalarGridSpec(
            num_scalar_prefetch=1,
            grid=(n,),
            in_specs=[pl.BlockSpec(block, lambda i, order_ref: at(order_ref[i]))],
            out_specs=pl.BlockSpec(block, lambda i, order_ref: at(i)),
        ),
        out_shape=jax.ShapeDtypeStruct(value.shape, value.dtype),
        name="move_blocks",
    )(jnp.array(order, jnp.int32), value)


def tie(value, *others):
    return lax.optimization_barrier((value,) + others)[0]


MESH = pl.DeviceIdType.MESH
dma = pltpu.SemaphoreType.DMA


class Axis:
    def __init__(self, name, rows, cols):
        self.name, self.rows, self.cols = name, rows, cols
        self.size = rows * cols

    def at(self, down, right):
        me = lax.axis_index(self.name)
        row, col = me // self.cols, lax.rem(me, self.cols)
        return lax.rem(row + down, self.rows) * self.cols + lax.rem(col + right, self.cols)

    def to(self, down, right):
        return {"device_id": {self.name: self.at(down, right)}, "device_id_type": MESH}


class Gather:
    def __init__(self, axis, block, outer):
        self.axis, self.outer, self.inputs = axis, outer, [block]
        n, self.chunks = axis.size, block.shape[0]
        lead = (n, self.chunks) if outer else (self.chunks, n)
        self.outputs = [jax.ShapeDtypeStruct(lead + block.shape[1:], block.dtype)]
        held, others = max(axis.rows - 1, 1), axis.cols - 1
        row, col = (held, self.chunks), (others, axis.rows, self.chunks)
        self.scratch = [dma((self.chunks,)), dma(row), dma(row), dma(col), dma(col)]
        self.peers = [(k, 0) for k in range(1, axis.rows)] + [(0, j) for j in range(1, axis.cols)]
        self.bytes = block.size * 2

    def bind(self, ins, outs, scratch):
        (self.src,), (self.dst,) = ins, outs
        self.keep, self.row_out, self.row_in, self.col_out, self.col_in = scratch

    def place(self, dev, c):
        return self.dst.at[dev, c] if self.outer else self.dst.at[c, dev]

    def along(self, k, c):
        axis = self.axis
        return pltpu.make_async_remote_copy(
            src_ref=self.src.at[c],
            dst_ref=self.place(axis.at(0, 0), c),
            send_sem=self.row_out.at[k - 1, c],
            recv_sem=self.row_in.at[k - 1, c],
            **axis.to(k, 0),
        )

    def across(self, k, j, c):
        axis = self.axis
        spot = self.place(axis.at((axis.rows - k) % axis.rows, 0), c)
        return pltpu.make_async_remote_copy(
            src_ref=self.src.at[c] if k == 0 else spot,
            dst_ref=spot,
            send_sem=self.col_out.at[j - 1, k, c],
            recv_sem=self.col_in.at[j - 1, k, c],
            **axis.to(0, j),
        )

    def own(self, c):
        return pltpu.make_async_copy(
            self.src.at[c], self.place(self.axis.at(0, 0), c), self.keep.at[c]
        )

    def start(self):
        for c in range(self.chunks):
            for k in range(1, self.axis.rows):
                self.along(k, c).start()
        for c in range(self.chunks):
            for j in range(1, self.axis.cols):
                self.across(0, j, c).start()
            self.own(c).start()

    def middle(self, part, parts):
        for c in range(self.chunks * part // parts, self.chunks * (part + 1) // parts):
            for k in range(1, self.axis.rows):
                self.along(k, c).wait_recv()
                for j in range(1, self.axis.cols):
                    self.across(k, j, c).start()

    def finish(self):
        for c in range(self.chunks):
            for k in range(1, self.axis.rows):
                self.along(k, c).wait_send()
            for k in range(self.axis.rows):
                for j in range(1, self.axis.cols):
                    self.across(k, j, c).wait()
            self.own(c).wait()


class Exchange:
    def __init__(self, axis, array, shape, source, target):
        self.axis, self.inputs = axis, [array]
        self.outputs = [jax.ShapeDtypeStruct(shape, array.dtype)]
        self.source, self.target = source, target
        n = axis.size
        self.scratch = [dma, dma((n - 1,)), dma((n - 1,))]
        self.peers = [(k, j) for k in range(axis.rows) for j in range(axis.cols)][1:]
        self.bytes = array.size

    def bind(self, ins, outs, scratch):
        (self.src,), (self.dst,) = ins, outs
        self.keep, self.out_sem, self.in_sem = scratch

    def copy(self, i):
        axis, (k, j) = self.axis, self.peers[i]
        return pltpu.make_async_remote_copy(
            src_ref=self.source(self.src, axis.at(k, j)),
            dst_ref=self.target(self.dst, axis.at(0, 0)),
            send_sem=self.out_sem.at[i],
            recv_sem=self.in_sem.at[i],
            **axis.to(k, j),
        )

    def own(self):
        me = self.axis.at(0, 0)
        return pltpu.make_async_copy(self.source(self.src, me), self.target(self.dst, me), self.keep)

    def start(self):
        self.own().start()
        for i in reversed(range(len(self.peers))):
            self.copy(i).start()

    def middle(self, part, parts):
        pass

    def finish(self):
        for i in reversed(range(len(self.peers))):
            self.copy(i).wait()
        self.own().wait()


class Scatter:
    def __init__(self, axis, parts, outer, dtype, ahead=None):
        self.axis, self.outer, self.dtype, self.inputs = axis, outer, dtype, [parts]
        self.chunks = parts.shape[1 if outer else 0]
        block = (self.chunks,) + parts.shape[2:]
        self.outputs = [jax.ShapeDtypeStruct(block, dtype)]
        rows, others, held = axis.rows, axis.cols - 1, max(axis.rows - 1, 1)
        row, col = (held, self.chunks), (others, rows, self.chunks)
        self.scratch = [
            pltpu.VMEM((rows,) + block, bf16),
            pltpu.VMEM((others, rows) + block, bf16),
            pltpu.VMEM((held,) + block, bf16),
            pltpu.VMEM((held,) + block, bf16),
            pltpu.VMEM(block, dtype),
            dma((rows, self.chunks)),
            dma(col),
            dma(col),
            dma(row),
            dma(row),
            dma((self.chunks,)),
        ]
        self.peers = [(k, 0) for k in range(1, rows)] + [(0, j) for j in range(1, axis.cols)]
        self.order = [(k, c) for k in list(range(1, rows)) + [0] for c in range(self.chunks)]
        self.ahead = min(ahead or len(self.order), len(self.order))
        self.bytes = parts.size // axis.size * 2

    def bind(self, ins, outs, scratch):
        (self.src,), (self.dst,) = ins, outs
        self.mine, self.met, self.sent, self.come, self.result = scratch[:5]
        self.load, self.col_out, self.col_in, self.row_out, self.row_in, self.store = scratch[5:]

    def terms(self, dev, c):
        return self.src.at[dev, c] if self.outer else self.src.at[c, dev]

    def read(self, k, c):
        return pltpu.make_async_copy(
            self.terms(self.axis.at(k, 0), c), self.mine.at[k, c], self.load.at[k, c]
        )

    def across(self, k, j, c):
        return pltpu.make_async_remote_copy(
            src_ref=self.terms(self.axis.at(k, j), c),
            dst_ref=self.met.at[j - 1, k, c],
            send_sem=self.col_out.at[j - 1, k, c],
            recv_sem=self.col_in.at[j - 1, k, c],
            **self.axis.to(0, j),
        )

    def along(self, k, c):
        return pltpu.make_async_remote_copy(
            src_ref=self.sent.at[k - 1, c],
            dst_ref=self.come.at[k - 1, c],
            send_sem=self.row_out.at[k - 1, c],
            recv_sem=self.row_in.at[k - 1, c],
            **self.axis.to(k, 0),
        )

    def write(self, c):
        return pltpu.make_async_copy(self.result.at[c], self.dst.at[c], self.store.at[c])

    def leave(self, i):
        if i < len(self.order):
            k, c = self.order[i]
            for j in range(1, self.axis.cols):
                self.across(k, j, c).start()

    def meet(self, k, c):
        self.read(k, c).wait()
        total = self.mine[k, c].astype(f32)
        for j in range(1, self.axis.cols):
            self.across(k, j, c).wait_recv()
            total = total + self.met[j - 1, k, c].astype(f32)
        self.leave(self.order.index((k, c)) + self.ahead)
        return total

    def start(self):
        for i, (k, c) in enumerate(self.order):
            if i < self.ahead:
                self.leave(i)
            self.read(k, c).start()

    def middle(self, part, parts):
        steps = [step for step in self.order if step[0]]
        for k, c in steps[len(steps) * part // parts : len(steps) * (part + 1) // parts]:
            self.sent[k - 1, c] = self.meet(k, c).astype(bf16)
            self.along(k, c).start()

    def finish(self):
        for c in range(self.chunks):
            total = self.meet(0, c)
            for k in range(1, self.axis.rows):
                self.along(k, c).wait_recv()
                total = total + self.come[k - 1, c].astype(f32)
            self.result[c] = total.astype(self.dtype)
            self.write(c).start()
        for k, c in self.order:
            for j in range(1, self.axis.cols):
                self.across(k, j, c).wait_send()
            if k:
                self.along(k, c).wait_send()
        for c in range(self.chunks):
            self.write(c).wait()


class Product:
    def __init__(self, pairs, over, tiles, rows=None):
        self.inputs, self.over = [matrix for pair in pairs for matrix in pair], over
        left, right = pairs[0]
        self.depth, n = left.shape[over[0]], right.shape[1 - over[1]]
        first, m = rows or (0, left.shape[1 - over[0]])
        self.outputs = [jax.ShapeDtypeStruct((m, n), bf16)]
        self.tm, self.tn = min(tiles[0], m), min(tiles[1], n)
        self.grid, self.skip = (m // self.tm, n // self.tn), first // self.tm
        self.scratch, self.peers, self.bytes = [], [], 0

    def bind(self, ins, outs, scratch):
        self.refs = (*ins, *outs)

    def start(self):
        pass

    def middle(self, part, parts):
        pass

    def finish(self):
        pass

    def compute(self):
        def body(*refs):
            total = contract(refs[0][...], refs[1][...], *self.over)
            for i in range(2, len(refs) - 1, 2):
                total = total + contract(refs[i][...], refs[i + 1][...], *self.over)
            refs[-1][...] = total.astype(bf16)

        def tile(size, over, index):
            def at(i, j):
                return (i + self.skip, j)[index]

            if over == 0:
                return pl.BlockSpec((self.depth, size), lambda i, j: (0, at(i, j)))
            return pl.BlockSpec((size, self.depth), lambda i, j: (at(i, j), 0))

        pair = [tile(self.tm, self.over[0], 0), tile(self.tn, self.over[1], 1)]
        pltpu.emit_pipeline(
            body,
            grid=self.grid,
            in_specs=pair * (len(self.inputs) // 2),
            out_specs=[pl.BlockSpec((self.tm, self.tn), lambda i, j: (i, j))],
        )(*self.refs)


class Net:
    def __init__(self, n_seq, n_fsdp):
        rows = 4 if n_fsdp % 4 == 0 else 1
        self.seq = Axis("seq", n_seq // 2, 2)
        self.fsdp = Axis("fsdp", rows, n_fsdp // rows)
        self.calls = 0

    def run(self, jobs, room=32):
        self.calls += 1
        ins = [array for job in jobs for array in job.inputs]
        outs = [shape for job in jobs for shape in job.outputs]
        scratch = [one for job in jobs for one in job.scratch]
        peers = []
        for job in jobs:
            for peer in job.peers:
                if (job.axis, peer) not in peers:
                    peers.append((job.axis, peer))

        def kernel(*refs):
            at = [0, len(ins), len(ins) + len(outs)]
            for job in jobs:
                taken = []
                for part, count in enumerate(
                    (len(job.inputs), len(job.outputs), len(job.scratch))
                ):
                    taken.append(refs[at[part] : at[part] + count])
                    at[part] += count
                job.bind(*taken)
            barrier = pltpu.get_barrier_semaphore()
            for axis, peer in peers:
                pl.semaphore_signal(barrier, inc=1, **axis.to(*peer))
            pl.semaphore_wait(barrier, len(peers))
            for job in jobs:
                job.start()
            products = [job for job in jobs if not job.peers]
            late = [job for job in jobs if products and isinstance(job, Gather)]
            parts = 4
            for some in ([job for job in jobs if job not in late], late):
                for part in range(parts):
                    for job in some:
                        job.middle(part, parts)
                if some is not late:
                    for job in products:
                        job.compute()
            for job in jobs:
                job.finish()

        anywhere = pl.BlockSpec(memory_space=pl.ANY)
        return pl.pallas_call(
            kernel,
            in_specs=[anywhere] * len(ins),
            out_specs=[anywhere] * len(outs),
            out_shape=outs,
            scratch_shapes=scratch,
            compiler_params=pltpu.CompilerParams(
                collective_id=self.calls, has_side_effects=True, vmem_limit_bytes=room << 20
            ),
            cost_estimate=pl.CostEstimate(
                flops=0, bytes_accessed=12 * max(job.bytes for job in jobs), transcendentals=0
            ),
            name="net",
        )(*ins)


def own_columns(weight, me, groups, order, each):
    shard, count = weight.shape[0], len(order)
    per = weight.shape[1] // (groups * count * each)
    if each % 128:
        cut = weight.reshape(shard, groups, count, per, each)
        cut = lax.dynamic_index_in_dim(cut, me, 3, keepdims=False)
        return [reorder(cut[:, g], order, 1).reshape(shard, count * each) for g in range(groups)]

    def kernel(me_ref, order_ref, *refs):
        for g in range(groups):
            refs[groups + g][...] = refs[g][...]

    def source(g):
        def at(i, me_ref, order_ref):
            return 0, (g * count + order_ref[i]) * per + me_ref[0]

        return pl.BlockSpec((shard, each), at)

    return pl.pallas_call(
        kernel,
        grid_spec=pltpu.PrefetchScalarGridSpec(
            num_scalar_prefetch=2,
            grid=(count,),
            in_specs=[source(g) for g in range(groups)],
            out_specs=[pl.BlockSpec((shard, each), lambda i, *refs: (0, i))] * groups,
        ),
        out_shape=[jax.ShapeDtypeStruct((shard, count * each), weight.dtype)] * groups,
        name="own_columns",
    )(me.reshape(1), jnp.array(order, jnp.int32), *([weight] * groups))


def spread_columns(arrays, groups, group, order, each, block_rows):
    devices, rows, _ = arrays[0].shape
    wide, count = devices * each, len(order)

    def kernel(order_ref, in_ref, *refs):
        for j in range(devices):
            refs[-1][:, j * each : (j + 1) * each] = in_ref[j].astype(f32)

    return pl.pallas_call(
        kernel,
        grid_spec=pltpu.PrefetchScalarGridSpec(
            num_scalar_prefetch=1,
            grid=(count, rows // block_rows),
            in_specs=[
                pl.BlockSpec((devices, block_rows, each), lambda i, r, order_ref: (0, r, i))
            ]
            + [pl.BlockSpec(memory_space=pl.ANY)] * (len(arrays) - 1),
            out_specs=pl.BlockSpec(
                (block_rows, wide), lambda i, r, order_ref: (r, group * count + order_ref[i])
            ),
        ),
        out_shape=jax.ShapeDtypeStruct((rows, groups * count * wide), f32),
        input_output_aliases={2: 0} if len(arrays) > 1 else {},
        name="spread_columns",
    )(jnp.array(order, jnp.int32), *arrays)


def mm(left, right):
    return jnp.dot(left, right, preferred_element_type=f32)


def mm_nt(left, right):
    return lax.dot_general(left, right, (((1,), (1,)), ((), ())), preferred_element_type=f32)


def mm_tn(left, right):
    return lax.dot_general(left, right, (((0,), (0,)), ((), ())), preferred_element_type=f32)


def make_body(n_seq, n_fsdp):
    def body(
        tokens,
        cotangent,
        w_qkv,
        w_out,
        w_gate_up,
        w_down,
        gain_attn,
        gain_ffn,
        gate_bias,
        memory_in,
        norms_in,
        resets,
        depth,
    ):
        _, segs, local, width = tokens.shape
        heads = gate_bias.shape[0]
        hdim = width // heads
        my_heads = heads // n_seq
        my_width = width // n_seq
        seg = local * n_seq
        rows = segs * local
        total_rows = segs * seg
        shard = w_qkv.shape[0]
        hidden_shard = w_down.shape[0]
        my_hidden = hidden_shard // n_seq
        out_rows = shard // n_seq
        net = Net(n_seq, n_fsdp)
        me = lax.axis_index("seq")

        ring = ring_order(n_fsdp)
        back = [ring.index(i) for i in range(n_fsdp)]
        (qkv_own,) = own_columns(w_qkv, me, 1, range(3), my_width)
        gate_own, up_own = own_columns(w_gate_up, me, 2, ring, my_hidden)
        down_own = lax.dynamic_slice(w_down, (me * my_hidden, 0), (my_hidden, width))
        out_own = lax.dynamic_slice(w_out, (me * out_rows, 0), (out_rows, width))

        x_flat = tokens.reshape(rows, width).astype(f32)
        r_one = rms(x_flat)
        h_one_own = reorder((r_one * gain_attn).astype(bf16), ring, 1)
        grad_y = cotangent.reshape(rows, width)

        def gather_rows(block):
            return lax.all_gather(block, "fsdp", axis=0, tiled=True, axis_index_groups=[ring])

        def token_parts(value):
            return value.reshape(segs, n_seq, local, width)

        def gather_own(value):
            return Gather(net.seq, value.reshape(segs, local, width), False)

        w_o = gather_rows(tie(out_own, h_one_own))
        w_q = gather_rows(tie(qkv_own, h_one_own))
        (h_one,) = net.run([gather_own(h_one_own)])
        h_one = h_one.reshape(total_rows, width)
        w_g = gather_rows(tie(gate_own, h_one))
        w_o = move_blocks(tie(w_o, h_one), back, 0)
        (whole_o,) = net.run([Gather(net.seq, w_o.reshape(n_fsdp, out_rows, width), False)])
        whole_o = whole_o.reshape(width, width)
        w_u = gather_rows(tie(up_own, whole_o))

        qkv = mm(h_one, w_q).astype(bf16)
        gate = jax.nn.sigmoid(lax.dynamic_slice(gate_bias, (me * my_heads,), (my_heads,)))
        memory = lax.dynamic_slice(memory_in[0], (me * my_heads, 0, 0), (my_heads, hdim, hdim))
        norms = lax.dynamic_slice(norms_in[0], (me * my_heads, 0), (my_heads, hdim))
        attn_heads, lse, mems, nrms = attention_forward(qkv, gate, resets[0], memory, norms, segs)

        half = width // 2
        w_d = gather_rows(tie(down_own, attn_heads))

        def columns_of(ref, i):
            return ref.at[:, :, pl.ds(pl.multiple_of(i * my_width, my_width), my_width)]

        def tokens_of(ref, i):
            return ref.at[:, i]

        (attn,) = net.run(
            [
                Exchange(
                    net.seq,
                    attn_heads.reshape(segs, n_seq, local, my_width),
                    (segs, local, width),
                    tokens_of,
                    columns_of,
                ),
            ]
        )
        attn = attn.reshape(rows, width)
        x_one = x_flat + mm(attn, whole_o)
        r_two = rms(x_one)
        h_two_own = reorder((r_two * gain_ffn).astype(bf16), ring, 1)
        (h_two,) = net.run([gather_own(h_two_own)])
        h_two = h_two.reshape(total_rows, width)
        grad_y_all, gate_part = net.run(
            [gather_own(tie(grad_y, h_two)), Product([(h_two, w_g)], (1, 0), (1024, 512))], 56
        )
        grad_y_all = grad_y_all.reshape(total_rows, width)
        up_part = mm(h_two, w_u).astype(bf16)
        hidden = swiglu(gate_part.astype(f32), up_part.astype(f32)).astype(bf16)

        def scatter_rows(parts):
            return lax.psum_scatter(
                parts, "fsdp", scatter_dimension=0, tiled=True, axis_index_groups=[ring]
            )

        down_parts = mm_tn(hidden, grad_y_all).astype(bf16)
        down_term = scatter_rows(down_parts)
        grad_hidden = mm_nt(tie(grad_y_all, down_parts), w_d)
        _, swiglu_back = jax.vjp(swiglu, gate_part.astype(f32), up_part.astype(f32))
        grad_gate, grad_up = swiglu_back(grad_hidden)
        grad_gate, grad_up = grad_gate.astype(bf16), grad_up.astype(bf16)

        def output_terms(s):
            return Product([(hidden, w_d)], (1, 0), (1024, 512), (s * seg, seg))

        def h_two_terms(s):
            pairs = [(grad_gate, w_g), (grad_up, w_u)]
            return Product(pairs, (1, 1), (512, 512), (s * seg, seg))

        gate_product = Product([(h_two, grad_gate)], (0, 0), (1024, 512))
        up_product = Product([(h_two, grad_up)], (0, 0), (1024, 512))
        beside = [[output_terms(s)] for s in range(1, segs)]
        beside += [[h_two_terms(s)] for s in range(segs)] + [[up_product]]
        beside[0].append(gate_product)
        terms = mm(hidden[:seg], tie(w_d, grad_up)).astype(bf16)
        sums, gate_parts = [], None
        for products in beside:
            parts = terms.reshape(n_seq, 2, local // 2, width)
            results = net.run([Scatter(net.seq, parts, True, f32)] + products, 56)
            sums.append(results[0])
            terms = results[1]
            if products[-1] is gate_product:
                gate_parts = results[-1]
                gate_term = scatter_rows(gate_parts)
        up_parts = terms
        up_term = scatter_rows(up_parts)
        output = jnp.stack(sums[:segs]).reshape(rows, width)
        grad_h_two = reorder(jnp.stack(sums[segs:]).reshape(rows, width), back, 1)

        gain_ffn_term = jnp.sum(grad_h_two * r_two, axis=0)
        _, norm_two_back = jax.vjp(rms, x_one)
        grad_x_one = grad_y.astype(f32) + norm_two_back(grad_h_two * gain_ffn)[0]
        grad_o = grad_x_one.astype(bf16)

        grad_attn_parts = mm_nt(grad_o, whole_o).astype(bf16)
        grad_attn, out_parts = net.run(
            [
                Exchange(
                    net.seq,
                    grad_attn_parts.reshape(segs, local, width),
                    (segs, n_seq, local, my_width),
                    columns_of,
                    tokens_of,
                ),
                Product([(attn, grad_o)], (0, 0), (1024, 512)),
            ],
            56,
        )
        grad_attn = tie(grad_attn.reshape(total_rows, my_width), down_term)
        grads_q, grads_k, grads_v, bias_terms = attention_backward(
            qkv, grad_attn, gate, resets[0], depth, lse, mems, nrms, segs
        )
        grad_qkv_rows = jnp.concatenate([grads_q, grads_k, grads_v], axis=1)
        out_parts = tie(out_parts, gate_term)
        out_sum, qkv_parts, grad_h_one = net.run(
            [
                Scatter(net.seq, out_parts.reshape(n_fsdp, n_seq, out_rows, width), False, bf16),
                Product([(h_one, grad_qkv_rows)], (0, 0), (1024, 512)),
                Product([(grad_qkv_rows, w_q)], (1, 1), (1024, 512)),
            ],
            56,
        )
        qkv_term = scatter_rows(qkv_parts)
        grad_h_one, out_term, down_all, gate_all = net.run(
            [
                Scatter(net.seq, token_parts(tie(grad_h_one, up_term)), False, f32),
                Scatter(net.fsdp, out_sum[:, None], True, bf16, 2),
                Gather(net.seq, down_term[None], True),
                Gather(net.seq, gate_term[None], True),
            ],
            56,
        )
        grad_h_one = move_blocks(grad_h_one.reshape(rows, width), back, 1)
        output = (x_one + output).astype(bf16).reshape(tokens.shape)
        gain_attn_term = jnp.sum(grad_h_one * r_one, axis=0)
        _, norm_one_back = jax.vjp(rms, x_flat)
        grad_x = grad_x_one + norm_one_back(grad_h_one * gain_attn)[0]
        input_grad = grad_x.astype(bf16).reshape(tokens.shape)

        bias_all = lax.dynamic_update_slice(
            jnp.zeros((heads,), f32), bias_terms[:, 0, 0], (me * my_heads,)
        )
        small = jnp.concatenate([gain_attn_term, gain_ffn_term, bias_all])
        wide = -(-small.shape[0] // 1024) * 128
        small = jnp.pad(small, (0, 8 * wide - small.shape[0])).reshape(1, 8, wide)

        down_all = down_all.reshape(hidden_shard, width).astype(f32)
        aligned = my_hidden % 128 == 0
        gate_up_all = gate_all[:, 0]
        if aligned:
            gate_up_all = spread_columns([gate_up_all], 2, 0, ring, my_hidden, shard)
        up_all = lax.all_gather(tie(up_term, grad_h_one), "seq", axis=0)
        qkv_all = lax.all_gather(tie(qkv_term, grad_h_one), "seq", axis=0)
        small, out_all = net.run([Gather(net.fsdp, small, True), Gather(net.seq, out_term, True)])
        (small,) = net.run([Gather(net.seq, jnp.sum(small, axis=0), True)])
        small = jnp.sum(small, axis=0).reshape(-1)
        out_all = out_all.reshape(shard, width).astype(f32)
        done = (down_all, gate_up_all, output, input_grad, small, out_all)
        qkv_all = tie(qkv_all, *done)
        up_all = tie(up_all, *done)
        qkv_all = spread_columns([qkv_all], 1, 0, range(3), my_width, shard // 2)
        if aligned:
            gate_up_all = spread_columns([up_all, gate_up_all], 2, 1, ring, my_hidden, shard)
        else:
            cut = jnp.stack([gate_up_all, up_all]).reshape(2, n_seq, shard, n_fsdp, my_hidden)
            cut = reorder(cut, back, 3)
            gate_up_all = jnp.transpose(cut, (2, 0, 3, 1, 4)).reshape(shard, -1).astype(f32)

        return (
            output,
            input_grad,
            qkv_all,
            out_all,
            gate_up_all,
            down_all,
            small[:width],
            small[width : 2 * width],
            small[2 * width : 2 * width + heads],
        )

    return body


def solution(mesh):
    rows = P("fsdp", None)
    tokens = P("fsdp", None, "seq", None)
    body = make_body(mesh.shape["seq"], mesh.shape["fsdp"])
    return jax.shard_map(
        body,
        mesh=mesh,
        in_specs=(
            tokens,
            tokens,
            rows,
            rows,
            rows,
            rows,
            P(),
            P(),
            P(),
            P("fsdp", None, None, None),
            P("fsdp", None, None),
            rows,
            P("fsdp"),
        ),
        out_specs=(tokens, tokens, rows, rows, rows, rows, P(), P(), P()),
        check_vma=False,
    )
```
